32 devices in a mesh: ctx: 8 (over z, y), ep: 4 (over x, core).
Axes of the slice: x: 2, y: 2, z: 4, core: 2. Of those that a mesh axis runs over, the one named last changes fastest.
Arguments:
- queries: bfloat16 [4, 1024, 2048], P('ep', 'ctx'), may hold values from -100 to 100
- keys: bfloat16 [4, 1024, 2048], P('ep', 'ctx'), may hold values from -4 to 4
- values: bfloat16 [4, 1024, 2048], P('ep', 'ctx'), may hold values from -6 to 6
- doc_ids: int32 [4, 1024], P('ep', 'ctx'), may hold values from 0 to 7, never falling along the last dimension, each value on 1 to 256 neighbouring positions
- routes: int32 [4, 1024, 1], P('ep', 'ctx'), may hold values from 0 to 63
- route_weight: float32 [4, 1024, 1], P('ep', 'ctx'), may hold values from 0.2 to 1
- norm_gain: float32 [2048], replicated, may hold values from 0.25 to 1.75
- w_gate: bfloat16 [2048, 90112], P(None, ('ctx', 'ep')), may hold values from -0.125 to 0.125
- w_up: bfloat16 [2048, 90112], P(None, ('ctx', 'ep')), may hold values from -0.125 to 0.125
- w_down: bfloat16 [90112, 2048], P(('ctx', 'ep')), may hold values from -0.15625 to 0.15625
- grad_out: bfloat16 [4, 1024, 2048], P('ep', 'ctx'), may hold values from -6 to 6
Outputs:
- grad_in: bfloat16 [4, 1024, 2048], P('ep', 'ctx')
The draws below stay inside these ranges and needn't reach their ends.
Inputs may be any that keep to these rules, and one draw needn't show every extreme that they name: `doc_ids`: no document has more than 256 tokens; ids never fall along a sequence.
All inputs are finite; a program needn't handle non-finite values.
Results may differ from the reference program's by a relative error of at most 0.0086.
Values may be sent and summed in bfloat16 or wider, within the bound.
No kernel may reach another device: no remote copies, remote signals or barrier semaphores. Data moves between devices by JAX's collectives and lax.ppermute only.
A program may use at most 128 MiB of HBM per device.

```python
import math
import jax
import jax.numpy as jnp
import numpy as np
from jax import lax

D = 2048
HEADS = 16
HEAD = 128
EXPERTS = 64
FF = 1408
ROUTES = 1
CAP = 2
STRETCH = 128
SEQS = 4
LENGTH = 1024
DOC_MAX = 256
DOCS = 8
REACH = 2
SLICE = 1408
SLICES = 1


def pair_fields(key):
    query_key = jax.random.fold_in(key, 101)
    key_key = jax.random.fold_in(key, 202)
    field_shape = (SEQS, LENGTH, D)
    drawn_queries = jax.random.truncated_normal(query_key, -4.0, 4.0, field_shape, jnp.float32)
    drawn_keys = jax.random.truncated_normal(key_key, -4.0, 4.0, field_shape, jnp.float32)
    return (drawn_queries, drawn_keys)


def draw_queries(key, part):
    return pair_fields(key)[0].astype(jnp.bfloat16)


def draw_keys(key, part):
    return pair_fields(key)[1].astype(jnp.bfloat16)


def block_levels(rng, extent, split, smallest, high):
    level = 1.0
    for position, blocks in split:
        steps = jax.random.uniform(jax.random.fold_in(jax.random.fold_in(rng, 6), position), (blocks,), jnp.float32, smallest / len(split), high / len(split))
        level = level * jnp.repeat(jnp.exp(steps), extent[position] // blocks).reshape((-1,) + (1,) * (len(extent) - 1 - position))
    return level


def picks_of(key, rows, count, top, lift):
    order = jax.random.permutation(jax.random.fold_in(key, 1), count)
    boost = order
    for power in range(3):
        boost = boost * boost // count
    boost = boost * lift // count
    tickets = jax.random.randint(jax.random.fold_in(key, 2), (rows, count), 0, 4096) + boost
    holders = jax.random.permutation(jax.random.fold_in(key, 3), rows)[jnp.arange(count) % rows]
    tickets = jnp.where(jnp.arange(rows)[:, None] == holders[None, :], 1 << 14, tickets)
    priority = tickets * count + jnp.arange(count)
    return lax.top_k(priority.astype(jnp.int32), top)[1].astype(jnp.int32)


def split_up(amount, total, most, lean):
    portions = [(1 << 20) // math.isqrt(standing ** lean) + 1 for standing in range(2, amount + 1)]
    surplus, given = total - most - (amount - 1), [1] * (amount - 1)
    while surplus > 0:
        movable = [i for i in range(amount - 1) if given[i] < most]
        mass, budget = sum([portions[i] for i in movable]), surplus
        for i in movable:
            extra = min(most - given[i], max(1, budget * portions[i] // mass), surplus)
            given[i] = given[i] + extra
            surplus = surplus - extra
    return np.array([most] + given)


def uneven_parts(stream_key, count, total, bound, skew):
    if count == 2:
        one = jax.random.randint(stream_key, (), max(1, total - bound), min(bound, total - 1) + 1)
        return jnp.stack([one, total - one])
    lengths = jnp.asarray(split_up(count, total, bound, skew), jnp.int32)
    couples = (count - 1) // 2
    giver, receiver = lengths[1:1 + 2 * couples:2], lengths[2:2 + 2 * couples:2]
    margin = jnp.minimum(giver - 1, bound - receiver)
    moved = jax.random.randint(jax.random.fold_in(stream_key, 1), (couples,), 0, 1 << 20) % (margin + 1)
    lengths = lengths.at[1:1 + 2 * couples:2].set(giver - moved).at[2:2 + 2 * couples:2].set(receiver + moved)
    return lengths[jax.random.permutation(jax.random.fold_in(stream_key, 2), count)]


def centred(stream_key, shape, scale, most, cuts=(), held_as=jnp.bfloat16):
    values = scale * jax.random.normal(stream_key, shape, jnp.float32)
    if cuts:
        values = values * block_levels(stream_key, shape, cuts, -0.22, 0.18)
    return jnp.clip(values, -most, most).astype(held_as)


def setup_inputs(seed: int = 0) -> dict:
    key_of = jax.random.split(jax.random.key(seed), 12)
    queries = draw_queries(jax.random.fold_in(key_of[11], 71), 0)
    keys = draw_keys(jax.random.fold_in(key_of[11], 71), 0)
    values = centred(key_of[2], (SEQS, LENGTH, D), 1.0, 6.0, ((0, 4), (1, 8)))
    doc_ids = jax.vmap(lambda own: jnp.searchsorted(jnp.cumsum(uneven_parts(own, DOCS, LENGTH, DOC_MAX, 2)), jnp.arange(LENGTH), side="right"))(jax.random.split(key_of[3], SEQS)).reshape((SEQS, LENGTH)).astype(jnp.int32)
    routes = picks_of(key_of[4], SEQS * LENGTH, EXPERTS, ROUTES, 256).reshape((SEQS, LENGTH, ROUTES))
    route_weight = jnp.clip(0.2 + 0.8 * jax.random.uniform(key_of[5], (SEQS, LENGTH, ROUTES), jnp.float32) ** block_levels(key_of[5], (SEQS, LENGTH, ROUTES), ((0, 4), (1, 8)), -0.2, 0.2), 0.2, 1.0)
    norm_gain = jnp.clip(1.0 + 0.15 * jax.random.normal(key_of[6], (D,), jnp.float32), 0.25, 1.75)
    w_gate = centred(key_of[7], (D, EXPERTS * FF), D ** -0.5, 0.125, ((1, 32),))
    w_up = centred(key_of[8], (D, EXPERTS * FF), D ** -0.5, 0.125, ((1, 32),))
    w_down = centred(key_of[9], (EXPERTS * FF, D), FF ** -0.5, 0.15625, ((0, 32),))
    grad_out = centred(key_of[10], (SEQS, LENGTH, D), 1.0, 6.0, ((0, 4), (1, 8)))
    return {"queries": queries, "keys": keys, "values": values, "doc_ids": doc_ids, "routes": routes, "route_weight": route_weight, "norm_gain": norm_gain, "w_gate": w_gate, "w_up": w_up, "w_down": w_down, "grad_out": grad_out}


def attend_sequence(operands):
    seq_queries, seq_keys, seq_values, seq_tags = operands
    padding = REACH * STRETCH
    keys_padded = jnp.concatenate([jnp.zeros((padding, D), seq_keys.dtype), seq_keys])
    values_padded = jnp.concatenate([jnp.zeros((padding, D), seq_values.dtype), seq_values])
    tags_padded = jnp.concatenate([jnp.full((padding,), -1, jnp.int32), seq_tags])
    score_scale = 1.0 / math.sqrt(HEAD)

    def one_block(block_index):
        first_row = block_index * STRETCH
        query_block = lax.dynamic_slice_in_dim(seq_queries, first_row, STRETCH, 0).astype(jnp.float32).reshape(STRETCH, HEADS, HEAD)
        key_block = lax.dynamic_slice_in_dim(keys_padded, first_row, padding + STRETCH, 0).astype(jnp.float32).reshape(padding + STRETCH, HEADS, HEAD)
        value_block = lax.dynamic_slice_in_dim(values_padded, first_row, padding + STRETCH, 0).astype(jnp.float32).reshape(padding + STRETCH, HEADS, HEAD)
        query_tags = lax.dynamic_slice_in_dim(seq_tags, first_row, STRETCH, 0)
        key_tags = lax.dynamic_slice_in_dim(tags_padded, first_row, padding + STRETCH, 0)
        scores = jnp.einsum('qhd,khd->hqk', query_block, key_block) * score_scale
        query_pos = jnp.arange(STRETCH, dtype=jnp.int32)[:, None] + padding
        key_pos = jnp.arange(padding + STRETCH, dtype=jnp.int32)[None, :]
        visible = (query_tags[:, None] == key_tags[None, :]) & (key_pos <= query_pos)
        scores = jnp.where(visible[None], scores, -1e+30)
        row_max = lax.optimization_barrier(jnp.max(scores, axis=-1, keepdims=True))
        weights_exp = jnp.exp(scores - row_max)
        probs = (weights_exp / lax.optimization_barrier(jnp.sum(weights_exp, axis=-1, keepdims=True))).astype(jnp.bfloat16)
        attended = jnp.einsum('hqk,khd->qhd', probs.astype(jnp.float32), value_block)
        return attended.reshape(STRETCH, D).astype(jnp.bfloat16)
    blocks = lax.map(one_block, jnp.arange(LENGTH // STRETCH, dtype=jnp.int32))
    return blocks.reshape(LENGTH, D)

def reference(queries, keys, values, doc_ids, routes, route_weight, norm_gain, w_gate, w_up, w_down, grad_out):
    hidden_bf = lax.map(attend_sequence, (queries, keys, values, doc_ids + 1))
    hidden = lax.optimization_barrier(hidden_bf).astype(jnp.float32)
    inv_rms = lax.rsqrt(lax.optimization_barrier(jnp.mean(hidden * hidden, axis=-1, keepdims=True)) + 1e-06)
    normed = (hidden * inv_rms * norm_gain).astype(jnp.bfloat16)
    grad_f = grad_out.astype(jnp.float32)
    grad_rows = (route_weight[..., 0:1] * grad_f).astype(jnp.bfloat16)
    block_count = SEQS * LENGTH // STRETCH
    expert_ids = routes[..., 0].reshape(block_count, STRETCH)
    onehot = (expert_ids[..., None] == jnp.arange(EXPERTS, dtype=jnp.int32)).astype(jnp.int32)
    running = jnp.cumsum(onehot, axis=1)
    slot_rank = lax.optimization_barrier(jnp.sum(onehot * (running - 1), axis=-1)).astype(jnp.int32)
    kept_rows = slot_rank < CAP
    slot_index = jnp.where(kept_rows, slot_rank, CAP).astype(jnp.int32)
    block_ids = jnp.broadcast_to(jnp.arange(block_count, dtype=jnp.int32)[:, None], (block_count, STRETCH))
    slot_inputs = jnp.zeros((EXPERTS, block_count, CAP + 1, D), jnp.bfloat16)
    slot_inputs = slot_inputs.at[expert_ids, block_ids, slot_index].set(normed.reshape(block_count, STRETCH, D))[:, :, :CAP]
    slot_grads = jnp.zeros((EXPERTS, block_count, CAP + 1, D), jnp.bfloat16)
    slot_grads = slot_grads.at[expert_ids, block_ids, slot_index].set(grad_rows.reshape(block_count, STRETCH, D))[:, :, :CAP]
    gate_table = w_gate.reshape(D, EXPERTS, FF).transpose(1, 0, 2)
    up_table = w_up.reshape(D, EXPERTS, FF).transpose(1, 0, 2)
    down_table = w_down.reshape(EXPERTS, FF, D)

    def expert_term(operands):
        rows_in, rows_grad, gate_w, up_w, down_w = operands
        row_count = block_count * CAP
        rows_in = rows_in.reshape(row_count, D)
        rows_grad = rows_grad.reshape(row_count, D)
        gate_pre = jnp.dot(rows_in, gate_w, preferred_element_type=jnp.float32)
        up_pre = jnp.dot(rows_in, up_w, preferred_element_type=jnp.float32)
        grad_act = jnp.dot(rows_grad, down_w.T, preferred_element_type=jnp.float32)
        sigmoid_gate = jax.nn.sigmoid(gate_pre)
        gate_act = gate_pre * sigmoid_gate
        act_slope = sigmoid_gate * (1.0 + gate_pre * (1.0 - sigmoid_gate))
        grad_gate = (grad_act * up_pre * act_slope).astype(jnp.bfloat16)
        grad_up = (grad_act * gate_act).astype(jnp.bfloat16)
        partial_gate = jnp.einsum('rkw,dkw->rkd', grad_gate.astype(jnp.float32).reshape(row_count, SLICES, SLICE), gate_w.astype(jnp.float32).reshape(D, SLICES, SLICE))
        partial_up = jnp.einsum('rkw,dkw->rkd', grad_up.astype(jnp.float32).reshape(row_count, SLICES, SLICE), up_w.astype(jnp.float32).reshape(D, SLICES, SLICE))
        partial_bf = lax.optimization_barrier((partial_gate + partial_up).astype(jnp.bfloat16))
        summed = lax.optimization_barrier(jnp.sum(partial_bf.astype(jnp.float32), axis=1)).astype(jnp.bfloat16)
        return summed.reshape(block_count, CAP, D)
    expert_grad = lax.map(expert_term, (slot_inputs, slot_grads, gate_table, up_table, down_table))
    expert_grad = lax.optimization_barrier(expert_grad)
    gathered = expert_grad[expert_ids, block_ids, jnp.clip(slot_rank, 0, CAP - 1).astype(jnp.int32)]
    grad_normed = gathered.astype(jnp.float32) * kept_rows[..., None].astype(jnp.float32)
    grad_normed = grad_normed.reshape(SEQS, LENGTH, D)
    gained = grad_normed * norm_gain
    grad_in = grad_f + inv_rms * gained - hidden * inv_rms * inv_rms * inv_rms * lax.optimization_barrier(jnp.mean(hidden * gained, axis=-1, keepdims=True))
    return grad_in.astype(jnp.bfloat16)
```

```python
import functools
import math

import jax
import jax.numpy as jnp
from jax import lax
from jax.experimental import pallas as pl
from jax.experimental.pallas import tpu as pltpu
from jax.sharding import PartitionSpec as P

HEADS = 16
HEAD = 128
EXPERTS = 64
FF = 1408
CAP = 2
CHUNK = 256
TAG_ROWS = 16
BF = jnp.bfloat16
F32 = jnp.float32
MB = 1024 * 1024


def iota(shape, dim):
    return lax.broadcasted_iota(jnp.int32, shape, dim)


def dot(left, right):
    return jnp.dot(left, right, preferred_element_type=F32)


def dot_nt(left, right):
    return lax.dot_general(left, right, (((1,), (1,)), ((), ())), preferred_element_type=F32)


class Plan:
    def __init__(self, devices, columns, width, stretch):
        self.devices = devices
        self.columns = columns
        self.model = width
        self.stretch = stretch
        self.local = max(1, columns // FF)
        self.sharers = max(1, FF // columns)
        self.slots = self.local * CAP
        self.fold = max(1, 8 // self.slots)
        self.width = width // self.fold
        self.rows = self.slots * self.fold
        self.total = devices * self.rows
        self.chunks = self.total // CHUNK
        self.group = CHUNK // self.rows
        self.expert_rows = devices * CAP
        self.block = CHUNK if columns % CHUNK == 0 else columns
        self.steps = columns // self.block


def message_slot(plan, chunk, shape, dim):
    row = iota(shape, dim)
    device = chunk * plan.group + row // plan.rows
    within = row % plan.rows
    first = device * plan.local if plan.sharers == 1 else device // plan.sharers
    return first * CAP + within % plan.slots, within // plan.slots


def write_messages(plan, target, value, out_ref):
    for chunk in range(plan.chunks):
        wanted, piece = message_slot(plan, chunk, (CHUNK, plan.stretch), 0)
        hit = wanted == target
        total = None
        for part in range(plan.fold):
            pick = jnp.where(hit & (piece == part), 1.0, 0.0).astype(BF)
            term = dot(pick, value[:, part * plan.width:(part + 1) * plan.width])
            total = term if total is None else total + term
        out_ref[chunk * CHUNK:(chunk + 1) * CHUNK, :] = total.astype(BF)


def expert_pick(plan, expert, part, shape, row_dim, message_dim):
    row = iota(shape, row_dim)
    message = iota(shape, message_dim)
    wanted = (row // CAP) * plan.rows + part * plan.slots + expert * CAP + row % CAP
    return jnp.where(wanted == message, 1.0, 0.0).astype(BF)


def read_expert_rows(plan, message_ref, rows_ref):
    count = plan.group * CAP
    for expert in range(plan.local):
        for part in range(plan.fold):
            pick = expert_pick(plan, expert, part, (count, CHUNK), 0, 1)
            for chunk in range(plan.chunks):
                base = expert * plan.expert_rows + chunk * count
                got = dot(pick, message_ref[chunk * CHUNK:(chunk + 1) * CHUNK, :])
                rows_ref[base:base + count, part * plan.width:(part + 1) * plan.width] = got.astype(BF)


def write_expert_rows(plan, rows_ref, message_ref):
    count = plan.group * CAP
    for chunk in range(plan.chunks):
        total = None
        for expert in range(plan.local):
            base = expert * plan.expert_rows + chunk * count
            for part in range(plan.fold):
                pick = expert_pick(plan, expert, part, (CHUNK, count), 1, 0)
                rows = rows_ref[base:base + count, part * plan.width:(part + 1) * plan.width]
                term = dot(pick, rows.astype(BF))
                total = term if total is None else total + term
        message_ref[chunk * CHUNK:(chunk + 1) * CHUNK, :] = total.astype(BF)


def to_column(row):
    size = row.shape[1]
    return jnp.transpose(jnp.broadcast_to(row, (size, size)))


def grads_kernel(plan, routes_ref, weight_ref, grad_ref, message_ref, target_ref):
    size = plan.stretch
    routes = routes_ref[...].astype(F32)
    column = to_column(routes)
    earlier = iota((size, size), 0) < iota((size, size), 1)
    same = (column == routes) & earlier
    rank = jnp.sum(jnp.where(same, 1.0, 0.0), axis=0, keepdims=True).astype(jnp.int32)
    target = jnp.where(rank < CAP, routes_ref[...] * CAP + rank, -1)
    target_ref[...] = target
    weight = to_column(weight_ref[...])[:, 0:1]
    grads = (weight * grad_ref[...].astype(F32)).astype(BF)
    write_messages(plan, target, grads, message_ref)


def attention_kernel(
    plan, tags_ref, target_ref, gain_ref, q_ref, k0_ref, k1_ref, k2_ref, v0_ref, v1_ref, v2_ref,
    hidden_ref, inv_ref, message_ref,
):
    size = plan.stretch
    own = tags_ref[...].astype(F32)
    before = v1_ref[size:size + TAG_ROWS, 0:size].astype(F32)[0:1]
    further = v2_ref[size:size + TAG_ROWS, 0:size].astype(F32)[0:1]
    column = to_column(own)
    masks = [
        (column == own) & (iota((size, size), 1) <= iota((size, size), 0)),
        column == before,
        column == further,
    ]
    squares = jnp.zeros((size, 1), F32)
    for head in range(HEADS):
        span = slice(head * HEAD, (head + 1) * HEAD)
        query = q_ref[:, span]
        scores = [
            jnp.where(mask, dot_nt(query, ref[:, span]) * (1.0 / math.sqrt(HEAD)), -1e30)
            for mask, ref in zip(masks, (k0_ref, k1_ref, k2_ref))
        ]
        top = jnp.max(
            jnp.maximum(jnp.maximum(scores[0], scores[1]), scores[2]), axis=-1, keepdims=True
        )
        weights = [jnp.exp(score - top) for score in scores]
        norm = jnp.sum(weights[0] + weights[1] + weights[2], axis=-1, keepdims=True)
        total = None
        for weight, ref in zip(weights, (v0_ref, v1_ref, v2_ref)):
            term = dot((weight / norm).astype(BF), ref[0:size, span])
            total = term if total is None else total + term
        hidden = total.astype(BF)
        hidden_ref[:, span] = hidden
        hidden = hidden.astype(F32)
        squares = squares + jnp.sum(hidden * hidden, axis=-1, keepdims=True)
    inv = lax.rsqrt(squares * (1.0 / plan.model) + 1e-06)
    inv_ref[...] = jnp.broadcast_to(inv, inv_ref.shape)
    normed = (hidden_ref[...].astype(F32) * inv * gain_ref[...]).astype(BF)
    write_messages(plan, target_ref[...], normed, message_ref)


def for_blocks(plan, inside, across):
    if plan.local == 1:
        inside(0)
        return
    start = pl.program_id(0) * plan.block
    for expert in range(plan.local):
        low, high = expert * FF, (expert + 1) * FF
        pl.when((start >= low) & (start + plan.block <= high))(functools.partial(inside, expert))
        if expert + 1 < plan.local and high % plan.block:
            split = high % plan.block
            mask = iota((1, plan.block), 1) < split
            pl.when(start == high - split)(functools.partial(across, expert, mask))


def act_kernel(plan, message_ref, down_ref, act_ref, rows_ref):
    @pl.when(pl.program_id(0) == 0)
    def _():
        read_expert_rows(plan, message_ref, rows_ref)

    def product(expert):
        rows = rows_ref[expert * plan.expert_rows:(expert + 1) * plan.expert_rows, :]
        return dot_nt(rows, down_ref[...])

    def inside(expert):
        act_ref[...] = product(expert)

    def across(expert, mask):
        act_ref[...] = jnp.where(mask, product(expert), product(expert + 1))

    for_blocks(plan, inside, across)


def expert_kernel(plan, message_ref, act_ref, gate_ref, up_ref, out_ref, rows_ref, sum_ref):
    step = pl.program_id(0)

    @pl.when(step == 0)
    def _():
        read_expert_rows(plan, message_ref, rows_ref)
        sum_ref[...] = jnp.zeros_like(sum_ref)

    def span(expert):
        return slice(expert * plan.expert_rows, (expert + 1) * plan.expert_rows)

    def slopes(gate_pre, up_pre):
        act = act_ref[...]
        sig = jax.nn.sigmoid(gate_pre)
        grad_gate = act * up_pre * (sig * (1.0 + gate_pre * (1.0 - sig)))
        grad_up = act * (gate_pre * sig)
        return grad_gate, grad_up

    def collect(expert, grad_gate, grad_up):
        sum_ref[span(expert), :] += dot_nt(grad_gate.astype(BF), gate_ref[...]) + dot_nt(
            grad_up.astype(BF), up_ref[...]
        )

    def inside(expert):
        rows = rows_ref[span(expert), :]
        collect(expert, *slopes(dot(rows, gate_ref[...]), dot(rows, up_ref[...])))

    def across(expert, mask):
        first, second = rows_ref[span(expert), :], rows_ref[span(expert + 1), :]
        gate_pre = jnp.where(mask, dot(first, gate_ref[...]), dot(second, gate_ref[...]))
        up_pre = jnp.where(mask, dot(first, up_ref[...]), dot(second, up_ref[...]))
        grad_gate, grad_up = slopes(gate_pre, up_pre)
        collect(expert, jnp.where(mask, grad_gate, 0.0), jnp.where(mask, grad_up, 0.0))
        collect(expert + 1, jnp.where(mask, 0.0, grad_gate), jnp.where(mask, 0.0, grad_up))

    for_blocks(plan, inside, across)

    @pl.when(step == plan.steps - 1)
    def _():
        write_expert_rows(plan, sum_ref, out_ref)


def finish_kernel(
    plan, target_ref, gain_ref, hidden_ref, inv_ref, grad_ref, message_ref, out_ref
):
    target = to_column(target_ref[...].astype(F32))[:, 0:1].astype(jnp.int32)
    parts = [None] * plan.fold
    for chunk in range(plan.chunks):
        wanted, piece = message_slot(plan, chunk, (plan.stretch, CHUNK), 1)
        messages = message_ref[chunk * CHUNK:(chunk + 1) * CHUNK, :]
        for part in range(plan.fold):
            pick = jnp.where((wanted == target) & (piece == part), 1.0, 0.0).astype(BF)
            term = dot(pick, messages)
            parts[part] = term if parts[part] is None else parts[part] + term
    inv = inv_ref[:, 0:1]
    spans = [slice(part * plan.width, (part + 1) * plan.width) for part in range(plan.fold)]
    gained = [
        part.astype(BF).astype(F32) * gain_ref[:, span] for part, span in zip(parts, spans)
    ]
    hidden = [hidden_ref[:, span].astype(F32) for span in spans]
    moment = sum(jnp.sum(h * g, axis=-1, keepdims=True) for h, g in zip(hidden, gained))
    mean = moment * (1.0 / plan.model)
    cube = inv * inv * inv
    for h, g, span in zip(hidden, gained, spans):
        out = grad_ref[:, span].astype(F32) + inv * g - h * cube * mean
        out_ref[:, span] = out.astype(BF)


def whole(shape):
    return pl.BlockSpec(shape, lambda *_: (0,) * len(shape))


def params(limit):
    return pltpu.CompilerParams(vmem_limit_bytes=limit)


def shards(
    queries, keys, values, doc_ids, routes, route_weight, norm_gain, w_gate, w_up, w_down, grad_out
):
    stretch, model = queries.shape[1:]
    ctx_count = lax.axis_size("ctx")
    axes = ("ctx", "ep")
    plan = Plan(ctx_count * lax.axis_size("ep"), w_gate.shape[1], model, stretch)
    messages = jax.ShapeDtypeStruct((plan.total, plan.width), BF)
    gain = norm_gain.reshape(1, model)

    def exchange(value):
        cut = value.reshape(plan.devices, plan.rows, plan.width)
        cut = lax.all_to_all(cut, axes, split_axis=0, concat_axis=0, tiled=True)
        return cut.reshape(plan.total, plan.width)

    odd = lax.axis_index("ctx") % 2 == 1
    two_up = [(source, source + 2) for source in range(ctx_count - 2)]
    pairs = [(source, source ^ 1) for source in range(ctx_count)]

    tags = doc_ids + 1
    tag_row = jnp.pad(tags.astype(BF), ((0, TAG_ROWS - 1), (0, model - stretch)))
    own_keys = keys[0]
    own_values = jnp.concatenate([values[0], tag_row])
    far_keys = lax.ppermute(own_keys, "ctx", two_up)
    far_values = lax.ppermute(own_values, "ctx", two_up)
    near_keys = lax.ppermute(jnp.where(odd, far_keys, own_keys), "ctx", pairs)
    near_values = lax.ppermute(jnp.where(odd, far_values, own_values), "ctx", pairs)

    grad_messages, target = pl.pallas_call(
        functools.partial(grads_kernel, plan),
        out_shape=(messages, jax.ShapeDtypeStruct((1, stretch), jnp.int32)),
        compiler_params=params(32 * MB),
        name="route_grads",
    )(routes.reshape(1, stretch), route_weight.reshape(1, stretch), grad_out[0])
    grad_messages, far_values = lax.optimization_barrier((grad_messages, far_values))
    got_grads = exchange(grad_messages)

    hidden, inv, normed_messages = pl.pallas_call(
        functools.partial(attention_kernel, plan),
        out_shape=(
            jax.ShapeDtypeStruct((stretch, model), BF),
            jax.ShapeDtypeStruct((stretch, 128), F32),
            messages,
        ),
        compiler_params=params(32 * MB),
        name="attention",
    )(
        tags, target, gain, queries[0], own_keys, near_keys, far_keys, own_values, near_values,
        far_values,
    )
    got_normed = exchange(normed_messages)

    rows = plan.local * plan.expert_rows
    act = pl.pallas_call(
        functools.partial(act_kernel, plan),
        grid=(plan.steps,),
        in_specs=[
            whole((plan.total, plan.width)),
            pl.BlockSpec((plan.block, model), lambda step: (step, 0)),
        ],
        out_specs=pl.BlockSpec((plan.expert_rows, plan.block), lambda step: (0, step)),
        out_shape=jax.ShapeDtypeStruct((plan.expert_rows, plan.columns), F32),
        scratch_shapes=[pltpu.VMEM((rows, model), BF)],
        compiler_params=params(40 * MB),
        cost_estimate=pl.CostEstimate(
            flops=2 * plan.expert_rows * plan.columns * model,
            bytes_accessed=2 * plan.columns * model,
            transcendentals=0,
        ),
        name="grad_act",
    )(got_grads, w_down)

    returned = pl.pallas_call(
        functools.partial(expert_kernel, plan),
        grid=(plan.steps,),
        in_specs=[
            whole((plan.total, plan.width)),
            pl.BlockSpec((plan.expert_rows, plan.block), lambda step: (0, step)),
            pl.BlockSpec((model, plan.block), lambda step: (0, step)),
            pl.BlockSpec((model, plan.block), lambda step: (0, step)),
        ],
        out_specs=whole((plan.total, plan.width)),
        out_shape=messages,
        scratch_shapes=[pltpu.VMEM((rows, model), BF), pltpu.VMEM((rows, model), F32)],
        compiler_params=params(48 * MB),
        cost_estimate=pl.CostEstimate(
            flops=8 * plan.expert_rows * plan.columns * model,
            bytes_accessed=4 * plan.columns * model,
            transcendentals=0,
        ),
        name="experts",
    )(got_normed, act, w_gate, w_up)
    combined = exchange(returned)

    grad_in = pl.pallas_call(
        functools.partial(finish_kernel, plan),
        out_shape=jax.ShapeDtypeStruct((stretch, model), BF),
        compiler_params=params(32 * MB),
        name="finish",
    )(target, gain, hidden, inv, grad_out[0], combined)
    return grad_in[None]


def solution(mesh):
    in_specs = (
        P("ep", "ctx", None),
        P("ep", "ctx", None),
        P("ep", "ctx", None),
        P("ep", "ctx"),
        P("ep", "ctx", None),
        P("ep", "ctx", None),
        P(),
        P(None, ("ctx", "ep")),
        P(None, ("ctx", "ep")),
        P(("ctx", "ep"), None),
        P("ep", "ctx", None),
    )
    out_specs = P("ep", "ctx", None)
    return jax.shard_map(shards, mesh=mesh, in_specs=in_specs, out_specs=out_specs, check_vma=False)
```

```python
import functools
import math

import jax
import jax.numpy as jnp
from jax import lax
from jax.experimental import pallas as pl
from jax.experimental.pallas import tpu as pltpu
from jax.sharding import PartitionSpec as P

HEADS = 16
HEAD = 128
EXPERTS = 64
FF = 1408
CAP = 2
REACH = 2
CHUNK = 256
TAG_ROWS = 16
BF = jnp.bfloat16
F32 = jnp.float32
MB = 1024 * 1024


def iota(shape, dim):
    return lax.broadcasted_iota(jnp.int32, shape, dim)


def dot(left, right):
    return jnp.dot(left, right, preferred_element_type=F32)


def dot_nt(left, right):
    return lax.dot_general(left, right, (((1,), (1,)), ((), ())), preferred_element_type=F32)


class Plan:
    def __init__(self, devices, columns, width, stretch):
        self.devices = devices
        self.columns = columns
        self.model = width
        self.stretch = stretch
        self.local = max(1, columns // FF)
        self.sharers = max(1, FF // columns)
        self.slots = self.local * CAP
        self.fold = max(1, 8 // self.slots)
        self.width = width // self.fold
        self.rows = self.slots * self.fold
        self.total = devices * self.rows
        self.chunks = self.total // CHUNK
        self.group = CHUNK // self.rows
        self.expert_rows = devices * CAP
        self.block = CHUNK if columns % CHUNK == 0 else columns
        self.steps = columns // self.block


def message_slot(plan, chunk, shape, dim):
    row = iota(shape, dim)
    device = chunk * plan.group + row // plan.rows
    within = row % plan.rows
    first = device * plan.local if plan.sharers == 1 else device // plan.sharers
    return first * CAP + within % plan.slots, within // plan.slots


def write_messages(plan, target, value, out_ref):
    for chunk in range(plan.chunks):
        wanted, piece = message_slot(plan, chunk, (CHUNK, plan.stretch), 0)
        hit = wanted == target
        total = None
        for part in range(plan.fold):
            pick = jnp.where(hit & (piece == part), 1.0, 0.0).astype(BF)
            term = dot(pick, value[:, part * plan.width:(part + 1) * plan.width])
            total = term if total is None else total + term
        out_ref[chunk * CHUNK:(chunk + 1) * CHUNK, :] = total.astype(BF)


def expert_pick(plan, expert, part, shape, row_dim, message_dim):
    row = iota(shape, row_dim)
    message = iota(shape, message_dim)
    wanted = (row // CAP) * plan.rows + part * plan.slots + expert * CAP + row % CAP
    return jnp.where(wanted == message, 1.0, 0.0).astype(BF)


def read_expert_rows(plan, message_ref, rows_ref):
    count = plan.group * CAP
    for expert in range(plan.local):
        for part in range(plan.fold):
            pick = expert_pick(plan, expert, part, (count, CHUNK), 0, 1)
            for chunk in range(plan.chunks):
                base = expert * plan.expert_rows + chunk * count
                got = dot(pick, message_ref[chunk * CHUNK:(chunk + 1) * CHUNK, :])
                rows_ref[base:base + count, part * plan.width:(part + 1) * plan.width] = got.astype(BF)


def write_expert_rows(plan, columns, message_ref):
    count = plan.local * plan.expert_rows
    for chunk in range(plan.chunks):
        message = iota((CHUNK, count), 0) + chunk * CHUNK
        row = iota((CHUNK, count), 1)
        sender = (row % plan.expert_rows) // CAP
        slot = (row // plan.expert_rows) * CAP + row % CAP
        total = None
        for part in range(plan.fold):
            wanted = sender * plan.rows + part * plan.slots + slot
            pick = jnp.where(wanted == message, 1.0, 0.0).astype(BF)
            term = dot_nt(pick, columns[part * plan.width:(part + 1) * plan.width, :])
            total = term if total is None else total + term
        message_ref[chunk * CHUNK:(chunk + 1) * CHUNK, :] = total.astype(BF)


def to_column(row):
    size = row.shape[1]
    return jnp.transpose(jnp.broadcast_to(row, (size, size)))


def grads_kernel(plan, routes_ref, weight_ref, grad_ref, message_ref, target_ref):
    size = plan.stretch
    routes = routes_ref[...].astype(F32)
    column = to_column(routes)
    earlier = iota((size, size), 0) < iota((size, size), 1)
    same = (column == routes) & earlier
    rank = jnp.sum(jnp.where(same, 1.0, 0.0), axis=0, keepdims=True).astype(jnp.int32)
    target = jnp.where(rank < CAP, routes_ref[...] * CAP + rank, -1)
    target_ref[...] = target
    weight = to_column(weight_ref[...])[:, 0:1]
    grads = (weight * grad_ref[...].astype(F32)).astype(BF)
    write_messages(plan, target, grads, message_ref)


def probs_kernel(plan, tags_ref, q_ref, k0_ref, k1_ref, k2_ref, probs_ref):
    size = plan.stretch
    own = tags_ref[...].astype(F32)
    before = k1_ref[size:size + TAG_ROWS, 0:size].astype(F32)[0:1]
    further = k2_ref[size:size + TAG_ROWS, 0:size].astype(F32)[0:1]
    column = to_column(own)
    masks = [
        (column == own) & (iota((size, size), 1) <= iota((size, size), 0)),
        column == before,
        column == further,
    ]
    for head in range(HEADS):
        span = slice(head * HEAD, (head + 1) * HEAD)
        rows = slice(head * size, (head + 1) * size)
        query = q_ref[:, span]
        scores = [
            jnp.where(mask, dot_nt(query, ref[0:size, span]) * (1.0 / math.sqrt(HEAD)), -1e30)
            for mask, ref in zip(masks, (k0_ref, k1_ref, k2_ref))
        ]
        top = jnp.max(
            jnp.maximum(jnp.maximum(scores[0], scores[1]), scores[2]), axis=-1, keepdims=True
        )
        weights = [jnp.exp(score - top) for score in scores]
        norm = jnp.sum(weights[0] + weights[1] + weights[2], axis=-1, keepdims=True)
        for index, weight in enumerate(weights):
            probs_ref[rows, index * size:(index + 1) * size] = (weight / norm).astype(BF)


def hidden_kernel(
    plan, target_ref, gain_ref, probs_ref, v0_ref, v1_ref, v2_ref, hidden_ref, inv_ref, message_ref
):
    size = plan.stretch
    squares = jnp.zeros((size, 1), F32)
    for head in range(HEADS):
        span = slice(head * HEAD, (head + 1) * HEAD)
        rows = slice(head * size, (head + 1) * size)
        total = None
        for index, ref in enumerate((v0_ref, v1_ref, v2_ref)):
            term = dot(probs_ref[rows, index * size:(index + 1) * size], ref[:, span])
            total = term if total is None else total + term
        hidden = total.astype(BF)
        hidden_ref[:, span] = hidden
        hidden = hidden.astype(F32)
        squares = squares + jnp.sum(hidden * hidden, axis=-1, keepdims=True)
    inv = lax.rsqrt(squares * (1.0 / plan.model) + 1e-06)
    inv_ref[...] = jnp.broadcast_to(inv, inv_ref.shape)
    normed = (hidden_ref[...].astype(F32) * inv * gain_ref[...]).astype(BF)
    write_messages(plan, target_ref[...], normed, message_ref)


def for_blocks(plan, inside, across):
    if plan.local == 1:
        inside(0)
        return
    start = pl.program_id(0) * plan.block
    for expert in range(plan.local):
        low, high = expert * FF, (expert + 1) * FF
        pl.when((start >= low) & (start + plan.block <= high))(functools.partial(inside, expert))
        if expert + 1 < plan.local and high % plan.block:
            split = high % plan.block
            mask = iota((1, plan.block), 1) < split
            pl.when(start == high - split)(functools.partial(across, expert, mask))


def act_kernel(plan, message_ref, down_ref, act_ref, rows_ref):
    @pl.when(pl.program_id(0) == 0)
    def _():
        read_expert_rows(plan, message_ref, rows_ref)

    product = jnp.transpose(dot_nt(down_ref[...], rows_ref[...]))

    def rows_of(expert):
        return product[expert * plan.expert_rows:(expert + 1) * plan.expert_rows, :]

    def inside(expert):
        act_ref[...] = rows_of(expert)

    def across(expert, mask):
        act_ref[...] = jnp.where(mask, rows_of(expert), rows_of(expert + 1))

    for_blocks(plan, inside, across)


def expert_kernel(plan, message_ref, act_ref, gate_ref, up_ref, out_ref, rows_ref, sum_ref):
    step = pl.program_id(0)

    @pl.when(step == 0)
    def _():
        read_expert_rows(plan, message_ref, rows_ref)
        sum_ref[...] = jnp.zeros_like(sum_ref)

    def rows_of(expert):
        return rows_ref[expert * plan.expert_rows:(expert + 1) * plan.expert_rows, :]

    def slopes(gate_pre, up_pre):
        act = act_ref[...]
        sig = jax.nn.sigmoid(gate_pre)
        grad_gate = act * up_pre * (sig * (1.0 + gate_pre * (1.0 - sig)))
        grad_up = act * (gate_pre * sig)
        return grad_gate, grad_up

    def placed(expert, value, mask):
        zero = jnp.zeros_like(value)
        pieces = [zero] * plan.local
        pieces[expert] = value if mask is None else jnp.where(mask, value, 0.0)
        if mask is not None:
            pieces[expert + 1] = jnp.where(mask, 0.0, value)
        return jnp.concatenate(pieces, axis=0).astype(BF)

    def collect(expert, mask, grad_gate, grad_up):
        sum_ref[...] += dot_nt(gate_ref[...], placed(expert, grad_gate, mask)) + dot_nt(
            up_ref[...], placed(expert, grad_up, mask)
        )

    def inside(expert):
        rows = rows_of(expert)
        collect(expert, None, *slopes(dot(rows, gate_ref[...]), dot(rows, up_ref[...])))

    def across(expert, mask):
        first, second = rows_of(expert), rows_of(expert + 1)
        gate_pre = jnp.where(mask, dot(first, gate_ref[...]), dot(second, gate_ref[...]))
        up_pre = jnp.where(mask, dot(first, up_ref[...]), dot(second, up_ref[...]))
        collect(expert, mask, *slopes(gate_pre, up_pre))

    for_blocks(plan, inside, across)

    @pl.when(step == plan.steps - 1)
    def _():
        write_expert_rows(plan, sum_ref[...].astype(BF), out_ref)


def finish_kernel(
    plan, target_ref, gain_ref, hidden_ref, inv_ref, grad_ref, message_ref, out_ref
):
    target = to_column(target_ref[...].astype(F32))[:, 0:1].astype(jnp.int32)
    parts = [None] * plan.fold
    for chunk in range(plan.chunks):
        wanted, piece = message_slot(plan, chunk, (plan.stretch, CHUNK), 1)
        messages = message_ref[chunk * CHUNK:(chunk + 1) * CHUNK, :]
        for part in range(plan.fold):
            pick = jnp.where((wanted == target) & (piece == part), 1.0, 0.0).astype(BF)
            term = dot(pick, messages)
            parts[part] = term if parts[part] is None else parts[part] + term
    inv = inv_ref[:, 0:1]
    spans = [slice(part * plan.width, (part + 1) * plan.width) for part in range(plan.fold)]
    gained = [
        part.astype(BF).astype(F32) * gain_ref[:, span] for part, span in zip(parts, spans)
    ]
    hidden = [hidden_ref[:, span].astype(F32) for span in spans]
    moment = sum(jnp.sum(h * g, axis=-1, keepdims=True) for h, g in zip(hidden, gained))
    mean = moment * (1.0 / plan.model)
    cube = inv * inv * inv
    for h, g, span in zip(hidden, gained, spans):
        out = grad_ref[:, span].astype(F32) + inv * g - h * cube * mean
        out_ref[:, span] = out.astype(BF)


def whole(shape):
    return pl.BlockSpec(shape, lambda *_: (0,) * len(shape))


def params(limit):
    return pltpu.CompilerParams(vmem_limit_bytes=limit)


def shards(
    queries, keys, values, doc_ids, routes, route_weight, norm_gain, w_gate, w_up, w_down, grad_out
):
    stretch, model = queries.shape[1:]
    ctx_count = lax.axis_size("ctx")
    axes = ("ctx", "ep")
    plan = Plan(ctx_count * lax.axis_size("ep"), w_gate.shape[1], model, stretch)
    messages = jax.ShapeDtypeStruct((plan.total, plan.width), BF)
    message_bytes = 2 * plan.total * plan.width
    gain = norm_gain.reshape(1, model)

    def exchange(value):
        cut = value.reshape(plan.devices, plan.rows, plan.width)
        cut = lax.all_to_all(cut, axes, split_axis=0, concat_axis=0, tiled=True)
        return cut.reshape(plan.total, plan.width)

    odd = lax.axis_index("ctx") % 2 == 1
    one_up = [(source, source + 1) for source in range(ctx_count - 1)]
    two_up = [(source, source + 2) for source in range(ctx_count - 2)]
    pairs = [(source, source ^ 1) for source in range(ctx_count)]

    tags = doc_ids + 1
    tag_row = jnp.pad(tags.astype(BF), ((0, TAG_ROWS - 1), (0, model - stretch)))
    own_keys = jnp.concatenate([keys[0], tag_row])
    own_values = values[0]
    far_values = lax.ppermute(own_values, "ctx", two_up)
    near_keys = lax.ppermute(own_keys, "ctx", one_up)
    far_keys = lax.ppermute(own_keys, "ctx", two_up)
    near_values = lax.ppermute(jnp.where(odd, far_values, own_values), "ctx", pairs)

    grad_messages, target = pl.pallas_call(
        functools.partial(grads_kernel, plan),
        out_shape=(messages, jax.ShapeDtypeStruct((1, stretch), jnp.int32)),
        compiler_params=params(8 * MB + 3 * message_bytes),
        name="route_grads",
    )(routes.reshape(1, stretch), route_weight.reshape(1, stretch), grad_out[0])
    got_grads = exchange(grad_messages)

    probs = pl.pallas_call(
        functools.partial(probs_kernel, plan),
        out_shape=jax.ShapeDtypeStruct((HEADS * stretch, (REACH + 1) * stretch), BF),
        compiler_params=params(16 * MB),
        name="probs",
    )(tags, queries[0], keys[0], near_keys, far_keys)
    hidden, inv, normed_messages = pl.pallas_call(
        functools.partial(hidden_kernel, plan),
        out_shape=(
            jax.ShapeDtypeStruct((stretch, model), BF),
            jax.ShapeDtypeStruct((stretch, 128), F32),
            messages,
        ),
        compiler_params=params(12 * MB + 3 * message_bytes),
        name="hidden",
    )(target, gain, probs, own_values, near_values, far_values)
    got_normed = exchange(normed_messages)

    rows = plan.local * plan.expert_rows
    act = pl.pallas_call(
        functools.partial(act_kernel, plan),
        grid=(plan.steps,),
        in_specs=[
            whole((plan.total, plan.width)),
            pl.BlockSpec((plan.block, model), lambda step: (step, 0)),
        ],
        out_specs=pl.BlockSpec((plan.expert_rows, plan.block), lambda step: (0, step)),
        out_shape=jax.ShapeDtypeStruct((plan.expert_rows, plan.columns), F32),
        scratch_shapes=[pltpu.VMEM((rows, model), BF)],
        compiler_params=params(12 * MB + 9 * message_bytes),
        cost_estimate=pl.CostEstimate(
            flops=2 * plan.expert_rows * plan.columns * model,
            bytes_accessed=2 * plan.columns * model,
            transcendentals=0,
        ),
        name="grad_act",
    )(got_grads, w_down)

    returned = pl.pallas_call(
        functools.partial(expert_kernel, plan),
        grid=(plan.steps,),
        in_specs=[
            whole((plan.total, plan.width)),
            pl.BlockSpec((plan.expert_rows, plan.block), lambda step: (0, step)),
            pl.BlockSpec((model, plan.block), lambda step: (0, step)),
            pl.BlockSpec((model, plan.block), lambda step: (0, step)),
        ],
        out_specs=whole((plan.total, plan.width)),
        out_shape=messages,
        scratch_shapes=[pltpu.VMEM((rows, model), BF), pltpu.VMEM((model, rows), F32)],
        compiler_params=params(12 * MB + 9 * message_bytes),
        cost_estimate=pl.CostEstimate(
            flops=8 * plan.expert_rows * plan.columns * model,
            bytes_accessed=4 * plan.columns * model,
            transcendentals=0,
        ),
        name="experts",
    )(got_normed, act, w_gate, w_up)
    combined = exchange(returned)

    grad_in = pl.pallas_call(
        functools.partial(finish_kernel, plan),
        out_shape=jax.ShapeDtypeStruct((stretch, model), BF),
        compiler_params=params(12 * MB + 3 * message_bytes),
        name="finish",
    )(target, gain, hidden, inv, grad_out[0], combined)
    return grad_in[None]


def solution(mesh):
    in_specs = (
        P("ep", "ctx", None),
        P("ep", "ctx", None),
        P("ep", "ctx", None),
        P("ep", "ctx"),
        P("ep", "ctx", None),
        P("ep", "ctx", None),
        P(),
        P(None, ("ctx", "ep")),
        P(None, ("ctx", "ep")),
        P(("ctx", "ep"), None),
        P("ep", "ctx", None),
    )
    out_specs = P("ep", "ctx", None)
    return jax.shard_map(shards, mesh=mesh, in_specs=in_specs, out_specs=out_specs, check_vma=False)
```

```python
import functools
import math

import jax
import jax.numpy as jnp
from jax import lax
from jax.experimental import pallas as pl
from jax.experimental.pallas import tpu as pltpu
from jax.sharding import PartitionSpec as P

HEADS = 16
HEAD = 128
EXPERTS = 64
FF = 1408
CAP = 2
REACH = 2
CHUNK = 256
BF = jnp.bfloat16
F32 = jnp.float32
MB = 1024 * 1024


def iota(shape, dim):
    return lax.broadcasted_iota(jnp.int32, shape, dim)


def dot(left, right):
    return jnp.dot(left, right, preferred_element_type=F32)


def dot_nt(left, right):
    return lax.dot_general(left, right, (((1,), (1,)), ((), ())), preferred_element_type=F32)


class Plan:
    def __init__(self, devices, columns, width, stretch):
        self.devices = devices
        self.columns = columns
        self.model = width
        self.stretch = stretch
        self.local = max(1, columns // FF)
        self.sharers = max(1, FF // columns)
        self.slots = self.local * CAP
        self.fold = max(1, 8 // self.slots)
        self.width = width // self.fold
        self.rows = self.slots * self.fold
        self.total = devices * self.rows
        self.chunks = self.total // CHUNK
        self.group = CHUNK // self.rows
        self.expert_rows = devices * CAP
        self.block = CHUNK if columns % CHUNK == 0 else columns
        self.steps = columns // self.block


def message_slot(plan, chunk, shape, dim):
    row = iota(shape, dim)
    device = chunk * plan.group + row // plan.rows
    within = row % plan.rows
    first = device * plan.local if plan.sharers == 1 else device // plan.sharers
    return first * CAP + within % plan.slots, within // plan.slots


def write_messages(plan, target, value, out_ref):
    for chunk in range(plan.chunks):
        wanted, piece = message_slot(plan, chunk, (CHUNK, plan.stretch), 0)
        hit = wanted == target
        total = None
        for part in range(plan.fold):
            pick = jnp.where(hit & (piece == part), 1.0, 0.0).astype(BF)
            term = dot(pick, value[:, part * plan.width:(part + 1) * plan.width])
            total = term if total is None else total + term
        out_ref[chunk * CHUNK:(chunk + 1) * CHUNK, :] = total.astype(BF)


def expert_pick(plan, expert, part, shape, row_dim, message_dim):
    row = iota(shape, row_dim)
    message = iota(shape, message_dim)
    wanted = (row // CAP) * plan.rows + part * plan.slots + expert * CAP + row % CAP
    return jnp.where(wanted == message, 1.0, 0.0).astype(BF)


def read_expert_rows(plan, message_ref, rows_ref):
    count = plan.group * CAP
    for expert in range(plan.local):
        for part in range(plan.fold):
            pick = expert_pick(plan, expert, part, (count, CHUNK), 0, 1)
            for chunk in range(plan.chunks):
                base = expert * plan.expert_rows + chunk * count
                got = dot(pick, message_ref[chunk * CHUNK:(chunk + 1) * CHUNK, :])
                rows_ref[base:base + count, part * plan.width:(part + 1) * plan.width] = got.astype(BF)


def write_expert_rows(plan, columns, message_ref):
    count = plan.local * plan.expert_rows
    for chunk in range(plan.chunks):
        message = iota((CHUNK, count), 0) + chunk * CHUNK
        row = iota((CHUNK, count), 1)
        sender = (row % plan.expert_rows) // CAP
        slot = (row // plan.expert_rows) * CAP + row % CAP
        total = None
        for part in range(plan.fold):
            wanted = sender * plan.rows + part * plan.slots + slot
            pick = jnp.where(wanted == message, 1.0, 0.0).astype(BF)
            term = dot_nt(pick, columns[part * plan.width:(part + 1) * plan.width, :])
            total = term if total is None else total + term
        message_ref[chunk * CHUNK:(chunk + 1) * CHUNK, :] = total.astype(BF)


def to_column(row):
    size = row.shape[1]
    return jnp.transpose(jnp.broadcast_to(row, (size, size)))


def grads_kernel(plan, routes_ref, weight_ref, grad_ref, message_ref, target_ref):
    size = plan.stretch
    routes = routes_ref[...].astype(F32)
    column = to_column(routes)
    earlier = iota((size, size), 0) < iota((size, size), 1)
    same = (column == routes) & earlier
    rank = jnp.sum(jnp.where(same, 1.0, 0.0), axis=0, keepdims=True).astype(jnp.int32)
    target = jnp.where(rank < CAP, routes_ref[...] * CAP + rank, -1)
    target_ref[...] = target
    weight = to_column(weight_ref[...])[:, 0:1]
    grads = (weight * grad_ref[...].astype(F32)).astype(BF)
    write_messages(plan, target, grads, message_ref)


def probs_kernel(plan, tags_ref, q_ref, k0_ref, k1a_ref, k1b_ref, k2_ref, probs_ref):
    size = plan.stretch
    tags = tags_ref[...].astype(F32)
    own, before, further = tags[2:3], tags[1:2], tags[0:1]
    column = to_column(own)
    masks = [
        (column == own) & (iota((size, size), 1) <= iota((size, size), 0)),
        column == before,
        column == further,
    ]
    for head in range(HEADS):
        span = slice(head * HEAD, (head + 1) * HEAD)
        rows = slice(head * size, (head + 1) * size)
        query = q_ref[:, span]
        key_blocks = (k0_ref[:, span], k1a_ref[:, span] + k1b_ref[:, span], k2_ref[:, span])
        scores = [
            jnp.where(mask, dot_nt(query, block) * (1.0 / math.sqrt(HEAD)), -1e30)
            for mask, block in zip(masks, key_blocks)
        ]
        top = jnp.max(
            jnp.maximum(jnp.maximum(scores[0], scores[1]), scores[2]), axis=-1, keepdims=True
        )
        weights = [jnp.exp(score - top) for score in scores]
        norm = jnp.sum(weights[0] + weights[1] + weights[2], axis=-1, keepdims=True)
        for index, weight in enumerate(weights):
            probs_ref[rows, index * size:(index + 1) * size] = (weight / norm).astype(BF)


def hidden_kernel(
    plan, target_ref, gain_ref, probs_ref, v0_ref, v1a_ref, v1b_ref, v2_ref,
    hidden_ref, inv_ref, message_ref,
):
    size = plan.stretch
    squares = jnp.zeros((size, 1), F32)
    for head in range(HEADS):
        span = slice(head * HEAD, (head + 1) * HEAD)
        rows = slice(head * size, (head + 1) * size)
        total = None
        blocks = (v0_ref[:, span], v1a_ref[:, span] + v1b_ref[:, span], v2_ref[:, span])
        for index, block in enumerate(blocks):
            term = dot(probs_ref[rows, index * size:(index + 1) * size], block)
            total = term if total is None else total + term
        hidden = total.astype(BF)
        hidden_ref[:, span] = hidden
        hidden = hidden.astype(F32)
        squares = squares + jnp.sum(hidden * hidden, axis=-1, keepdims=True)
    inv = lax.rsqrt(squares * (1.0 / plan.model) + 1e-06)
    inv_ref[...] = jnp.broadcast_to(inv, inv_ref.shape)
    normed = (hidden_ref[...].astype(F32) * inv * gain_ref[...]).astype(BF)
    write_messages(plan, target_ref[...], normed, message_ref)


def for_blocks(plan, inside, across):
    for expert in range(plan.local):
        low = -(-expert * FF // plan.block) if plan.local > 1 else 0
        high = (expert + 1) * FF // plan.block if plan.local > 1 else plan.steps
        for block in range(low, high):
            inside(expert, block * plan.block)
        if expert + 1 < plan.local and (expert + 1) * FF % plan.block:
            mask = iota((1, plan.block), 1) < (expert + 1) * FF % plan.block
            across(expert, high * plan.block, mask)


def act_kernel(
    plan, message_ref, down_hbm, gate_hbm, up_hbm, act_ref, gate_ref, up_ref,
    down_ref, rows_ref, down_sem, gate_sem, up_sem,
):
    def piece(start):
        span = pl.ds(start, plan.block)
        return pltpu.make_async_copy(
            down_hbm.at[span], down_ref.at[span], down_sem.at[start // plan.block]
        )

    gate_copy = pltpu.make_async_copy(gate_hbm, gate_ref, gate_sem)
    up_copy = pltpu.make_async_copy(up_hbm, up_ref, up_sem)
    for step in range(plan.steps):
        piece(step * plan.block).start()
    gate_copy.start()
    up_copy.start()
    read_expert_rows(plan, message_ref, rows_ref)

    def product(start):
        piece(start).wait()
        span = slice(start, start + plan.block)
        return jnp.transpose(dot_nt(down_ref[span, :], rows_ref[...]))

    def rows_of(value, expert):
        return value[expert * plan.expert_rows:(expert + 1) * plan.expert_rows, :]

    def inside(expert, start):
        act_ref[:, start:start + plan.block] = rows_of(product(start), expert)

    def across(expert, start, mask):
        value = product(start)
        act_ref[:, start:start + plan.block] = jnp.where(
            mask, rows_of(value, expert), rows_of(value, expert + 1)
        )

    for_blocks(plan, inside, across)
    gate_copy.wait()
    up_copy.wait()


def expert_kernel(
    plan, message_ref, act_ref, gate_ref, up_ref, out_ref,
    rows_ref, grad_gate_ref, grad_up_ref, sum_ref,
):
    read_expert_rows(plan, message_ref, rows_ref)

    def rows_of(expert):
        return rows_ref[expert * plan.expert_rows:(expert + 1) * plan.expert_rows, :]

    def store(expert, span, mask, gate_pre, up_pre):
        act = act_ref[:, span]
        sig = jax.nn.sigmoid(gate_pre)
        grad_gate = act * up_pre * (sig * (1.0 + gate_pre * (1.0 - sig)))
        grad_up = act * (gate_pre * sig)
        for value, ref in ((grad_gate, grad_gate_ref), (grad_up, grad_up_ref)):
            pieces = [jnp.zeros_like(value)] * plan.local
            pieces[expert] = value if mask is None else jnp.where(mask, value, 0.0)
            if mask is not None:
                pieces[expert + 1] = jnp.where(mask, 0.0, value)
            ref[:, span] = jnp.concatenate(pieces, axis=0).astype(BF)

    def inside(expert, start):
        span = slice(start, start + plan.block)
        rows = rows_of(expert)
        store(expert, span, None, dot(rows, gate_ref[:, span]), dot(rows, up_ref[:, span]))

    def across(expert, start, mask):
        span = slice(start, start + plan.block)
        gate, up = gate_ref[:, span], up_ref[:, span]
        first, second = rows_of(expert), rows_of(expert + 1)
        store(
            expert, span, mask,
            jnp.where(mask, dot(first, gate), dot(second, gate)),
            jnp.where(mask, dot(first, up), dot(second, up)),
        )

    for_blocks(plan, inside, across)

    @pl.loop(0, plan.model // CHUNK)
    def _(tile):
        span = pl.ds(pl.multiple_of(tile * CHUNK, CHUNK), CHUNK)
        total = dot_nt(gate_ref[span, :], grad_gate_ref[...])
        total = total + dot_nt(up_ref[span, :], grad_up_ref[...])
        sum_ref[span, :] = total.astype(BF)

    write_expert_rows(plan, sum_ref, out_ref)


def finish_kernel(
    plan, target_ref, gain_ref, hidden_ref, inv_ref, grad_ref, message_ref, out_ref
):
    target = to_column(target_ref[...].astype(F32))[:, 0:1].astype(jnp.int32)
    parts = [None] * plan.fold
    for chunk in range(plan.chunks):
        wanted, piece = message_slot(plan, chunk, (plan.stretch, CHUNK), 1)
        messages = message_ref[chunk * CHUNK:(chunk + 1) * CHUNK, :]
        for part in range(plan.fold):
            pick = jnp.where((wanted == target) & (piece == part), 1.0, 0.0).astype(BF)
            term = dot(pick, messages)
            parts[part] = term if parts[part] is None else parts[part] + term
    inv = inv_ref[:, 0:1]
    spans = [slice(part * plan.width, (part + 1) * plan.width) for part in range(plan.fold)]
    gained = [
        part.astype(BF).astype(F32) * gain_ref[:, span] for part, span in zip(parts, spans)
    ]
    hidden = [hidden_ref[:, span].astype(F32) for span in spans]
    moment = sum(jnp.sum(h * g, axis=-1, keepdims=True) for h, g in zip(hidden, gained))
    mean = moment * (1.0 / plan.model)
    cube = inv * inv * inv
    for h, g, span in zip(hidden, gained, spans):
        out = grad_ref[:, span].astype(F32) + inv * g - h * cube * mean
        out_ref[:, span] = out.astype(BF)


def params(limit):
    return pltpu.CompilerParams(vmem_limit_bytes=limit)


def shards(
    queries, keys, values, doc_ids, routes, route_weight, norm_gain, w_gate, w_up, w_down, grad_out
):
    stretch, model = queries.shape[1:]
    ctx_count = lax.axis_size("ctx")
    axes = ("ctx", "ep")
    plan = Plan(ctx_count * lax.axis_size("ep"), w_gate.shape[1], model, stretch)
    messages = jax.ShapeDtypeStruct((plan.total, plan.width), BF)
    message_bytes = 2 * plan.total * plan.width
    gain = norm_gain.reshape(1, model)

    def exchange(value):
        cut = value.reshape(plan.devices, plan.rows, plan.width)
        cut = lax.all_to_all(cut, axes, split_axis=0, concat_axis=0, tiled=True)
        return cut.reshape(plan.total, plan.width)

    two_up = [(source, source + 2) for source in range(ctx_count - 2)]
    even_up = [(source, source + 1) for source in range(0, ctx_count - 1, 2)]
    odd_down = [(source, source - 1) for source in range(1, ctx_count, 2)]

    own_keys, own_values = keys[0], values[0]
    far_keys = lax.ppermute(own_keys, "ctx", two_up)
    far_values = lax.ppermute(own_values, "ctx", two_up)
    even_keys = lax.ppermute(own_keys, "ctx", even_up)
    even_values = lax.ppermute(own_values, "ctx", even_up)
    odd_keys = lax.ppermute(far_keys, "ctx", odd_down)
    odd_values = lax.ppermute(far_values, "ctx", odd_down)
    all_tags = lax.all_gather(doc_ids[0] + 1, "ctx")
    all_tags = jnp.pad(all_tags, ((REACH, 0), (0, 0)))
    tags = lax.dynamic_slice_in_dim(all_tags, lax.axis_index("ctx"), REACH + 1, 0)

    grad_messages, target = pl.pallas_call(
        functools.partial(grads_kernel, plan),
        out_shape=(messages, jax.ShapeDtypeStruct((1, stretch), jnp.int32)),
        compiler_params=params(8 * MB + 3 * message_bytes),
        name="route_grads",
    )(routes.reshape(1, stretch), route_weight.reshape(1, stretch), grad_out[0])
    grad_messages, odd_keys = lax.optimization_barrier((grad_messages, odd_keys))
    got_grads = exchange(grad_messages)

    probs = pl.pallas_call(
        functools.partial(probs_kernel, plan),
        out_shape=jax.ShapeDtypeStruct((HEADS * stretch, (REACH + 1) * stretch), BF),
        compiler_params=params(16 * MB),
        name="probs",
    )(tags, queries[0], own_keys, even_keys, odd_keys, far_keys)
    hidden, inv, normed_messages = pl.pallas_call(
        functools.partial(hidden_kernel, plan),
        out_shape=(
            jax.ShapeDtypeStruct((stretch, model), BF),
            jax.ShapeDtypeStruct((stretch, 128), F32),
            messages,
        ),
        compiler_params=params(12 * MB + 3 * message_bytes),
        name="hidden",
    )(target, gain, probs, own_values, even_values, odd_values, far_values)
    got_normed = exchange(normed_messages)

    rows = plan.local * plan.expert_rows
    weight_bytes = 2 * plan.columns * model
    anywhere = pl.BlockSpec(memory_space=pl.ANY)
    inside = pl.BlockSpec(memory_space=pltpu.VMEM)
    act, gate, up = pl.pallas_call(
        functools.partial(act_kernel, plan),
        in_specs=[inside, anywhere, anywhere, anywhere],
        out_specs=[inside, anywhere, anywhere],
        out_shape=(
            jax.ShapeDtypeStruct((plan.expert_rows, plan.columns), F32),
            pltpu.VMEM(w_gate.shape, BF),
            pltpu.VMEM(w_up.shape, BF),
        ),
        scratch_shapes=[
            pltpu.VMEM(w_down.shape, BF),
            pltpu.VMEM((rows, model), BF),
            pltpu.SemaphoreType.DMA((plan.steps,)),
            pltpu.SemaphoreType.DMA,
            pltpu.SemaphoreType.DMA,
        ],
        compiler_params=params(8 * MB + 6 * message_bytes + weight_bytes),
        cost_estimate=pl.CostEstimate(
            flops=2 * plan.expert_rows * plan.columns * model,
            bytes_accessed=3 * weight_bytes,
            transcendentals=0,
        ),
        name="grad_act",
    )(got_grads, w_down, w_gate, w_up)

    returned = pl.pallas_call(
        functools.partial(expert_kernel, plan),
        out_shape=messages,
        scratch_shapes=[
            pltpu.VMEM((rows, model), BF),
            pltpu.VMEM((rows, plan.columns), BF),
            pltpu.VMEM((rows, plan.columns), BF),
            pltpu.VMEM((model, rows), BF),
        ],
        compiler_params=params(12 * MB + 6 * message_bytes),
        cost_estimate=pl.CostEstimate(
            flops=8 * plan.expert_rows * plan.columns * model,
            bytes_accessed=2 * weight_bytes,
            transcendentals=0,
        ),
        name="experts",
    )(got_normed, act, gate, up)
    combined = exchange(returned)

    grad_in = pl.pallas_call(
        functools.partial(finish_kernel, plan),
        out_shape=jax.ShapeDtypeStruct((stretch, model), BF),
        compiler_params=params(12 * MB + 3 * message_bytes),
        name="finish",
    )(target, gain, hidden, inv, grad_out[0], combined)
    return grad_in[None]


def solution(mesh):
    in_specs = (
        P("ep", "ctx", None),
        P("ep", "ctx", None),
        P("ep", "ctx", None),
        P("ep", "ctx"),
        P("ep", "ctx", None),
        P("ep", "ctx", None),
        P(),
        P(None, ("ctx", "ep")),
        P(None, ("ctx", "ep")),
        P(("ctx", "ep"), None),
        P("ep", "ctx", None),
    )
    out_specs = P("ep", "ctx", None)
    return jax.shard_map(shards, mesh=mesh, in_specs=in_specs, out_specs=out_specs, check_vma=False)
```

```python
import functools
import math

import jax
import jax.numpy as jnp
from jax import lax
from jax.experimental import pallas as pl
from jax.experimental.pallas import tpu as pltpu
from jax.sharding import PartitionSpec as P

HEADS = 16
HEAD = 128
EXPERTS = 64
FF = 1408
CAP = 2
REACH = 2
CHUNK = 256
BF = jnp.bfloat16
F32 = jnp.float32
MB = 1024 * 1024


def iota(shape, dim):
    return lax.broadcasted_iota(jnp.int32, shape, dim)


def dot(left, right):
    return jnp.dot(left, right, preferred_element_type=F32)


def dot_nt(left, right):
    return lax.dot_general(left, right, (((1,), (1,)), ((), ())), preferred_element_type=F32)


class Plan:
    def __init__(self, devices, columns, width, stretch):
        self.devices = devices
        self.columns = columns
        self.model = width
        self.stretch = stretch
        self.local = max(1, columns // FF)
        self.sharers = max(1, FF // columns)
        self.slots = self.local * CAP
        self.fold = max(1, 8 // self.slots)
        self.width = width // self.fold
        self.rows = self.slots * self.fold
        self.total = devices * self.rows
        self.chunks = self.total // CHUNK
        self.group = CHUNK // self.rows
        self.expert_rows = devices * CAP
        self.block = CHUNK if columns % CHUNK == 0 else columns
        self.steps = columns // self.block


def message_slot(plan, chunk, shape, dim):
    row = iota(shape, dim)
    device = chunk * plan.group + row // plan.rows
    within = row % plan.rows
    first = device * plan.local if plan.sharers == 1 else device // plan.sharers
    return first * CAP + within % plan.slots, within // plan.slots


def write_messages(plan, target, value, out_ref):
    for chunk in range(plan.chunks):
        wanted, piece = message_slot(plan, chunk, (CHUNK, plan.stretch), 0)
        hit = wanted == target
        total = None
        for part in range(plan.fold):
            pick = jnp.where(hit & (piece == part), 1.0, 0.0).astype(BF)
            term = dot(pick, value[:, part * plan.width:(part + 1) * plan.width])
            total = term if total is None else total + term
        out_ref[chunk * CHUNK:(chunk + 1) * CHUNK, :] = total.astype(BF)


def expert_pick(plan, expert, part, shape, row_dim, message_dim):
    row = iota(shape, row_dim)
    message = iota(shape, message_dim)
    wanted = (row // CAP) * plan.rows + part * plan.slots + expert * CAP + row % CAP
    return jnp.where(wanted == message, 1.0, 0.0).astype(BF)


def read_expert_rows(plan, message_ref, rows_ref):
    count = plan.group * CAP
    for expert in range(plan.local):
        for part in range(plan.fold):
            pick = expert_pick(plan, expert, part, (count, CHUNK), 0, 1)
            for chunk in range(plan.chunks):
                base = expert * plan.expert_rows + chunk * count
                got = dot(pick, message_ref[chunk * CHUNK:(chunk + 1) * CHUNK, :])
                rows_ref[base:base + count, part * plan.width:(part + 1) * plan.width] = got.astype(BF)


def write_expert_rows(plan, columns, message_ref):
    count = plan.local * plan.expert_rows
    for chunk in range(plan.chunks):
        message = iota((CHUNK, count), 0) + chunk * CHUNK
        row = iota((CHUNK, count), 1)
        sender = (row % plan.expert_rows) // CAP
        slot = (row // plan.expert_rows) * CAP + row % CAP
        total = None
        for part in range(plan.fold):
            wanted = sender * plan.rows + part * plan.slots + slot
            pick = jnp.where(wanted == message, 1.0, 0.0).astype(BF)
            term = dot_nt(pick, columns[part * plan.width:(part + 1) * plan.width, :])
            total = term if total is None else total + term
        message_ref[chunk * CHUNK:(chunk + 1) * CHUNK, :] = total.astype(BF)


def to_column(row):
    size = row.shape[1]
    return jnp.transpose(jnp.broadcast_to(row, (size, size)))


def grads_kernel(plan, routes_ref, weight_ref, grad_ref, message_ref, target_ref):
    size = plan.stretch
    routes = routes_ref[...].astype(F32)
    column = to_column(routes)
    earlier = iota((size, size), 0) < iota((size, size), 1)
    same = (column == routes) & earlier
    rank = jnp.sum(jnp.where(same, 1.0, 0.0), axis=0, keepdims=True).astype(jnp.int32)
    target = jnp.where(rank < CAP, routes_ref[...] * CAP + rank, -1)
    target_ref[...] = target
    weight = to_column(weight_ref[...])[:, 0:1]
    grads = (weight * grad_ref[...].astype(F32)).astype(BF)
    write_messages(plan, target, grads, message_ref)


def probs_kernel(plan, tags_ref, q_ref, k0_ref, k1a_ref, k1b_ref, k2_ref, probs_ref):
    size = plan.stretch
    tags = tags_ref[...].astype(F32)
    own, before, further = tags[2:3], tags[1:2], tags[0:1]
    column = to_column(own)
    masks = [
        (column == own) & (iota((size, size), 1) <= iota((size, size), 0)),
        column == before,
        column == further,
    ]
    for head in range(HEADS):
        span = slice(head * HEAD, (head + 1) * HEAD)
        rows = slice(head * size, (head + 1) * size)
        query = q_ref[:, span]
        key_blocks = (k0_ref[:, span], k1a_ref[:, span] + k1b_ref[:, span], k2_ref[:, span])
        scores = [
            jnp.where(mask, dot_nt(query, block) * (1.0 / math.sqrt(HEAD)), -1e30)
            for mask, block in zip(masks, key_blocks)
        ]
        top = jnp.max(
            jnp.maximum(jnp.maximum(scores[0], scores[1]), scores[2]), axis=-1, keepdims=True
        )
        weights = [jnp.exp(score - top) for score in scores]
        norm = jnp.sum(weights[0] + weights[1] + weights[2], axis=-1, keepdims=True)
        for index, weight in enumerate(weights):
            probs_ref[rows, index * size:(index + 1) * size] = (weight / norm).astype(BF)


def hidden_kernel(
    plan, target_ref, gain_ref, probs_ref, v0_ref, v1a_ref, v1b_ref, v2_ref,
    hidden_ref, inv_ref, message_ref,
):
    size = plan.stretch
    squares = jnp.zeros((size, 1), F32)
    for head in range(HEADS):
        span = slice(head * HEAD, (head + 1) * HEAD)
        rows = slice(head * size, (head + 1) * size)
        total = None
        blocks = (v0_ref[:, span], v1a_ref[:, span] + v1b_ref[:, span], v2_ref[:, span])
        for index, block in enumerate(blocks):
            term = dot(probs_ref[rows, index * size:(index + 1) * size], block)
            total = term if total is None else total + term
        hidden = total.astype(BF)
        hidden_ref[:, span] = hidden
        hidden = hidden.astype(F32)
        squares = squares + jnp.sum(hidden * hidden, axis=-1, keepdims=True)
    inv = lax.rsqrt(squares * (1.0 / plan.model) + 1e-06)
    inv_ref[...] = jnp.broadcast_to(inv, inv_ref.shape)
    normed = (hidden_ref[...].astype(F32) * inv * gain_ref[...]).astype(BF)
    write_messages(plan, target_ref[...], normed, message_ref)


def for_blocks(plan, inside, across):
    for expert in range(plan.local):
        low = -(-expert * FF // plan.block) if plan.local > 1 else 0
        high = (expert + 1) * FF // plan.block if plan.local > 1 else plan.steps
        for block in range(low, high):
            inside(expert, block * plan.block)
        if expert + 1 < plan.local and (expert + 1) * FF % plan.block:
            mask = iota((1, plan.block), 1) < (expert + 1) * FF % plan.block
            across(expert, high * plan.block, mask)


def act_kernel(plan, message_ref, down_hbm, act_ref, down_ref, rows_ref, down_sem):
    def piece(start):
        span = pl.ds(start, plan.block)
        return pltpu.make_async_copy(
            down_hbm.at[span], down_ref.at[span], down_sem.at[start // plan.block]
        )

    for step in range(plan.steps):
        piece(step * plan.block).start()
    read_expert_rows(plan, message_ref, rows_ref)

    def product(start):
        piece(start).wait()
        span = slice(start, start + plan.block)
        return jnp.transpose(dot_nt(down_ref[span, :], rows_ref[...]))

    def rows_of(value, expert):
        return value[expert * plan.expert_rows:(expert + 1) * plan.expert_rows, :]

    def inside(expert, start):
        act_ref[:, start:start + plan.block] = rows_of(product(start), expert)

    def across(expert, start, mask):
        value = product(start)
        act_ref[:, start:start + plan.block] = jnp.where(
            mask, rows_of(value, expert), rows_of(value, expert + 1)
        )

    for_blocks(plan, inside, across)


def expert_kernel(
    plan, message_ref, act_ref, gate_hbm, up_hbm, out_ref,
    gate_ref, up_ref, rows_ref, grad_gate_ref, grad_up_ref, sum_ref, gate_sem, up_sem,
):
    def pieces_at(start):
        span = pl.ds(start, plan.block)
        index = start // plan.block
        return (
            pltpu.make_async_copy(gate_hbm.at[:, span], gate_ref.at[:, span], gate_sem.at[index]),
            pltpu.make_async_copy(up_hbm.at[:, span], up_ref.at[:, span], up_sem.at[index]),
        )

    for step in range(plan.steps):
        for piece in pieces_at(step * plan.block):
            piece.start()
    read_expert_rows(plan, message_ref, rows_ref)

    def arrive(start):
        for piece in pieces_at(start):
            piece.wait()

    def rows_of(expert):
        return rows_ref[expert * plan.expert_rows:(expert + 1) * plan.expert_rows, :]

    def store(expert, span, mask, gate_pre, up_pre):
        act = act_ref[:, span]
        sig = jax.nn.sigmoid(gate_pre)
        grad_gate = act * up_pre * (sig * (1.0 + gate_pre * (1.0 - sig)))
        grad_up = act * (gate_pre * sig)
        for value, ref in ((grad_gate, grad_gate_ref), (grad_up, grad_up_ref)):
            pieces = [jnp.zeros_like(value)] * plan.local
            pieces[expert] = value if mask is None else jnp.where(mask, value, 0.0)
            if mask is not None:
                pieces[expert + 1] = jnp.where(mask, 0.0, value)
            ref[:, span] = jnp.concatenate(pieces, axis=0).astype(BF)

    def inside(expert, start):
        arrive(start)
        span = slice(start, start + plan.block)
        rows = rows_of(expert)
        store(expert, span, None, dot(rows, gate_ref[:, span]), dot(rows, up_ref[:, span]))

    def across(expert, start, mask):
        arrive(start)
        span = slice(start, start + plan.block)
        gate, up = gate_ref[:, span], up_ref[:, span]
        first, second = rows_of(expert), rows_of(expert + 1)
        store(
            expert, span, mask,
            jnp.where(mask, dot(first, gate), dot(second, gate)),
            jnp.where(mask, dot(first, up), dot(second, up)),
        )

    for_blocks(plan, inside, across)

    @pl.loop(0, plan.model // CHUNK)
    def _(tile):
        span = pl.ds(pl.multiple_of(tile * CHUNK, CHUNK), CHUNK)
        total = dot_nt(gate_ref[span, :], grad_gate_ref[...])
        total = total + dot_nt(up_ref[span, :], grad_up_ref[...])
        sum_ref[span, :] = total.astype(BF)

    write_expert_rows(plan, sum_ref, out_ref)


def finish_kernel(
    plan, target_ref, gain_ref, hidden_ref, inv_ref, grad_ref, message_ref, out_ref
):
    target = to_column(target_ref[...].astype(F32))[:, 0:1].astype(jnp.int32)
    parts = [None] * plan.fold
    for chunk in range(plan.chunks):
        wanted, piece = message_slot(plan, chunk, (plan.stretch, CHUNK), 1)
        messages = message_ref[chunk * CHUNK:(chunk + 1) * CHUNK, :]
        for part in range(plan.fold):
            pick = jnp.where((wanted == target) & (piece == part), 1.0, 0.0).astype(BF)
            term = dot(pick, messages)
            parts[part] = term if parts[part] is None else parts[part] + term
    inv = inv_ref[:, 0:1]
    spans = [slice(part * plan.width, (part + 1) * plan.width) for part in range(plan.fold)]
    gained = [
        part.astype(BF).astype(F32) * gain_ref[:, span] for part, span in zip(parts, spans)
    ]
    hidden = [hidden_ref[:, span].astype(F32) for span in spans]
    moment = sum(jnp.sum(h * g, axis=-1, keepdims=True) for h, g in zip(hidden, gained))
    mean = moment * (1.0 / plan.model)
    cube = inv * inv * inv
    for h, g, span in zip(hidden, gained, spans):
        out = grad_ref[:, span].astype(F32) + inv * g - h * cube * mean
        out_ref[:, span] = out.astype(BF)


def params(limit):
    return pltpu.CompilerParams(vmem_limit_bytes=limit)


def estimate(microseconds):
    return pl.CostEstimate(
        flops=0, bytes_accessed=microseconds * 3_600_000, transcendentals=0
    )


def shards(
    queries, keys, values, doc_ids, routes, route_weight, norm_gain, w_gate, w_up, w_down, grad_out
):
    stretch, model = queries.shape[1:]
    ctx_count = lax.axis_size("ctx")
    axes = ("ctx", "ep")
    plan = Plan(ctx_count * lax.axis_size("ep"), w_gate.shape[1], model, stretch)
    messages = jax.ShapeDtypeStruct((plan.total, plan.width), BF)
    message_bytes = 2 * plan.total * plan.width
    gain = norm_gain.reshape(1, model)

    def exchange(value):
        cut = value.reshape(plan.devices, plan.rows, plan.width)
        cut = lax.all_to_all(cut, axes, split_axis=0, concat_axis=0, tiled=True)
        return cut.reshape(plan.total, plan.width)

    two_up = [(source, source + 2) for source in range(ctx_count - 2)]
    even_up = [(source, source + 1) for source in range(0, ctx_count - 1, 2)]
    odd_down = [(source, source - 1) for source in range(1, ctx_count, 2)]

    own_keys, own_values = keys[0], values[0]
    def send(value, route):
        return lax.ppermute(value, "ctx", route)

    own_tags = doc_ids + 1
    far_keys, even_keys = send(own_keys, two_up), send(own_keys, even_up)
    far_keys, even_keys, sent_values, sent_tags = lax.optimization_barrier(
        (far_keys, even_keys, own_values, own_tags)
    )
    odd_keys = send(far_keys, odd_down)
    far_values, even_values = send(sent_values, two_up), send(sent_values, even_up)
    far_tags, even_tags = send(sent_tags, two_up), send(sent_tags, even_up)

    grad_messages, target = pl.pallas_call(
        functools.partial(grads_kernel, plan),
        out_shape=(messages, jax.ShapeDtypeStruct((1, stretch), jnp.int32)),
        compiler_params=params(8 * MB + 3 * message_bytes),
        name="route_grads",
    )(routes.reshape(1, stretch), route_weight.reshape(1, stretch), grad_out[0])
    odd_keys, far_values, even_values, far_tags, even_tags, grad_messages = (
        lax.optimization_barrier(
            (odd_keys, far_values, even_values, far_tags, even_tags, grad_messages)
        )
    )
    odd_values = send(far_values, odd_down)
    odd_tags = send(far_tags, odd_down)
    got_grads = exchange(grad_messages)
    tags = jnp.concatenate([far_tags, even_tags + odd_tags, own_tags])

    probs = pl.pallas_call(
        functools.partial(probs_kernel, plan),
        out_shape=jax.ShapeDtypeStruct((HEADS * stretch, (REACH + 1) * stretch), BF),
        compiler_params=params(16 * MB),
        cost_estimate=estimate(4),
        name="probs",
    )(tags, queries[0], own_keys, even_keys, odd_keys, far_keys)
    hidden, inv, normed_messages = pl.pallas_call(
        functools.partial(hidden_kernel, plan),
        out_shape=(
            jax.ShapeDtypeStruct((stretch, model), BF),
            jax.ShapeDtypeStruct((stretch, 128), F32),
            messages,
        ),
        compiler_params=params(12 * MB + 3 * message_bytes),
        cost_estimate=estimate(16),
        name="hidden",
    )(target, gain, probs, own_values, even_values, odd_values, far_values)
    got_normed = exchange(normed_messages)

    rows = plan.local * plan.expert_rows
    weight_bytes = 2 * plan.columns * model
    anywhere = pl.BlockSpec(memory_space=pl.ANY)
    inside = pl.BlockSpec(memory_space=pltpu.VMEM)
    act = pl.pallas_call(
        functools.partial(act_kernel, plan),
        in_specs=[inside, anywhere],
        out_shape=jax.ShapeDtypeStruct((plan.expert_rows, plan.columns), F32),
        scratch_shapes=[
            pltpu.VMEM(w_down.shape, BF),
            pltpu.VMEM((rows, model), BF),
            pltpu.SemaphoreType.DMA((plan.steps,)),
        ],
        compiler_params=params(8 * MB + 6 * message_bytes + weight_bytes),
        cost_estimate=pl.CostEstimate(
            flops=2 * plan.expert_rows * plan.columns * model,
            bytes_accessed=weight_bytes,
            transcendentals=0,
        ),
        name="grad_act",
    )(got_grads, w_down)

    returned = pl.pallas_call(
        functools.partial(expert_kernel, plan),
        in_specs=[inside, inside, anywhere, anywhere],
        out_shape=messages,
        scratch_shapes=[
            pltpu.VMEM(w_gate.shape, BF),
            pltpu.VMEM(w_up.shape, BF),
            pltpu.VMEM((rows, model), BF),
            pltpu.VMEM((rows, plan.columns), BF),
            pltpu.VMEM((rows, plan.columns), BF),
            pltpu.VMEM((model, rows), BF),
            pltpu.SemaphoreType.DMA((plan.steps,)),
            pltpu.SemaphoreType.DMA((plan.steps,)),
        ],
        compiler_params=params(12 * MB + 6 * message_bytes + 2 * weight_bytes),
        cost_estimate=pl.CostEstimate(
            flops=8 * plan.expert_rows * plan.columns * model,
            bytes_accessed=2 * weight_bytes,
            transcendentals=0,
        ),
        name="experts",
    )(got_normed, act, w_gate, w_up)
    combined = exchange(returned)

    grad_in = pl.pallas_call(
        functools.partial(finish_kernel, plan),
        out_shape=jax.ShapeDtypeStruct((stretch, model), BF),
        compiler_params=params(12 * MB + 3 * message_bytes),
        name="finish",
    )(target, gain, hidden, inv, grad_out[0], combined)
    return grad_in[None]


def solution(mesh):
    in_specs = (
        P("ep", "ctx", None),
        P("ep", "ctx", None),
        P("ep", "ctx", None),
        P("ep", "ctx"),
        P("ep", "ctx", None),
        P("ep", "ctx", None),
        P(),
        P(None, ("ctx", "ep")),
        P(None, ("ctx", "ep")),
        P(("ctx", "ep"), None),
        P("ep", "ctx", None),
    )
    out_specs = P("ep", "ctx", None)
    return jax.shard_map(shards, mesh=mesh, in_specs=in_specs, out_specs=out_specs, check_vma=False)
```

```python
import functools
import math

import jax
import jax.numpy as jnp
from jax import lax
from jax.experimental import pallas as pl
from jax.experimental.pallas import tpu as pltpu
from jax.sharding import PartitionSpec as P

HEADS = 16
HEAD = 128
EXPERTS = 64
FF = 1408
CAP = 2
CHUNK = 256
TAG_ROWS = 16
BF = jnp.bfloat16
F32 = jnp.float32
MB = 1024 * 1024


def iota(shape, dim):
    return lax.broadcasted_iota(jnp.int32, shape, dim)


def dot(left, right):
    return jnp.dot(left, right, preferred_element_type=F32)


def dot_nt(left, right):
    return lax.dot_general(left, right, (((1,), (1,)), ((), ())), preferred_element_type=F32)


class Plan:
    def __init__(self, devices, columns, width, stretch):
        self.devices = devices
        self.columns = columns
        self.model = width
        self.stretch = stretch
        self.local = max(1, columns // FF)
        self.sharers = max(1, FF // columns)
        self.slots = self.local * CAP
        self.fold = max(1, 8 // self.slots)
        self.width = width // self.fold
        self.rows = self.slots * self.fold
        self.total = devices * self.rows
        self.chunks = self.total // CHUNK
        self.group = CHUNK // self.rows
        self.expert_rows = devices * CAP
        self.block = CHUNK if columns % CHUNK == 0 else columns
        self.steps = columns // self.block


def message_slot(plan, chunk, shape, dim):
    row = iota(shape, dim)
    device = chunk * plan.group + row // plan.rows
    within = row % plan.rows
    first = device * plan.local if plan.sharers == 1 else device // plan.sharers
    return first * CAP + within % plan.slots, within // plan.slots


def write_messages(plan, target, value, out_ref):
    for chunk in range(plan.chunks):
        wanted, piece = message_slot(plan, chunk, (CHUNK, plan.stretch), 0)
        hit = wanted == target
        total = None
        for part in range(plan.fold):
            pick = jnp.where(hit & (piece == part), 1.0, 0.0).astype(BF)
            term = dot(pick, value[:, part * plan.width:(part + 1) * plan.width])
            total = term if total is None else total + term
        out_ref[chunk * CHUNK:(chunk + 1) * CHUNK, :] = total.astype(BF)


def expert_pick(plan, expert, part, shape, row_dim, message_dim):
    row = iota(shape, row_dim)
    message = iota(shape, message_dim)
    wanted = (row // CAP) * plan.rows + part * plan.slots + expert * CAP + row % CAP
    return jnp.where(wanted == message, 1.0, 0.0).astype(BF)


def read_expert_rows(plan, message_ref, rows_ref):
    count = plan.group * CAP
    for expert in range(plan.local):
        for part in range(plan.fold):
            pick = expert_pick(plan, expert, part, (count, CHUNK), 0, 1)
            for chunk in range(plan.chunks):
                base = expert * plan.expert_rows + chunk * count
                got = dot(pick, message_ref[chunk * CHUNK:(chunk + 1) * CHUNK, :])
                rows_ref[base:base + count, part * plan.width:(part + 1) * plan.width] = got.astype(BF)


def write_expert_rows(plan, columns, message_ref):
    count = plan.local * plan.expert_rows
    for chunk in range(plan.chunks):
        message = iota((CHUNK, count), 0) + chunk * CHUNK
        row = iota((CHUNK, count), 1)
        sender = (row % plan.expert_rows) // CAP
        slot = (row // plan.expert_rows) * CAP + row % CAP
        total = None
        for part in range(plan.fold):
            wanted = sender * plan.rows + part * plan.slots + slot
            pick = jnp.where(wanted == message, 1.0, 0.0).astype(BF)
            term = dot_nt(pick, columns[part * plan.width:(part + 1) * plan.width, :])
            total = term if total is None else total + term
        message_ref[chunk * CHUNK:(chunk + 1) * CHUNK, :] = total.astype(BF)


def to_column(row):
    size = row.shape[1]
    return jnp.transpose(jnp.broadcast_to(row, (size, size)))


def grads_kernel(plan, routes_ref, weight_ref, grad_ref, message_ref, target_ref):
    size = plan.stretch
    routes = routes_ref[...].astype(F32)
    column = to_column(routes)
    earlier = iota((size, size), 0) < iota((size, size), 1)
    same = (column == routes) & earlier
    rank = jnp.sum(jnp.where(same, 1.0, 0.0), axis=0, keepdims=True).astype(jnp.int32)
    target = jnp.where(rank < CAP, routes_ref[...] * CAP + rank, -1)
    target_ref[...] = target
    weight = to_column(weight_ref[...])[:, 0:1]
    grads = (weight * grad_ref[...].astype(F32)).astype(BF)
    write_messages(plan, target, grads, message_ref)


def softmax_kernel(
    plan, tags_ref, q_hbm, k0_hbm, v0_hbm, k1_ref, k2_ref, v2_ref, probs_ref, part_ref,
    q_ref, k0_ref, v0_ref, sems,
):
    size = plan.stretch
    copies = [
        pltpu.make_async_copy(source, held, sems.at[index])
        for index, (source, held) in enumerate(
            ((q_hbm, q_ref), (k0_hbm, k0_ref), (v0_hbm, v0_ref))
        )
    ]
    for copy in copies:
        copy.start()
    own = tags_ref[...].astype(F32)
    before = k1_ref[size:size + TAG_ROWS, 0:size].astype(F32)[0:1]
    further = k2_ref[size:size + TAG_ROWS, 0:size].astype(F32)[0:1]
    column = to_column(own)
    masks = [
        (column == own) & (iota((size, size), 1) <= iota((size, size), 0)),
        column == before,
        column == further,
    ]
    for copy in copies:
        copy.wait()
    for head in range(HEADS):
        span = slice(head * HEAD, (head + 1) * HEAD)
        rows = slice(head * size, (head + 1) * size)
        query = q_ref[:, span]
        scores = [
            jnp.where(mask, dot_nt(query, ref[0:size, span]) * (1.0 / math.sqrt(HEAD)), -1e30)
            for mask, ref in zip(masks, (k0_ref, k1_ref, k2_ref))
        ]
        top = jnp.max(
            jnp.maximum(jnp.maximum(scores[0], scores[1]), scores[2]), axis=-1, keepdims=True
        )
        weights = [jnp.exp(score - top) for score in scores]
        norm = jnp.sum(weights[0] + weights[1] + weights[2], axis=-1, keepdims=True)
        probs = [(weight / norm).astype(BF) for weight in weights]
        probs_ref[rows, :] = probs[1]
        part_ref[:, span] = dot(probs[0], v0_ref[:, span]) + dot(probs[2], v2_ref[:, span])


def hidden_kernel(
    plan, target_ref, gain_ref, probs_ref, part_ref, swapped_ref, relayed_ref,
    hidden_ref, inv_ref, message_ref,
):
    size = plan.stretch
    odd = lax.axis_index("ctx") % 2 == 1
    squares = jnp.zeros((size, 1), F32)
    for head in range(HEADS):
        span = slice(head * HEAD, (head + 1) * HEAD)
        rows = slice(head * size, (head + 1) * size)
        near = jnp.where(odd, swapped_ref[:, span], relayed_ref[:, span])
        hidden = (part_ref[:, span] + dot(probs_ref[rows, :], near)).astype(BF)
        hidden_ref[:, span] = hidden
        hidden = hidden.astype(F32)
        squares = squares + jnp.sum(hidden * hidden, axis=-1, keepdims=True)
    inv = lax.rsqrt(squares * (1.0 / plan.model) + 1e-06)
    inv_ref[...] = jnp.broadcast_to(inv, inv_ref.shape)
    normed = (hidden_ref[...].astype(F32) * inv * gain_ref[...]).astype(BF)
    write_messages(plan, target_ref[...], normed, message_ref)


def for_blocks(plan, inside, across):
    for expert in range(plan.local):
        low = -(-expert * FF // plan.block) if plan.local > 1 else 0
        high = (expert + 1) * FF // plan.block if plan.local > 1 else plan.steps
        for block in range(low, high):
            inside(expert, block * plan.block)
        if expert + 1 < plan.local and (expert + 1) * FF % plan.block:
            mask = iota((1, plan.block), 1) < (expert + 1) * FF % plan.block
            across(expert, high * plan.block, mask)


def act_kernel(plan, message_ref, down_hbm, act_ref, down_ref, rows_ref, down_sem):
    def piece(start):
        span = pl.ds(start, plan.block)
        return pltpu.make_async_copy(
            down_hbm.at[span], down_ref.at[span], down_sem.at[start // plan.block]
        )

    for step in range(plan.steps):
        piece(step * plan.block).start()
    read_expert_rows(plan, message_ref, rows_ref)

    def product(start):
        piece(start).wait()
        span = slice(start, start + plan.block)
        return jnp.transpose(dot_nt(down_ref[span, :], rows_ref[...]))

    def rows_of(value, expert):
        return value[expert * plan.expert_rows:(expert + 1) * plan.expert_rows, :]

    def inside(expert, start):
        act_ref[:, start:start + plan.block] = rows_of(product(start), expert)

    def across(expert, start, mask):
        value = product(start)
        act_ref[:, start:start + plan.block] = jnp.where(
            mask, rows_of(value, expert), rows_of(value, expert + 1)
        )

    for_blocks(plan, inside, across)


def expert_kernel(
    plan, message_ref, act_ref, gate_hbm, up_hbm, out_ref,
    gate_ref, up_ref, rows_ref, grad_gate_ref, grad_up_ref, sum_ref, gate_sem, up_sem,
):
    def pieces_at(start):
        span = pl.ds(start, plan.block)
        index = start // plan.block
        return (
            pltpu.make_async_copy(gate_hbm.at[:, span], gate_ref.at[:, span], gate_sem.at[index]),
            pltpu.make_async_copy(up_hbm.at[:, span], up_ref.at[:, span], up_sem.at[index]),
        )

    for step in range(plan.steps):
        for piece in pieces_at(step * plan.block):
            piece.start()
    read_expert_rows(plan, message_ref, rows_ref)

    def arrive(start):
        for piece in pieces_at(start):
            piece.wait()

    def rows_of(expert):
        return rows_ref[expert * plan.expert_rows:(expert + 1) * plan.expert_rows, :]

    def store(expert, span, mask, gate_pre, up_pre):
        act = act_ref[:, span]
        sig = jax.nn.sigmoid(gate_pre)
        grad_gate = act * up_pre * (sig * (1.0 + gate_pre * (1.0 - sig)))
        grad_up = act * (gate_pre * sig)
        for value, ref in ((grad_gate, grad_gate_ref), (grad_up, grad_up_ref)):
            pieces = [jnp.zeros_like(value)] * plan.local
            pieces[expert] = value if mask is None else jnp.where(mask, value, 0.0)
            if mask is not None:
                pieces[expert + 1] = jnp.where(mask, 0.0, value)
            ref[:, span] = jnp.concatenate(pieces, axis=0).astype(BF)

    def inside(expert, start):
        arrive(start)
        span = slice(start, start + plan.block)
        rows = rows_of(expert)
        store(expert, span, None, dot(rows, gate_ref[:, span]), dot(rows, up_ref[:, span]))

    def across(expert, start, mask):
        arrive(start)
        span = slice(start, start + plan.block)
        gate, up = gate_ref[:, span], up_ref[:, span]
        first, second = rows_of(expert), rows_of(expert + 1)
        store(
            expert, span, mask,
            jnp.where(mask, dot(first, gate), dot(second, gate)),
            jnp.where(mask, dot(first, up), dot(second, up)),
        )

    for_blocks(plan, inside, across)

    @pl.loop(0, plan.model // CHUNK)
    def _(tile):
        span = pl.ds(pl.multiple_of(tile * CHUNK, CHUNK), CHUNK)
        total = dot_nt(gate_ref[span, :], grad_gate_ref[...])
        total = total + dot_nt(up_ref[span, :], grad_up_ref[...])
        sum_ref[span, :] = total.astype(BF)

    write_expert_rows(plan, sum_ref, out_ref)


def finish_kernel(
    plan, target_ref, gain_ref, hidden_ref, inv_ref, grad_ref, message_ref, out_ref
):
    target = to_column(target_ref[...].astype(F32))[:, 0:1].astype(jnp.int32)
    parts = [None] * plan.fold
    for chunk in range(plan.chunks):
        wanted, piece = message_slot(plan, chunk, (plan.stretch, CHUNK), 1)
        messages = message_ref[chunk * CHUNK:(chunk + 1) * CHUNK, :]
        for part in range(plan.fold):
            pick = jnp.where((wanted == target) & (piece == part), 1.0, 0.0).astype(BF)
            term = dot(pick, messages)
            parts[part] = term if parts[part] is None else parts[part] + term
    inv = inv_ref[:, 0:1]
    spans = [slice(part * plan.width, (part + 1) * plan.width) for part in range(plan.fold)]
    gained = [
        part.astype(BF).astype(F32) * gain_ref[:, span] for part, span in zip(parts, spans)
    ]
    hidden = [hidden_ref[:, span].astype(F32) for span in spans]
    moment = sum(jnp.sum(h * g, axis=-1, keepdims=True) for h, g in zip(hidden, gained))
    mean = moment * (1.0 / plan.model)
    cube = inv * inv * inv
    for h, g, span in zip(hidden, gained, spans):
        out = grad_ref[:, span].astype(F32) + inv * g - h * cube * mean
        out_ref[:, span] = out.astype(BF)


def params(limit):
    return pltpu.CompilerParams(vmem_limit_bytes=limit)


def in_hbm(value):
    return pltpu.with_memory_space_constraint(value, pltpu.HBM)


def shards(
    queries, keys, values, doc_ids, routes, route_weight, norm_gain, w_gate, w_up, w_down, grad_out
):
    stretch, model = queries.shape[1:]
    ctx_count = lax.axis_size("ctx")
    axes = ("ctx", "ep")
    plan = Plan(ctx_count * lax.axis_size("ep"), w_gate.shape[1], model, stretch)
    messages = jax.ShapeDtypeStruct((plan.total, plan.width), BF)
    message_bytes = 2 * plan.total * plan.width
    gain = norm_gain.reshape(1, model)

    def exchange(value):
        cut = value.reshape(plan.devices, plan.rows, plan.width)
        cut = lax.all_to_all(cut, axes, split_axis=0, concat_axis=0, tiled=True)
        return cut.reshape(plan.total, plan.width)

    one_up = [(source, source + 1) for source in range(ctx_count - 1)]
    two_up = [(source, source + 2) for source in range(ctx_count - 2)]
    even_two_up = [(source, source + 2) for source in range(0, ctx_count - 2, 2)]
    pairs = [(source, source ^ 1) for source in range(ctx_count)]

    def send(value, route):
        return lax.ppermute(value, "ctx", route)

    own_values = values[0]
    swapped_values = send(own_values, pairs)
    far_values = send(own_values, two_up)
    own_tags = doc_ids + 1
    tag_row = jnp.pad(own_tags.astype(BF), ((0, TAG_ROWS - 1), (0, model - stretch)))
    tagged_keys = jnp.concatenate([keys[0], tag_row])
    near_keys, far_keys = send(tagged_keys, one_up), send(tagged_keys, two_up)
    relayed_values = send(swapped_values, even_two_up)

    grad_messages, target = pl.pallas_call(
        functools.partial(grads_kernel, plan),
        out_shape=(messages, jax.ShapeDtypeStruct((1, stretch), jnp.int32)),
        compiler_params=params(8 * MB + 3 * message_bytes),
        name="route_grads",
    )(routes.reshape(1, stretch), route_weight.reshape(1, stretch), grad_out[0])
    grad_messages, _ = lax.optimization_barrier((grad_messages, swapped_values))
    got_grads = exchange(grad_messages)

    inside = pl.BlockSpec(memory_space=pltpu.VMEM)
    outside = pl.BlockSpec(memory_space=pltpu.HBM)
    block = (stretch, model)
    probs, part = pl.pallas_call(
        functools.partial(softmax_kernel, plan),
        in_specs=[inside, outside, outside, outside, inside, inside, inside],
        out_shape=(
            jax.ShapeDtypeStruct((HEADS * stretch, stretch), BF),
            jax.ShapeDtypeStruct(block, F32),
        ),
        scratch_shapes=[pltpu.VMEM(block, BF)] * 3 + [pltpu.SemaphoreType.DMA((3,))],
        compiler_params=params(16 * MB),
        name="softmax",
    )(
        own_tags, in_hbm(queries[0]), in_hbm(keys[0]), in_hbm(own_values), near_keys, far_keys,
        far_values,
    )
    hidden, inv, normed_messages = pl.pallas_call(
        functools.partial(hidden_kernel, plan),
        out_shape=(
            jax.ShapeDtypeStruct(block, BF),
            jax.ShapeDtypeStruct((stretch, 128), F32),
            messages,
        ),
        compiler_params=params(12 * MB + 3 * message_bytes),
        name="hidden",
    )(target, gain, probs, part, swapped_values, relayed_values)
    got_normed = exchange(normed_messages)

    rows = plan.local * plan.expert_rows
    weight_bytes = 2 * plan.columns * model
    act = pl.pallas_call(
        functools.partial(act_kernel, plan),
        in_specs=[inside, outside],
        out_shape=jax.ShapeDtypeStruct((plan.expert_rows, plan.columns), F32),
        scratch_shapes=[
            pltpu.VMEM(w_down.shape, BF),
            pltpu.VMEM((rows, model), BF),
            pltpu.SemaphoreType.DMA((plan.steps,)),
        ],
        compiler_params=params(8 * MB + 6 * message_bytes + weight_bytes),
        cost_estimate=pl.CostEstimate(
            flops=2 * plan.expert_rows * plan.columns * model,
            bytes_accessed=weight_bytes,
            transcendentals=0,
        ),
        name="grad_act",
    )(got_grads, in_hbm(w_down))

    returned = pl.pallas_call(
        functools.partial(expert_kernel, plan),
        in_specs=[inside, inside, outside, outside],
        out_shape=messages,
        scratch_shapes=[
            pltpu.VMEM(w_gate.shape, BF),
            pltpu.VMEM(w_up.shape, BF),
            pltpu.VMEM((rows, model), BF),
            pltpu.VMEM((rows, plan.columns), BF),
            pltpu.VMEM((rows, plan.columns), BF),
            pltpu.VMEM((model, rows), BF),
            pltpu.SemaphoreType.DMA((plan.steps,)),
            pltpu.SemaphoreType.DMA((plan.steps,)),
        ],
        compiler_params=params(12 * MB + 6 * message_bytes + 2 * weight_bytes),
        cost_estimate=pl.CostEstimate(
            flops=8 * plan.expert_rows * plan.columns * model,
            bytes_accessed=2 * weight_bytes,
            transcendentals=0,
        ),
        name="experts",
    )(got_normed, act, in_hbm(w_gate), in_hbm(w_up))
    combined = exchange(returned)

    grad_in = pl.pallas_call(
        functools.partial(finish_kernel, plan),
        out_shape=jax.ShapeDtypeStruct((stretch, model), BF),
        compiler_params=params(12 * MB + 3 * message_bytes),
        name="finish",
    )(target, gain, hidden, inv, grad_out[0], combined)
    return grad_in[None]


def solution(mesh):
    in_specs = (
        P("ep", "ctx", None),
        P("ep", "ctx", None),
        P("ep", "ctx", None),
        P("ep", "ctx"),
        P("ep", "ctx", None),
        P("ep", "ctx", None),
        P(),
        P(None, ("ctx", "ep")),
        P(None, ("ctx", "ep")),
        P(("ctx", "ep"), None),
        P("ep", "ctx", None),
    )
    out_specs = P("ep", "ctx", None)
    return jax.shard_map(shards, mesh=mesh, in_specs=in_specs, out_specs=out_specs, check_vma=False)
```

```python
import functools
import math

import jax
import jax.numpy as jnp
from jax import lax
from jax.experimental import pallas as pl
from jax.experimental.pallas import tpu as pltpu
from jax.sharding import PartitionSpec as P

HEADS = 16
HEAD = 128
EXPERTS = 64
FF = 1408
CAP = 2
REACH = 2
CHUNK = 256
TAG_ROWS = 16
PARTS = 4
AHEAD = 3
BF = jnp.bfloat16
F32 = jnp.float32
MB = 1024 * 1024


def iota(shape, dim):
    return lax.broadcasted_iota(jnp.int32, shape, dim)


def dot(left, right):
    return jnp.dot(left, right, preferred_element_type=F32)


def dot_nt(left, right):
    return lax.dot_general(left, right, (((1,), (1,)), ((), ())), preferred_element_type=F32)


class Plan:
    def __init__(self, devices, columns, width, stretch):
        self.devices = devices
        self.columns = columns
        self.model = width
        self.stretch = stretch
        self.local = max(1, columns // FF)
        self.sharers = max(1, FF // columns)
        self.slots = self.local * CAP
        self.fold = max(1, 8 // self.slots)
        self.width = width // self.fold
        self.rows = self.slots * self.fold
        self.total = devices * self.rows
        self.chunks = self.total // CHUNK
        self.group = CHUNK // self.rows
        self.expert_rows = devices * CAP
        self.block = CHUNK if columns % CHUNK == 0 else columns
        self.steps = columns // self.block


def message_slot(plan, chunk, shape, dim):
    row = iota(shape, dim)
    device = chunk * plan.group + row // plan.rows
    within = row % plan.rows
    first = device * plan.local if plan.sharers == 1 else device // plan.sharers
    return first * CAP + within % plan.slots, within // plan.slots


def write_messages(plan, target, value, out_ref):
    for chunk in range(plan.chunks):
        wanted, piece = message_slot(plan, chunk, (CHUNK, plan.stretch), 0)
        hit = wanted == target
        total = None
        for part in range(plan.fold):
            pick = jnp.where(hit & (piece == part), 1.0, 0.0).astype(BF)
            term = dot(pick, value[:, part * plan.width:(part + 1) * plan.width])
            total = term if total is None else total + term
        out_ref[chunk * CHUNK:(chunk + 1) * CHUNK, :] = total.astype(BF)


def expert_pick(plan, expert, part, shape, row_dim, message_dim):
    row = iota(shape, row_dim)
    message = iota(shape, message_dim)
    wanted = (row // CAP) * plan.rows + part * plan.slots + expert * CAP + row % CAP
    return jnp.where(wanted == message, 1.0, 0.0).astype(BF)


def read_expert_rows(plan, message_ref, rows_ref):
    count = plan.group * CAP
    for expert in range(plan.local):
        for part in range(plan.fold):
            pick = expert_pick(plan, expert, part, (count, CHUNK), 0, 1)
            for chunk in range(plan.chunks):
                base = expert * plan.expert_rows + chunk * count
                got = dot(pick, message_ref[chunk * CHUNK:(chunk + 1) * CHUNK, :])
                rows_ref[base:base + count, part * plan.width:(part + 1) * plan.width] = got.astype(BF)


def write_expert_rows(plan, columns, message_ref):
    count = plan.local * plan.expert_rows
    for chunk in range(plan.chunks):
        message = iota((CHUNK, count), 0) + chunk * CHUNK
        row = iota((CHUNK, count), 1)
        sender = (row % plan.expert_rows) // CAP
        slot = (row // plan.expert_rows) * CAP + row % CAP
        total = None
        for part in range(plan.fold):
            wanted = sender * plan.rows + part * plan.slots + slot
            pick = jnp.where(wanted == message, 1.0, 0.0).astype(BF)
            term = dot_nt(pick, columns[part * plan.width:(part + 1) * plan.width, :])
            total = term if total is None else total + term
        message_ref[chunk * CHUNK:(chunk + 1) * CHUNK, :] = total.astype(BF)


def to_column(row):
    size = row.shape[1]
    return jnp.transpose(jnp.broadcast_to(row, (size, size)))


def grads_kernel(plan, routes_ref, weight_ref, grad_ref, message_ref, target_ref):
    size = plan.stretch
    routes = routes_ref[...].astype(F32)
    column = to_column(routes)
    earlier = iota((size, size), 0) < iota((size, size), 1)
    same = (column == routes) & earlier
    rank = jnp.sum(jnp.where(same, 1.0, 0.0), axis=0, keepdims=True).astype(jnp.int32)
    target = jnp.where(rank < CAP, routes_ref[...] * CAP + rank, -1)
    target_ref[...] = target
    weight = to_column(weight_ref[...])[:, 0:1]
    grads = (weight * grad_ref[...].astype(F32)).astype(BF)
    write_messages(plan, target, grads, message_ref)


def fetches(pairs, sems):
    width = pairs[0][0].shape[1] // PARTS
    return [
        [
            pltpu.make_async_copy(
                source.at[:, pl.ds(part * width, width)],
                held.at[:, pl.ds(part * width, width)],
                sems.at[index, part],
            )
            for index, (source, held) in enumerate(pairs)
        ]
        for part in range(PARTS)
    ]


def softmax_kernel(
    plan, tags_ref, q_hbm, k0_hbm, k1_odd_ref, k1_even_ref, k2_ref, v1_ref, v2_odd_ref,
    v2_even_ref, probs_ref, q_ref, k0_ref, sems,
):
    size = plan.stretch
    copies = fetches(((q_hbm, q_ref), (k0_hbm, k0_ref)), sems)
    for group in copies:
        for copy in group:
            copy.start()
    odd = lax.axis_index("ctx") % 2 == 1

    def tag_row(ref):
        return ref[size:size + TAG_ROWS, 0:size].astype(F32)[0:1]

    own = tags_ref[...].astype(F32)
    column = to_column(own)
    masks = [
        (column == own) & (iota((size, size), 1) <= iota((size, size), 0)),
        column == tag_row(v1_ref),
        column == jnp.where(odd, tag_row(v2_odd_ref), tag_row(v2_even_ref)),
    ]
    for head in range(HEADS):
        if head % (HEADS // PARTS) == 0:
            for copy in copies[head // (HEADS // PARTS)]:
                copy.wait()
        span = slice(head * HEAD, (head + 1) * HEAD)
        rows = slice(head * size, (head + 1) * size)
        query = q_ref[:, span]
        near = jnp.where(odd, k1_odd_ref[:, span], k1_even_ref[:, span])
        scores = [
            jnp.where(mask, dot_nt(query, block) * (1.0 / math.sqrt(HEAD)), -1e30)
            for mask, block in zip(masks, (k0_ref[:, span], near, k2_ref[:, span]))
        ]
        top = jnp.max(
            jnp.maximum(jnp.maximum(scores[0], scores[1]), scores[2]), axis=-1, keepdims=True
        )
        weights = [jnp.exp(score - top) for score in scores]
        norm = jnp.sum(weights[0] + weights[1] + weights[2], axis=-1, keepdims=True)
        for index, weight in enumerate(weights):
            probs_ref[rows, index * size:(index + 1) * size] = (weight / norm).astype(BF)


def hidden_kernel(
    plan, target_ref, gain_ref, probs_ref, v0_hbm, v1_ref, v2_odd_ref, v2_even_ref,
    hidden_ref, inv_ref, message_ref, v0_ref, sems,
):
    size = plan.stretch
    copies = fetches(((v0_hbm, v0_ref),), sems)
    for group in copies:
        for copy in group:
            copy.start()
    odd = lax.axis_index("ctx") % 2 == 1
    squares = jnp.zeros((size, 1), F32)
    for head in range(HEADS):
        if head % (HEADS // PARTS) == 0:
            for copy in copies[head // (HEADS // PARTS)]:
                copy.wait()
        span = slice(head * HEAD, (head + 1) * HEAD)
        rows = slice(head * size, (head + 1) * size)
        far = jnp.where(odd, v2_odd_ref[0:size, span], v2_even_ref[0:size, span])
        total = None
        for index, block in enumerate((v0_ref[:, span], v1_ref[0:size, span], far)):
            term = dot(probs_ref[rows, index * size:(index + 1) * size], block)
            total = term if total is None else total + term
        hidden = total.astype(BF)
        hidden_ref[:, span] = hidden
        hidden = hidden.astype(F32)
        squares = squares + jnp.sum(hidden * hidden, axis=-1, keepdims=True)
    inv = lax.rsqrt(squares * (1.0 / plan.model) + 1e-06)
    inv_ref[...] = jnp.broadcast_to(inv, inv_ref.shape)
    normed = (hidden_ref[...].astype(F32) * inv * gain_ref[...]).astype(BF)
    write_messages(plan, target_ref[...], normed, message_ref)


def for_blocks(plan, inside, across):
    for expert in range(plan.local):
        low = -(-expert * FF // plan.block) if plan.local > 1 else 0
        high = (expert + 1) * FF // plan.block if plan.local > 1 else plan.steps
        for block in range(low, high):
            inside(expert, block * plan.block)
        if expert + 1 < plan.local and (expert + 1) * FF % plan.block:
            mask = iota((1, plan.block), 1) < (expert + 1) * FF % plan.block
            across(expert, high * plan.block, mask)


def act_kernel(plan, message_ref, down_hbm, act_ref, down_ref, rows_ref, down_sem):
    def piece(start):
        span = pl.ds(start, plan.block)
        return pltpu.make_async_copy(
            down_hbm.at[span], down_ref.at[span], down_sem.at[start // plan.block]
        )

    for step in range(plan.steps):
        piece(step * plan.block).start()
    read_expert_rows(plan, message_ref, rows_ref)

    def product(start):
        piece(start).wait()
        span = slice(start, start + plan.block)
        return jnp.transpose(dot_nt(down_ref[span, :], rows_ref[...]))

    def rows_of(value, expert):
        return value[expert * plan.expert_rows:(expert + 1) * plan.expert_rows, :]

    def inside(expert, start):
        act_ref[:, start:start + plan.block] = rows_of(product(start), expert)

    def across(expert, start, mask):
        value = product(start)
        act_ref[:, start:start + plan.block] = jnp.where(
            mask, rows_of(value, expert), rows_of(value, expert + 1)
        )

    for_blocks(plan, inside, across)


def expert_kernel(
    plan, message_ref, act_ref, gate_hbm, up_hbm, out_ref,
    gate_ref, up_ref, rows_ref, grad_gate_ref, grad_up_ref, sum_ref, gate_sem, up_sem,
):
    def pieces_at(start):
        span = pl.ds(start, plan.block)
        index = start // plan.block
        return (
            pltpu.make_async_copy(gate_hbm.at[:, span], gate_ref.at[:, span], gate_sem.at[index]),
            pltpu.make_async_copy(up_hbm.at[:, span], up_ref.at[:, span], up_sem.at[index]),
        )

    def begin(start):
        if start < plan.columns:
            for piece in pieces_at(start):
                piece.start()

    for step in range(AHEAD):
        begin(step * plan.block)
    read_expert_rows(plan, message_ref, rows_ref)

    def arrive(start):
        for piece in pieces_at(start):
            piece.wait()
        begin(start + AHEAD * plan.block)

    def rows_of(expert):
        return rows_ref[expert * plan.expert_rows:(expert + 1) * plan.expert_rows, :]

    def store(expert, span, mask, gate_pre, up_pre):
        act = act_ref[:, span]
        sig = jax.nn.sigmoid(gate_pre)
        grad_gate = act * up_pre * (sig * (1.0 + gate_pre * (1.0 - sig)))
        grad_up = act * (gate_pre * sig)
        for value, ref in ((grad_gate, grad_gate_ref), (grad_up, grad_up_ref)):
            pieces = [jnp.zeros_like(value)] * plan.local
            pieces[expert] = value if mask is None else jnp.where(mask, value, 0.0)
            if mask is not None:
                pieces[expert + 1] = jnp.where(mask, 0.0, value)
            ref[:, span] = jnp.concatenate(pieces, axis=0).astype(BF)

    def inside(expert, start):
        arrive(start)
        span = slice(start, start + plan.block)
        rows = rows_of(expert)
        store(expert, span, None, dot(rows, gate_ref[:, span]), dot(rows, up_ref[:, span]))

    def across(expert, start, mask):
        arrive(start)
        span = slice(start, start + plan.block)
        gate, up = gate_ref[:, span], up_ref[:, span]
        first, second = rows_of(expert), rows_of(expert + 1)
        store(
            expert, span, mask,
            jnp.where(mask, dot(first, gate), dot(second, gate)),
            jnp.where(mask, dot(first, up), dot(second, up)),
        )

    for_blocks(plan, inside, across)

    @pl.loop(0, plan.model // CHUNK)
    def _(tile):
        span = pl.ds(pl.multiple_of(tile * CHUNK, CHUNK), CHUNK)
        total = dot_nt(gate_ref[span, :], grad_gate_ref[...])
        total = total + dot_nt(up_ref[span, :], grad_up_ref[...])
        sum_ref[span, :] = total.astype(BF)

    write_expert_rows(plan, sum_ref, out_ref)


def finish_kernel(
    plan, target_ref, gain_ref, hidden_ref, inv_ref, grad_ref, message_ref, out_ref
):
    target = to_column(target_ref[...].astype(F32))[:, 0:1].astype(jnp.int32)
    parts = [None] * plan.fold
    for chunk in range(plan.chunks):
        wanted, piece = message_slot(plan, chunk, (plan.stretch, CHUNK), 1)
        messages = message_ref[chunk * CHUNK:(chunk + 1) * CHUNK, :]
        for part in range(plan.fold):
            pick = jnp.where((wanted == target) & (piece == part), 1.0, 0.0).astype(BF)
            term = dot(pick, messages)
            parts[part] = term if parts[part] is None else parts[part] + term
    inv = inv_ref[:, 0:1]
    spans = [slice(part * plan.width, (part + 1) * plan.width) for part in range(plan.fold)]
    gained = [
        part.astype(BF).astype(F32) * gain_ref[:, span] for part, span in zip(parts, spans)
    ]
    hidden = [hidden_ref[:, span].astype(F32) for span in spans]
    moment = sum(jnp.sum(h * g, axis=-1, keepdims=True) for h, g in zip(hidden, gained))
    mean = moment * (1.0 / plan.model)
    cube = inv * inv * inv
    for h, g, span in zip(hidden, gained, spans):
        out = grad_ref[:, span].astype(F32) + inv * g - h * cube * mean
        out_ref[:, span] = out.astype(BF)


def params(limit):
    return pltpu.CompilerParams(vmem_limit_bytes=limit)


def in_hbm(value):
    return pltpu.with_memory_space_constraint(value, pltpu.HBM)


def shards(
    queries, keys, values, doc_ids, routes, route_weight, norm_gain, w_gate, w_up, w_down, grad_out
):
    stretch, model = queries.shape[1:]
    ctx_count = lax.axis_size("ctx")
    axes = ("ctx", "ep")
    plan = Plan(ctx_count * lax.axis_size("ep"), w_gate.shape[1], model, stretch)
    messages = jax.ShapeDtypeStruct((plan.total, plan.width), BF)
    message_bytes = 2 * plan.total * plan.width
    gain = norm_gain.reshape(1, model)

    def exchange(value):
        cut = value.reshape(plan.devices, plan.rows, plan.width)
        cut = lax.all_to_all(cut, axes, split_axis=0, concat_axis=0, tiled=True)
        return cut.reshape(plan.total, plan.width)

    one_up = [(source, source + 1) for source in range(ctx_count - 1)]
    two_up = [(source, source + 2) for source in range(ctx_count - 2)]
    even_two_up = [(source, source + 2) for source in range(0, ctx_count - 2, 2)]
    even_up = [(source, source + 1) for source in range(0, ctx_count - 1, 2)]
    odd_down = [(source, source - 1) for source in range(1, ctx_count, 2)]

    def send(value, route):
        return lax.ppermute(value, "ctx", route)

    own_keys = keys[0]
    own_tags = doc_ids + 1
    tag_row = jnp.pad(own_tags.astype(BF), ((0, TAG_ROWS - 1), (0, model - stretch)))
    own_values = jnp.concatenate([values[0], tag_row])
    far_keys, odd_near_keys = send(own_keys, two_up), send(own_keys, even_up)
    near_values, even_far_values = send(own_values, one_up), send(own_values, even_two_up)

    grad_messages, target = pl.pallas_call(
        functools.partial(grads_kernel, plan),
        out_shape=(messages, jax.ShapeDtypeStruct((1, stretch), jnp.int32)),
        compiler_params=params(8 * MB + 3 * message_bytes),
        name="route_grads",
    )(routes.reshape(1, stretch), route_weight.reshape(1, stretch), grad_out[0])
    far_keys, odd_near_keys, near_values, even_far_values, grad_messages = (
        lax.optimization_barrier(
            (far_keys, odd_near_keys, near_values, even_far_values, grad_messages)
        )
    )
    even_near_keys = send(far_keys, odd_down)
    odd_far_values = send(near_values, even_up)
    got_grads = exchange(grad_messages)

    inside = pl.BlockSpec(memory_space=pltpu.VMEM)
    outside = pl.BlockSpec(memory_space=pltpu.HBM)
    block = (stretch, model)
    probs = pl.pallas_call(
        functools.partial(softmax_kernel, plan),
        in_specs=[inside, outside, outside] + [inside] * 6,
        out_shape=jax.ShapeDtypeStruct((HEADS * stretch, (REACH + 1) * stretch), BF),
        scratch_shapes=[pltpu.VMEM(block, BF)] * 2 + [pltpu.SemaphoreType.DMA((2, PARTS))],
        compiler_params=params(16 * MB),
        name="softmax",
    )(
        own_tags, in_hbm(queries[0]), in_hbm(own_keys), odd_near_keys, even_near_keys, far_keys,
        near_values, odd_far_values, even_far_values,
    )
    hidden, inv, normed_messages = pl.pallas_call(
        functools.partial(hidden_kernel, plan),
        in_specs=[inside] * 3 + [outside] + [inside] * 3,
        out_shape=(
            jax.ShapeDtypeStruct(block, BF),
            jax.ShapeDtypeStruct((stretch, 128), F32),
            messages,
        ),
        scratch_shapes=[pltpu.VMEM(block, BF), pltpu.SemaphoreType.DMA((1, PARTS))],
        compiler_params=params(12 * MB + 3 * message_bytes),
        name="hidden",
    )(target, gain, probs, in_hbm(values[0]), near_values, odd_far_values, even_far_values)
    got_normed = exchange(normed_messages)

    rows = plan.local * plan.expert_rows
    weight_bytes = 2 * plan.columns * model
    act = pl.pallas_call(
        functools.partial(act_kernel, plan),
        in_specs=[inside, outside],
        out_shape=jax.ShapeDtypeStruct((plan.expert_rows, plan.columns), F32),
        scratch_shapes=[
            pltpu.VMEM(w_down.shape, BF),
            pltpu.VMEM((rows, model), BF),
            pltpu.SemaphoreType.DMA((plan.steps,)),
        ],
        compiler_params=params(8 * MB + 6 * message_bytes + weight_bytes),
        cost_estimate=pl.CostEstimate(
            flops=2 * plan.expert_rows * plan.columns * model,
            bytes_accessed=weight_bytes,
            transcendentals=0,
        ),
        name="grad_act",
    )(got_grads, in_hbm(w_down))

    returned = pl.pallas_call(
        functools.partial(expert_kernel, plan),
        in_specs=[inside, inside, outside, outside],
        out_shape=messages,
        scratch_shapes=[
            pltpu.VMEM(w_gate.shape, BF),
            pltpu.VMEM(w_up.shape, BF),
            pltpu.VMEM((rows, model), BF),
            pltpu.VMEM((rows, plan.columns), BF),
            pltpu.VMEM((rows, plan.columns), BF),
            pltpu.VMEM((model, rows), BF),
            pltpu.SemaphoreType.DMA((plan.steps,)),
            pltpu.SemaphoreType.DMA((plan.steps,)),
        ],
        compiler_params=params(12 * MB + 6 * message_bytes + 2 * weight_bytes),
        cost_estimate=pl.CostEstimate(
            flops=8 * plan.expert_rows * plan.columns * model,
            bytes_accessed=2 * weight_bytes,
            transcendentals=0,
        ),
        name="experts",
    )(got_normed, act, in_hbm(w_gate), in_hbm(w_up))
    combined = exchange(returned)

    grad_in = pl.pallas_call(
        functools.partial(finish_kernel, plan),
        out_shape=jax.ShapeDtypeStruct((stretch, model), BF),
        compiler_params=params(12 * MB + 3 * message_bytes),
        name="finish",
    )(target, gain, hidden, inv, grad_out[0], combined)
    return grad_in[None]


def solution(mesh):
    in_specs = (
        P("ep", "ctx", None),
        P("ep", "ctx", None),
        P("ep", "ctx", None),
        P("ep", "ctx"),
        P("ep", "ctx", None),
        P("ep", "ctx", None),
        P(),
        P(None, ("ctx", "ep")),
        P(None, ("ctx", "ep")),
        P(("ctx", "ep"), None),
        P("ep", "ctx", None),
    )
    out_specs = P("ep", "ctx", None)
    return jax.shard_map(shards, mesh=mesh, in_specs=in_specs, out_specs=out_specs, check_vma=False)
```

```python
import functools
import math

import jax
import jax.numpy as jnp
from jax import lax
from jax.experimental import pallas as pl
from jax.experimental.pallas import tpu as pltpu
from jax.sharding import PartitionSpec as P

HEADS = 16
HEAD = 128
EXPERTS = 64
FF = 1408
CAP = 2
REACH = 2
CHUNK = 256
TAG_ROWS = 16
AHEAD = 3
BF = jnp.bfloat16
F32 = jnp.float32
MB = 1024 * 1024


def iota(shape, dim):
    return lax.broadcasted_iota(jnp.int32, shape, dim)


def dot(left, right):
    return jnp.dot(left, right, preferred_element_type=F32)


def dot_nt(left, right):
    return lax.dot_general(left, right, (((1,), (1,)), ((), ())), preferred_element_type=F32)


class Plan:
    def __init__(self, devices, eps, columns, width, stretch):
        self.devices = devices
        self.eps = eps
        self.columns = columns
        self.model = width
        self.stretch = stretch
        self.local = max(1, columns // FF)
        self.sharers = max(1, FF // columns)
        self.slots = self.local * CAP
        self.fold = max(2, 8 // self.slots)
        self.width = width // self.fold
        self.rows = self.slots * self.fold
        self.total = devices * self.rows
        self.chunks = self.total // CHUNK
        self.group = CHUNK // self.rows
        self.expert_rows = devices * CAP
        self.half = width // 2
        self.half_parts = self.fold // 2
        self.block = CHUNK if columns % CHUNK == 0 else columns
        self.steps = columns // self.block


def message_slot(plan, chunk, shape, dim):
    row = iota(shape, dim)
    device = chunk * plan.group + row // plan.rows
    within = row % plan.rows
    first = device * plan.local if plan.sharers == 1 else device // plan.sharers
    return first * CAP + within % plan.slots, within // plan.slots


def write_messages(plan, targets, values, out_ref):
    for chunk in range(plan.chunks):
        wanted, piece = message_slot(plan, chunk, (CHUNK, plan.stretch), 0)
        total = None
        for part in range(plan.fold):
            hit = (wanted == targets[part]) & (piece == part)
            term = dot(jnp.where(hit, 1.0, 0.0).astype(BF), values[part])
            total = term if total is None else total + term
        out_ref[chunk * CHUNK:(chunk + 1) * CHUNK, :] = total.astype(BF)


def split_columns(plan, value):
    count = value.shape[1] // plan.width
    return [value[:, part * plan.width:(part + 1) * plan.width] for part in range(count)]


def expert_pick(plan, expert, part, shape, row_dim, message_dim):
    row = iota(shape, row_dim)
    message = iota(shape, message_dim)
    wanted = (row // CAP) * plan.rows + part * plan.slots + expert * CAP + row % CAP
    return jnp.where(wanted == message, 1.0, 0.0).astype(BF)


def read_expert_rows(plan, message_ref, rows_ref):
    count = plan.group * CAP
    for expert in range(plan.local):
        for part in range(plan.fold):
            pick = expert_pick(plan, expert, part, (count, CHUNK), 0, 1)
            for chunk in range(plan.chunks):
                base = expert * plan.expert_rows + chunk * count
                got = dot(pick, message_ref[chunk * CHUNK:(chunk + 1) * CHUNK, :])
                rows_ref[base:base + count, part * plan.width:(part + 1) * plan.width] = got.astype(BF)


def read_hidden_rows(plan, message_ref, gain_ref, held_ref, rows_ref):
    count = plan.group * CAP
    shape = (count, CHUNK)
    row, message = iota(shape, 0), iota(shape, 1)
    owner = row // CAP
    parity = (owner // plan.eps) % 2
    for half in range(2):
        source = owner + (half - parity) * plan.eps
        for part in range(plan.half_parts):
            start = half * plan.half + part * plan.width
            first = source * plan.rows + (parity * plan.half_parts + part) * plan.slots
            for expert in range(plan.local):
                wanted = first + expert * CAP + row % CAP
                pick = jnp.where(wanted == message, 1.0, 0.0).astype(BF)
                for chunk in range(plan.chunks):
                    base = expert * plan.expert_rows + chunk * count
                    held_ref[base:base + count, start:start + plan.width] = dot(
                        pick, message_ref[chunk * CHUNK:(chunk + 1) * CHUNK, :]
                    )
    held = held_ref[...]
    mean = jnp.sum(held * held, axis=-1, keepdims=True) * (1.0 / plan.model)
    rows_ref[...] = (held * lax.rsqrt(mean + 1e-06) * gain_ref[...]).astype(BF)


def write_expert_rows(plan, columns, message_ref):
    count = plan.local * plan.expert_rows
    for chunk in range(plan.chunks):
        message = iota((CHUNK, count), 0) + chunk * CHUNK
        row = iota((CHUNK, count), 1)
        sender = (row % plan.expert_rows) // CAP
        slot = (row // plan.expert_rows) * CAP + row % CAP
        total = None
        for part in range(plan.fold):
            wanted = sender * plan.rows + part * plan.slots + slot
            pick = jnp.where(wanted == message, 1.0, 0.0).astype(BF)
            term = dot_nt(pick, columns[part * plan.width:(part + 1) * plan.width, :])
            total = term if total is None else total + term
        message_ref[chunk * CHUNK:(chunk + 1) * CHUNK, :] = total.astype(BF)


def to_column(row):
    size = row.shape[1]
    return jnp.transpose(jnp.broadcast_to(row, (size, size)))


def pack_kernel(
    plan, tags_ref, routes_ref, q_hbm, k_hbm, v_hbm,
    mine_ref, other_ref, q_mine_ref, q_other_ref, target_ref, sems,
):
    size = plan.stretch
    odd = lax.axis_index("ctx") % 2
    mine = pl.ds(pl.multiple_of(odd * plan.half, HEAD), plan.half)
    other = pl.ds(pl.multiple_of((1 - odd) * plan.half, HEAD), plan.half)
    first, second = pl.ds(0, size), pl.ds(size, size)
    pieces = (
        (k_hbm.at[:, other], other_ref.at[first]),
        (v_hbm.at[:, other], other_ref.at[second]),
        (k_hbm.at[:, mine], mine_ref.at[first]),
        (v_hbm.at[:, mine], mine_ref.at[second]),
        (q_hbm.at[:, other], q_other_ref),
        (q_hbm.at[:, mine], q_mine_ref),
    )
    copies = [
        pltpu.make_async_copy(source, held, sems.at[index])
        for index, (source, held) in enumerate(pieces)
    ]
    for copy in copies:
        copy.start()
    routes = routes_ref[...].astype(F32)
    earlier = iota((size, size), 0) < iota((size, size), 1)
    same = (to_column(routes) == routes) & earlier
    rank = jnp.sum(jnp.where(same, 1.0, 0.0), axis=0, keepdims=True)
    target = jnp.where(rank < CAP, routes * CAP + rank, -1.0)
    target_ref[...] = target.astype(jnp.int32)
    tags = tags_ref[...].astype(F32) + 1.0
    row = iota((TAG_ROWS, size), 0)
    block = jnp.where(row == 0, tags, jnp.where(row == 1, target, 0.0)).astype(BF)
    for ref in (mine_ref, other_ref):
        ref[2 * size:, :] = jnp.zeros((TAG_ROWS, plan.half), BF)
        ref[2 * size:, 0:size] = block
    for copy in copies:
        copy.wait()


def grads_kernel(plan, target_ref, weight_ref, grad_ref, message_ref):
    weight = to_column(weight_ref[...])[:, 0:1]
    grads = (weight * grad_ref[...].astype(F32)).astype(BF)
    write_messages(
        plan, [target_ref[...]] * plan.fold, split_columns(plan, grads), message_ref
    )


class Pair:
    def __init__(self, plan, mine_ref, pair_ref, far_ref, cross_ref):
        self.size = plan.stretch
        self.odd = lax.axis_index("ctx") % 2 == 1
        self.refs = (
            (cross_ref, far_ref), (far_ref, cross_ref), (pair_ref, mine_ref), (mine_ref, pair_ref)
        )

    def choose(self, if_odd, if_even):
        return jnp.where(self.odd, if_odd, if_even)

    def part(self, block, rows, span):
        if_odd, if_even = self.refs[block]
        return self.choose(if_odd[rows, span], if_even[rows, span])

    def keys(self, block, span):
        return self.part(block, slice(0, self.size), span)

    def values(self, block, span):
        return self.part(block, slice(self.size, 2 * self.size), span)

    def integers(self, block, row):
        rows = slice(2 * self.size, 2 * self.size + TAG_ROWS)
        return self.part(block, rows, slice(0, self.size)).astype(F32)[row:row + 1]


def softmax_kernel(
    plan, q_mine_ref, q_pair_ref, mine_ref, pair_ref, far_ref, cross_ref, probs_ref
):
    size = plan.stretch
    pair = Pair(plan, mine_ref, pair_ref, far_ref, cross_ref)
    tags = [pair.integers(block, 0) for block in range(4)]
    causal = iota((size, size), 1) <= iota((size, size), 0)
    masks = []
    for query in range(2):
        column = to_column(tags[2 + query])
        masks.append([column == tags[query + block] for block in range(3)])
        masks[query][2] = masks[query][2] & causal
    heads = plan.half // HEAD
    for head in range(heads):
        span = slice(head * HEAD, (head + 1) * HEAD)
        q_mine, q_pair = q_mine_ref[:, span], q_pair_ref[:, span]
        queries = (pair.choose(q_pair, q_mine), pair.choose(q_mine, q_pair))
        blocks = [pair.keys(block, span) for block in range(4)]
        for query in range(2):
            scores = [
                jnp.where(
                    masks[query][block],
                    dot_nt(queries[query], blocks[query + block]) * (1.0 / math.sqrt(HEAD)),
                    -1e30,
                )
                for block in range(3)
            ]
            top = jnp.max(
                jnp.maximum(jnp.maximum(scores[0], scores[1]), scores[2]), axis=-1, keepdims=True
            )
            weights = [jnp.exp(score - top) for score in scores]
            norm = jnp.sum(weights[0] + weights[1] + weights[2], axis=-1, keepdims=True)
            first = (query * heads + head) * size
            for index, weight in enumerate(weights):
                probs_ref[first:first + size, index * size:(index + 1) * size] = (
                    weight / norm
                ).astype(BF)


def hidden_kernel(
    plan, probs_ref, mine_ref, pair_ref, far_ref, cross_ref,
    kept_ref, sent_ref, message_ref, hidden_ref,
):
    size = plan.stretch
    pair = Pair(plan, mine_ref, pair_ref, far_ref, cross_ref)
    heads = plan.half // HEAD
    for head in range(heads):
        span = slice(head * HEAD, (head + 1) * HEAD)
        blocks = [pair.values(block, span) for block in range(4)]
        for query in range(2):
            first = (query * heads + head) * size
            total = None
            for index in range(3):
                probs = probs_ref[first:first + size, index * size:(index + 1) * size]
                term = dot(probs, blocks[query + index])
                total = term if total is None else total + term
            hidden_ref[query * size:(query + 1) * size, span] = total.astype(BF)
    even_rows, odd_rows = hidden_ref[0:size, :], hidden_ref[size:2 * size, :]
    kept_ref[...] = pair.choose(odd_rows, even_rows)
    sent_ref[...] = pair.choose(even_rows, odd_rows)
    targets = [pair.integers(2 + query, 1).astype(jnp.int32) for query in range(2)]
    write_messages(
        plan,
        [targets[part // plan.half_parts] for part in range(plan.fold)],
        split_columns(plan, even_rows) + split_columns(plan, odd_rows),
        message_ref,
    )


def for_blocks(plan, inside, across):
    for expert in range(plan.local):
        low = -(-expert * FF // plan.block) if plan.local > 1 else 0
        high = (expert + 1) * FF // plan.block if plan.local > 1 else plan.steps
        for block in range(low, high):
            inside(expert, block * plan.block)
        if expert + 1 < plan.local and (expert + 1) * FF % plan.block:
            mask = iota((1, plan.block), 1) < (expert + 1) * FF % plan.block
            across(expert, high * plan.block, mask)


def act_kernel(plan, message_ref, down_hbm, act_ref, down_ref, rows_ref, down_sem):
    def piece(start):
        span = pl.ds(start, plan.block)
        return pltpu.make_async_copy(
            down_hbm.at[span], down_ref.at[span], down_sem.at[start // plan.block]
        )

    for step in range(plan.steps):
        piece(step * plan.block).start()
    read_expert_rows(plan, message_ref, rows_ref)

    def product(start):
        piece(start).wait()
        span = slice(start, start + plan.block)
        return jnp.transpose(dot_nt(down_ref[span, :], rows_ref[...]))

    def rows_of(value, expert):
        return value[expert * plan.expert_rows:(expert + 1) * plan.expert_rows, :]

    def inside(expert, start):
        act_ref[:, start:start + plan.block] = rows_of(product(start), expert)

    def across(expert, start, mask):
        value = product(start)
        act_ref[:, start:start + plan.block] = jnp.where(
            mask, rows_of(value, expert), rows_of(value, expert + 1)
        )

    for_blocks(plan, inside, across)


def expert_kernel(
    plan, message_ref, gain_ref, act_ref, gate_hbm, up_hbm, out_ref,
    gate_ref, up_ref, held_ref, rows_ref, grad_gate_ref, grad_up_ref, sum_ref, gate_sem, up_sem,
):
    def pieces_at(start):
        span = pl.ds(start, plan.block)
        index = start // plan.block
        return (
            pltpu.make_async_copy(gate_hbm.at[:, span], gate_ref.at[:, span], gate_sem.at[index]),
            pltpu.make_async_copy(up_hbm.at[:, span], up_ref.at[:, span], up_sem.at[index]),
        )

    def begin(start):
        if start < plan.columns:
            for piece in pieces_at(start):
                piece.start()

    for step in range(AHEAD):
        begin(step * plan.block)
    read_hidden_rows(plan, message_ref, gain_ref, held_ref, rows_ref)

    def arrive(start):
        for piece in pieces_at(start):
            piece.wait()
        begin(start + AHEAD * plan.block)

    def rows_of(expert):
        return rows_ref[expert * plan.expert_rows:(expert + 1) * plan.expert_rows, :]

    def store(expert, span, mask, gate_pre, up_pre):
        act = act_ref[:, span]
        sig = jax.nn.sigmoid(gate_pre)
        grad_gate = act * up_pre * (sig * (1.0 + gate_pre * (1.0 - sig)))
        grad_up = act * (gate_pre * sig)
        for value, ref in ((grad_gate, grad_gate_ref), (grad_up, grad_up_ref)):
            pieces = [jnp.zeros_like(value)] * plan.local
            pieces[expert] = value if mask is None else jnp.where(mask, value, 0.0)
            if mask is not None:
                pieces[expert + 1] = jnp.where(mask, 0.0, value)
            ref[:, span] = jnp.concatenate(pieces, axis=0).astype(BF)

    def inside(expert, start):
        arrive(start)
        span = slice(start, start + plan.block)
        rows = rows_of(expert)
        store(expert, span, None, dot(rows, gate_ref[:, span]), dot(rows, up_ref[:, span]))

    def across(expert, start, mask):
        arrive(start)
        span = slice(start, start + plan.block)
        gate, up = gate_ref[:, span], up_ref[:, span]
        first, second = rows_of(expert), rows_of(expert + 1)
        store(
            expert, span, mask,
            jnp.where(mask, dot(first, gate), dot(second, gate)),
            jnp.where(mask, dot(first, up), dot(second, up)),
        )

    for_blocks(plan, inside, across)

    @pl.loop(0, plan.model // CHUNK)
    def _(tile):
        span = pl.ds(pl.multiple_of(tile * CHUNK, CHUNK), CHUNK)
        total = dot_nt(gate_ref[span, :], grad_gate_ref[...])
        total = total + dot_nt(up_ref[span, :], grad_up_ref[...])
        sum_ref[span, :] = total.astype(BF)

    write_expert_rows(plan, sum_ref, out_ref)


def finish_kernel(
    plan, target_ref, gain_ref, kept_ref, back_ref, grad_ref, message_ref, out_ref
):
    target = to_column(target_ref[...].astype(F32))[:, 0:1].astype(jnp.int32)
    parts = [None] * plan.fold
    for chunk in range(plan.chunks):
        wanted, piece = message_slot(plan, chunk, (plan.stretch, CHUNK), 1)
        messages = message_ref[chunk * CHUNK:(chunk + 1) * CHUNK, :]
        for part in range(plan.fold):
            pick = jnp.where((wanted == target) & (piece == part), 1.0, 0.0).astype(BF)
            term = dot(pick, messages)
            parts[part] = term if parts[part] is None else parts[part] + term
    spans = [slice(part * plan.width, (part + 1) * plan.width) for part in range(plan.fold)]
    gained = [
        part.astype(BF).astype(F32) * gain_ref[:, span] for part, span in zip(parts, spans)
    ]
    odd = lax.axis_index("ctx") % 2 == 1
    kept, back = kept_ref[...], back_ref[...]
    halves = (jnp.where(odd, back, kept), jnp.where(odd, kept, back))
    hidden = [
        piece.astype(F32) for half in halves for piece in split_columns(plan, half)
    ]
    squares = sum(jnp.sum(h * h, axis=-1, keepdims=True) for h in hidden)
    inv = lax.rsqrt(squares * (1.0 / plan.model) + 1e-06)
    moment = sum(jnp.sum(h * g, axis=-1, keepdims=True) for h, g in zip(hidden, gained))
    mean = moment * (1.0 / plan.model)
    cube = inv * inv * inv
    for h, g, span in zip(hidden, gained, spans):
        out = grad_ref[:, span].astype(F32) + inv * g - h * cube * mean
        out_ref[:, span] = out.astype(BF)


def params(limit):
    return pltpu.CompilerParams(vmem_limit_bytes=limit)


def in_hbm(value):
    return pltpu.with_memory_space_constraint(value, pltpu.HBM)


def shards(
    queries, keys, values, doc_ids, routes, route_weight, norm_gain, w_gate, w_up, w_down, grad_out
):
    stretch, model = queries.shape[1:]
    ctx_count = lax.axis_size("ctx")
    axes = ("ctx", "ep")
    ep_count = lax.axis_size("ep")
    plan = Plan(ctx_count * ep_count, ep_count, w_gate.shape[1], model, stretch)
    messages = jax.ShapeDtypeStruct((plan.total, plan.width), BF)
    message_bytes = 2 * plan.total * plan.width
    gain = norm_gain.reshape(1, model)

    def exchange(value):
        cut = value.reshape(plan.devices, plan.rows, plan.width)
        cut = lax.all_to_all(cut, axes, split_axis=0, concat_axis=0, tiled=True)
        return cut.reshape(plan.total, plan.width)

    two_up = [(source, source + 2) for source in range(ctx_count - 2)]
    next_pair = [(source, (source ^ 1) + 2) for source in range(ctx_count - 2)]
    pairs = [(source, source ^ 1) for source in range(ctx_count)]

    def send(value, route):
        return lax.ppermute(value, "ctx", route)

    inside = pl.BlockSpec(memory_space=pltpu.VMEM)
    outside = pl.BlockSpec(memory_space=pltpu.HBM)
    block = jax.ShapeDtypeStruct((2 * stretch + TAG_ROWS, plan.half), BF)
    half = jax.ShapeDtypeStruct((stretch, plan.half), BF)
    mine, other, q_mine, q_other, target = pl.pallas_call(
        functools.partial(pack_kernel, plan),
        in_specs=[inside, inside, outside, outside, outside],
        out_shape=(block, block, half, half, jax.ShapeDtypeStruct((1, stretch), jnp.int32)),
        scratch_shapes=[pltpu.SemaphoreType.DMA((6,))],
        compiler_params=params(8 * MB),
        name="pack",
    )(
        doc_ids, routes.reshape(1, stretch), in_hbm(queries[0]), in_hbm(keys[0]),
        in_hbm(values[0]),
    )
    far, cross = send(mine, two_up), send(other, next_pair)
    pair, q_pair = send(other, pairs), send(q_other, pairs)

    grad_messages = pl.pallas_call(
        functools.partial(grads_kernel, plan),
        out_shape=messages,
        compiler_params=params(8 * MB + 3 * message_bytes),
        name="route_grads",
    )(target, route_weight.reshape(1, stretch), grad_out[0])
    far, cross, pair, q_pair, grad_messages = lax.optimization_barrier(
        (far, cross, pair, q_pair, grad_messages)
    )
    got_grads = exchange(grad_messages)

    probs = pl.pallas_call(
        functools.partial(softmax_kernel, plan),
        out_shape=jax.ShapeDtypeStruct((HEADS * stretch, (REACH + 1) * stretch), BF),
        compiler_params=params(16 * MB),
        name="softmax",
    )(q_mine, q_pair, mine, pair, far, cross)
    kept, sent, hidden_messages = pl.pallas_call(
        functools.partial(hidden_kernel, plan),
        out_shape=(half, half, messages),
        scratch_shapes=[pltpu.VMEM((2 * stretch, plan.half), BF)],
        compiler_params=params(12 * MB + 3 * message_bytes),
        name="hidden",
    )(probs, mine, pair, far, cross)
    got_hidden = exchange(hidden_messages)
    back = send(sent, pairs)

    rows = plan.local * plan.expert_rows
    weight_bytes = 2 * plan.columns * model
    act = pl.pallas_call(
        functools.partial(act_kernel, plan),
        in_specs=[inside, outside],
        out_shape=jax.ShapeDtypeStruct((plan.expert_rows, plan.columns), F32),
        scratch_shapes=[
            pltpu.VMEM(w_down.shape, BF),
            pltpu.VMEM((rows, model), BF),
            pltpu.SemaphoreType.DMA((plan.steps,)),
        ],
        compiler_params=params(8 * MB + 6 * message_bytes + weight_bytes),
        cost_estimate=pl.CostEstimate(
            flops=2 * plan.expert_rows * plan.columns * model,
            bytes_accessed=weight_bytes,
            transcendentals=0,
        ),
        name="grad_act",
    )(got_grads, in_hbm(w_down))

    returned = pl.pallas_call(
        functools.partial(expert_kernel, plan),
        in_specs=[inside, inside, inside, outside, outside],
        out_shape=messages,
        scratch_shapes=[
            pltpu.VMEM(w_gate.shape, BF),
            pltpu.VMEM(w_up.shape, BF),
            pltpu.VMEM((rows, model), F32),
            pltpu.VMEM((rows, model), BF),
            pltpu.VMEM((rows, plan.columns), BF),
            pltpu.VMEM((rows, plan.columns), BF),
            pltpu.VMEM((model, rows), BF),
            pltpu.SemaphoreType.DMA((plan.steps,)),
            pltpu.SemaphoreType.DMA((plan.steps,)),
        ],
        compiler_params=params(12 * MB + 8 * message_bytes + 2 * weight_bytes),
        cost_estimate=pl.CostEstimate(
            flops=8 * plan.expert_rows * plan.columns * model,
            bytes_accessed=2 * weight_bytes,
            transcendentals=0,
        ),
        name="experts",
    )(got_hidden, gain, act, in_hbm(w_gate), in_hbm(w_up))
    combined = exchange(returned)

    grad_in = pl.pallas_call(
        functools.partial(finish_kernel, plan),
        out_shape=jax.ShapeDtypeStruct((stretch, model), BF),
        compiler_params=params(12 * MB + 3 * message_bytes),
        name="finish",
    )(target, gain, kept, back, grad_out[0], combined)
    return grad_in[None]


def solution(mesh):
    in_specs = (
        P("ep", "ctx", None),
        P("ep", "ctx", None),
        P("ep", "ctx", None),
        P("ep", "ctx"),
        P("ep", "ctx", None),
        P("ep", "ctx", None),
        P(),
        P(None, ("ctx", "ep")),
        P(None, ("ctx", "ep")),
        P(("ctx", "ep"), None),
        P("ep", "ctx", None),
    )
    out_specs = P("ep", "ctx", None)
    return jax.shard_map(shards, mesh=mesh, in_specs=in_specs, out_specs=out_specs, check_vma=False)
```

```python
import functools
import math

import jax
import jax.numpy as jnp
from jax import lax
from jax.experimental import pallas as pl
from jax.experimental.pallas import tpu as pltpu
from jax.sharding import PartitionSpec as P

HEADS = 16
HEAD = 128
EXPERTS = 64
FF = 1408
CAP = 2
REACH = 2
CHUNK = 256
TAG_ROWS = 16
BF = jnp.bfloat16
F32 = jnp.float32
MB = 1024 * 1024


def iota(shape, dim):
    return lax.broadcasted_iota(jnp.int32, shape, dim)


def dot(left, right):
    return jnp.dot(left, right, preferred_element_type=F32)


def dot_nt(left, right):
    return lax.dot_general(left, right, (((1,), (1,)), ((), ())), preferred_element_type=F32)


class Plan:
    def __init__(self, devices, eps, columns, width, stretch):
        self.devices = devices
        self.eps = eps
        self.columns = columns
        self.model = width
        self.stretch = stretch
        self.local = max(1, columns // FF)
        self.sharers = max(1, FF // columns)
        self.slots = self.local * CAP
        self.fold = max(2, 8 // self.slots)
        self.width = width // self.fold
        self.rows = self.slots * self.fold
        self.total = devices * self.rows
        self.chunks = self.total // CHUNK
        self.group = CHUNK // self.rows
        self.expert_rows = devices * CAP
        self.half = width // 2
        self.half_parts = self.fold // 2
        self.block = CHUNK if columns % CHUNK == 0 else columns
        self.steps = columns // self.block


def message_slot(plan, chunk, shape, dim):
    row = iota(shape, dim)
    device = chunk * plan.group + row // plan.rows
    within = row % plan.rows
    first = device * plan.local if plan.sharers == 1 else device // plan.sharers
    return first * CAP + within % plan.slots, within // plan.slots


def write_messages(plan, targets, values, out_ref):
    for chunk in range(plan.chunks):
        wanted, piece = message_slot(plan, chunk, (CHUNK, plan.stretch), 0)
        total = None
        for part in range(plan.fold):
            hit = (wanted == targets[part]) & (piece == part)
            term = dot(jnp.where(hit, 1.0, 0.0).astype(BF), values[part])
            total = term if total is None else total + term
        out_ref[chunk * CHUNK:(chunk + 1) * CHUNK, :] = total.astype(BF)


def split_columns(plan, value):
    count = value.shape[1] // plan.width
    return [value[:, part * plan.width:(part + 1) * plan.width] for part in range(count)]


def expert_pick(plan, expert, part, shape, row_dim, message_dim):
    row = iota(shape, row_dim)
    message = iota(shape, message_dim)
    wanted = (row // CAP) * plan.rows + part * plan.slots + expert * CAP + row % CAP
    return jnp.where(wanted == message, 1.0, 0.0).astype(BF)


def read_expert_rows(plan, message_ref, rows_ref):
    count = plan.group * CAP
    for expert in range(plan.local):
        for part in range(plan.fold):
            pick = expert_pick(plan, expert, part, (count, CHUNK), 0, 1)
            for chunk in range(plan.chunks):
                base = expert * plan.expert_rows + chunk * count
                got = dot(pick, message_ref[chunk * CHUNK:(chunk + 1) * CHUNK, :])
                rows_ref[base:base + count, part * plan.width:(part + 1) * plan.width] = got.astype(BF)


def read_hidden_rows(plan, message_ref, gain_ref, held_ref, rows_ref):
    count = plan.group * CAP
    shape = (count, CHUNK)
    row, message = iota(shape, 0), iota(shape, 1)
    owner = row // CAP
    parity = (owner // plan.eps) % 2
    for half in range(2):
        source = owner + (half - parity) * plan.eps
        for part in range(plan.half_parts):
            start = half * plan.half + part * plan.width
            first = source * plan.rows + (parity * plan.half_parts + part) * plan.slots
            for expert in range(plan.local):
                wanted = first + expert * CAP + row % CAP
                pick = jnp.where(wanted == message, 1.0, 0.0).astype(BF)
                for chunk in range(plan.chunks):
                    base = expert * plan.expert_rows + chunk * count
                    held_ref[base:base + count, start:start + plan.width] = dot(
                        pick, message_ref[chunk * CHUNK:(chunk + 1) * CHUNK, :]
                    )
    held = held_ref[...]
    mean = jnp.sum(held * held, axis=-1, keepdims=True) * (1.0 / plan.model)
    rows_ref[...] = (held * lax.rsqrt(mean + 1e-06) * gain_ref[...]).astype(BF)


def write_expert_rows(plan, columns_refs, message_ref):
    for chunk in range(plan.chunks):
        message = iota((CHUNK, plan.expert_rows), 0) + chunk * CHUNK
        row = iota((CHUNK, plan.expert_rows), 1)
        total = None
        for expert, columns_ref in enumerate(columns_refs):
            for part in range(plan.fold):
                wanted = (row // CAP) * plan.rows + part * plan.slots + expert * CAP + row % CAP
                pick = jnp.where(wanted == message, 1.0, 0.0).astype(BF)
                term = dot_nt(pick, columns_ref[part * plan.width:(part + 1) * plan.width, :])
                total = term if total is None else total + term
        message_ref[chunk * CHUNK:(chunk + 1) * CHUNK, :] = total.astype(BF)


def to_column(row):
    size = row.shape[1]
    return jnp.transpose(jnp.broadcast_to(row, (size, size)))


def pack_kernel(
    plan, tags_hbm, routes_hbm, weight_hbm, q_hbm, k_hbm, v_hbm, grad_hbm,
    message_ref, mine_ref, other_ref, q_mine_ref, q_other_ref, target_ref,
    tags_ref, routes_ref, weight_ref, grad_ref, sems,
):
    size = plan.stretch
    odd = lax.axis_index("ctx") % 2
    mine = pl.ds(pl.multiple_of(odd * plan.half, HEAD), plan.half)
    other = pl.ds(pl.multiple_of((1 - odd) * plan.half, HEAD), plan.half)
    first, second = pl.ds(0, size), pl.ds(size, size)
    pieces = (
        (tags_hbm, tags_ref),
        (routes_hbm, routes_ref),
        (weight_hbm, weight_ref),
        (grad_hbm, grad_ref),
        (k_hbm.at[:, other], other_ref.at[first]),
        (v_hbm.at[:, other], other_ref.at[second]),
        (k_hbm.at[:, mine], mine_ref.at[first]),
        (v_hbm.at[:, mine], mine_ref.at[second]),
        (q_hbm.at[:, other], q_other_ref),
        (q_hbm.at[:, mine], q_mine_ref),
    )
    copies = [
        pltpu.make_async_copy(source, held, sems.at[index])
        for index, (source, held) in enumerate(pieces)
    ]
    for copy in copies:
        copy.start()
    for copy in copies[:4]:
        copy.wait()
    routes = routes_ref[...].astype(F32)
    earlier = iota((size, size), 0) < iota((size, size), 1)
    same = (to_column(routes) == routes) & earlier
    rank = jnp.sum(jnp.where(same, 1.0, 0.0), axis=0, keepdims=True)
    target = jnp.where(rank < CAP, routes * CAP + rank, -1.0)
    whole_target = target.astype(jnp.int32)
    target_ref[...] = whole_target
    tags = tags_ref[...].astype(F32) + 1.0
    row = iota((TAG_ROWS, size), 0)
    block = jnp.where(row == 0, tags, jnp.where(row == 1, target, 0.0)).astype(BF)
    for ref in (mine_ref, other_ref):
        ref[2 * size:, :] = jnp.zeros((TAG_ROWS, plan.half), BF)
        ref[2 * size:, 0:size] = block
    weight = to_column(weight_ref[...])[:, 0:1]
    grads = (weight * grad_ref[...].astype(F32)).astype(BF)
    write_messages(plan, [whole_target] * plan.fold, split_columns(plan, grads), message_ref)
    for copy in copies[4:]:
        copy.wait()


class Pair:
    def __init__(self, plan, mine_ref, pair_ref, far_ref, cross_ref):
        self.size = plan.stretch
        self.odd = lax.axis_index("ctx") % 2 == 1
        self.refs = (
            (cross_ref, far_ref), (far_ref, cross_ref), (pair_ref, mine_ref), (mine_ref, pair_ref)
        )

    def choose(self, if_odd, if_even):
        return jnp.where(self.odd, if_odd, if_even)

    def part(self, block, rows, span):
        if_odd, if_even = self.refs[block]
        return self.choose(if_odd[rows, span], if_even[rows, span])

    def keys(self, block, span):
        return self.part(block, slice(0, self.size), span)

    def values(self, block, span):
        return self.part(block, slice(self.size, 2 * self.size), span)

    def integers(self, block, row):
        rows = slice(2 * self.size, 2 * self.size + TAG_ROWS)
        return self.part(block, rows, slice(0, self.size)).astype(F32)[row:row + 1]


def softmax_kernel(
    plan, q_mine_ref, q_pair_ref, mine_ref, pair_ref, far_ref, cross_ref, probs_ref
):
    size = plan.stretch
    pair = Pair(plan, mine_ref, pair_ref, far_ref, cross_ref)
    tags = [pair.integers(block, 0) for block in range(4)]
    causal = iota((size, size), 1) <= iota((size, size), 0)
    masks = []
    for query in range(2):
        column = to_column(tags[2 + query])
        masks.append([column == tags[query + block] for block in range(3)])
        masks[query][2] = masks[query][2] & causal
    heads = plan.half // HEAD
    for head in range(heads):
        span = slice(head * HEAD, (head + 1) * HEAD)
        q_mine, q_pair = q_mine_ref[:, span], q_pair_ref[:, span]
        queries = (pair.choose(q_pair, q_mine), pair.choose(q_mine, q_pair))
        blocks = [pair.keys(block, span) for block in range(4)]
        for query in range(2):
            scores = [
                jnp.where(
                    masks[query][block],
                    dot_nt(queries[query], blocks[query + block]) * (1.0 / math.sqrt(HEAD)),
                    -1e30,
                )
                for block in range(3)
            ]
            top = jnp.max(
                jnp.maximum(jnp.maximum(scores[0], scores[1]), scores[2]), axis=-1, keepdims=True
            )
            weights = [jnp.exp(score - top) for score in scores]
            norm = jnp.sum(weights[0] + weights[1] + weights[2], axis=-1, keepdims=True)
            first = (query * heads + head) * size
            for index, weight in enumerate(weights):
                probs_ref[first:first + size, index * size:(index + 1) * size] = (
                    weight / norm
                ).astype(BF)


def hidden_kernel(
    plan, probs_ref, mine_ref, pair_ref, far_ref, cross_ref,
    kept_ref, sent_ref, message_ref, hidden_ref,
):
    size = plan.stretch
    pair = Pair(plan, mine_ref, pair_ref, far_ref, cross_ref)
    heads = plan.half // HEAD
    for head in range(heads):
        span = slice(head * HEAD, (head + 1) * HEAD)
        blocks = [pair.values(block, span) for block in range(4)]
        for query in range(2):
            first = (query * heads + head) * size
            total = None
            for index in range(3):
                probs = probs_ref[first:first + size, index * size:(index + 1) * size]
                term = dot(probs, blocks[query + index])
                total = term if total is None else total + term
            hidden_ref[query * size:(query + 1) * size, span] = total.astype(BF)
    even_rows, odd_rows = hidden_ref[0:size, :], hidden_ref[size:2 * size, :]
    kept_ref[...] = pair.choose(odd_rows, even_rows)
    sent_ref[...] = pair.choose(even_rows, odd_rows)
    targets = [pair.integers(2 + query, 1).astype(jnp.int32) for query in range(2)]
    write_messages(
        plan,
        [targets[part // plan.half_parts] for part in range(plan.fold)],
        split_columns(plan, even_rows) + split_columns(plan, odd_rows),
        message_ref,
    )


def for_blocks(plan, inside, across, after=None):
    for expert in range(plan.local):
        low = -(-expert * FF // plan.block) if plan.local > 1 else 0
        high = (expert + 1) * FF // plan.block if plan.local > 1 else plan.steps
        for block in range(low, high):
            inside(expert, block * plan.block)
        if expert + 1 < plan.local and (expert + 1) * FF % plan.block:
            mask = iota((1, plan.block), 1) < (expert + 1) * FF % plan.block
            across(expert, high * plan.block, mask)
        if after is not None:
            after(expert)


def act_kernel(plan, message_ref, down_hbm, act_ref, down_ref, rows_ref, down_sem):
    def piece(start):
        span = pl.ds(start, plan.block)
        return pltpu.make_async_copy(
            down_hbm.at[span], down_ref.at[span], down_sem.at[start // plan.block]
        )

    for step in range(plan.steps):
        piece(step * plan.block).start()
    read_expert_rows(plan, message_ref, rows_ref)

    def product(start):
        piece(start).wait()
        span = slice(start, start + plan.block)
        return jnp.transpose(dot_nt(down_ref[span, :], rows_ref[...]))

    def rows_of(value, expert):
        return value[expert * plan.expert_rows:(expert + 1) * plan.expert_rows, :]

    def inside(expert, start):
        act_ref[:, start:start + plan.block] = rows_of(product(start), expert)

    def across(expert, start, mask):
        value = product(start)
        act_ref[:, start:start + plan.block] = jnp.where(
            mask, rows_of(value, expert), rows_of(value, expert + 1)
        )

    for_blocks(plan, inside, across)


def expert_kernel(
    plan, message_ref, gain_ref, act_ref, gate_hbm, up_hbm, out_ref,
    gate_ref, up_ref, held_ref, rows_ref, grad_gate_ref, grad_up_ref, gate_sem, up_sem,
    *sum_refs,
):
    def pieces_at(start):
        span = pl.ds(start, plan.block)
        index = start // plan.block
        return (
            pltpu.make_async_copy(gate_hbm.at[:, span], gate_ref.at[:, span], gate_sem.at[index]),
            pltpu.make_async_copy(up_hbm.at[:, span], up_ref.at[:, span], up_sem.at[index]),
        )

    for step in range(plan.steps):
        for piece in pieces_at(step * plan.block):
            piece.start()
    read_hidden_rows(plan, message_ref, gain_ref, held_ref, rows_ref)

    def arrive(start):
        for piece in pieces_at(start):
            piece.wait()

    def rows_of(expert):
        return rows_ref[expert * plan.expert_rows:(expert + 1) * plan.expert_rows, :]

    def store(span, gate_pre, up_pre):
        act = act_ref[:, span]
        sig = jax.nn.sigmoid(gate_pre)
        grad_gate_ref[:, span] = (act * up_pre * (sig * (1.0 + gate_pre * (1.0 - sig)))).astype(BF)
        grad_up_ref[:, span] = (act * (gate_pre * sig)).astype(BF)

    def inside(expert, start):
        arrive(start)
        span = slice(start, start + plan.block)
        rows = rows_of(expert)
        store(span, dot(rows, gate_ref[:, span]), dot(rows, up_ref[:, span]))

    def across(expert, start, mask):
        arrive(start)
        span = slice(start, start + plan.block)
        gate, up = gate_ref[:, span], up_ref[:, span]
        first, second = rows_of(expert), rows_of(expert + 1)
        store(
            span,
            jnp.where(mask, dot(first, gate), dot(second, gate)),
            jnp.where(mask, dot(first, up), dot(second, up)),
        )

    def after(expert):
        own = slice(expert * FF, (expert + 1) * FF) if plan.local > 1 else slice(0, plan.columns)

        @pl.loop(0, plan.model // CHUNK)
        def _(tile):
            span = pl.ds(pl.multiple_of(tile * CHUNK, CHUNK), CHUNK)
            total = dot_nt(gate_ref[span, own], grad_gate_ref[:, own])
            total = total + dot_nt(up_ref[span, own], grad_up_ref[:, own])
            sum_refs[expert][span, :] = total.astype(BF)

    for_blocks(plan, inside, across, after)
    write_expert_rows(plan, sum_refs, out_ref)


def finish_kernel(
    plan, target_ref, gain_ref, kept_ref, back_ref, grad_ref, message_ref, out_ref
):
    target = to_column(target_ref[...].astype(F32))[:, 0:1].astype(jnp.int32)
    parts = [None] * plan.fold
    for chunk in range(plan.chunks):
        wanted, piece = message_slot(plan, chunk, (plan.stretch, CHUNK), 1)
        messages = message_ref[chunk * CHUNK:(chunk + 1) * CHUNK, :]
        for part in range(plan.fold):
            pick = jnp.where((wanted == target) & (piece == part), 1.0, 0.0).astype(BF)
            term = dot(pick, messages)
            parts[part] = term if parts[part] is None else parts[part] + term
    spans = [slice(part * plan.width, (part + 1) * plan.width) for part in range(plan.fold)]
    gained = [
        part.astype(BF).astype(F32) * gain_ref[:, span] for part, span in zip(parts, spans)
    ]
    odd = lax.axis_index("ctx") % 2 == 1
    kept, back = kept_ref[...], back_ref[...]
    halves = (jnp.where(odd, back, kept), jnp.where(odd, kept, back))
    hidden = [
        piece.astype(F32) for half in halves for piece in split_columns(plan, half)
    ]
    squares = sum(jnp.sum(h * h, axis=-1, keepdims=True) for h in hidden)
    inv = lax.rsqrt(squares * (1.0 / plan.model) + 1e-06)
    moment = sum(jnp.sum(h * g, axis=-1, keepdims=True) for h, g in zip(hidden, gained))
    mean = moment * (1.0 / plan.model)
    cube = inv * inv * inv
    for h, g, span in zip(hidden, gained, spans):
        out = grad_ref[:, span].astype(F32) + inv * g - h * cube * mean
        out_ref[:, span] = out.astype(BF)


def params(limit):
    return pltpu.CompilerParams(vmem_limit_bytes=limit)


def in_hbm(value):
    return pltpu.with_memory_space_constraint(value, pltpu.HBM)


def shards(
    queries, keys, values, doc_ids, routes, route_weight, norm_gain, w_gate, w_up, w_down, grad_out
):
    stretch, model = queries.shape[1:]
    ctx_count = lax.axis_size("ctx")
    axes = ("ctx", "ep")
    ep_count = lax.axis_size("ep")
    plan = Plan(ctx_count * ep_count, ep_count, w_gate.shape[1], model, stretch)
    messages = jax.ShapeDtypeStruct((plan.total, plan.width), BF)
    message_bytes = 2 * plan.total * plan.width
    gain = norm_gain.reshape(1, model)

    def exchange(value):
        cut = value.reshape(plan.devices, plan.rows, plan.width)
        cut = lax.all_to_all(cut, axes, split_axis=0, concat_axis=0, tiled=True)
        return cut.reshape(plan.total, plan.width)

    two_up = [(source, source + 2) for source in range(ctx_count - 2)]
    next_pair = [(source, (source ^ 1) + 2) for source in range(ctx_count - 2)]
    pairs = [(source, source ^ 1) for source in range(ctx_count)]

    def send(value, route):
        return lax.ppermute(value, "ctx", route)

    inside = pl.BlockSpec(memory_space=pltpu.VMEM)
    outside = pl.BlockSpec(memory_space=pltpu.HBM)
    block = jax.ShapeDtypeStruct((2 * stretch + TAG_ROWS, plan.half), BF)
    half = jax.ShapeDtypeStruct((stretch, plan.half), BF)
    row = jax.ShapeDtypeStruct((1, stretch), jnp.int32)
    grad_messages, mine, other, q_mine, q_other, target = pl.pallas_call(
        functools.partial(pack_kernel, plan),
        in_specs=[outside] * 7,
        out_shape=(messages, block, block, half, half, row),
        scratch_shapes=[
            pltpu.VMEM((1, stretch), jnp.int32),
            pltpu.VMEM((1, stretch), jnp.int32),
            pltpu.VMEM((1, stretch), F32),
            pltpu.VMEM((stretch, model), BF),
            pltpu.SemaphoreType.DMA((10,)),
        ],
        compiler_params=params(12 * MB + 3 * message_bytes),
        name="pack",
    )(
        *map(
            in_hbm,
            (
                doc_ids, routes.reshape(1, stretch), route_weight.reshape(1, stretch),
                queries[0], keys[0], values[0], grad_out[0],
            ),
        )
    )
    got_grads = exchange(grad_messages)
    far, cross = send(mine, two_up), send(other, next_pair)
    pair, q_pair = send(other, pairs), send(q_other, pairs)
    far, cross, pair, q_pair = lax.optimization_barrier((far, cross, pair, q_pair))

    probs = pl.pallas_call(
        functools.partial(softmax_kernel, plan),
        out_shape=jax.ShapeDtypeStruct((HEADS * stretch, (REACH + 1) * stretch), BF),
        compiler_params=params(16 * MB),
        name="softmax",
    )(q_mine, q_pair, mine, pair, far, cross)
    kept, sent, hidden_messages = pl.pallas_call(
        functools.partial(hidden_kernel, plan),
        out_shape=(half, half, messages),
        scratch_shapes=[pltpu.VMEM((2 * stretch, plan.half), BF)],
        compiler_params=params(12 * MB + 3 * message_bytes),
        name="hidden",
    )(probs, mine, pair, far, cross)
    got_hidden = exchange(hidden_messages)
    back = send(sent, pairs)

    rows = plan.local * plan.expert_rows
    weight_bytes = 2 * plan.columns * model
    act = pl.pallas_call(
        functools.partial(act_kernel, plan),
        in_specs=[inside, outside],
        out_shape=jax.ShapeDtypeStruct((plan.expert_rows, plan.columns), F32),
        scratch_shapes=[
            pltpu.VMEM(w_down.shape, BF),
            pltpu.VMEM((rows, model), BF),
            pltpu.SemaphoreType.DMA((plan.steps,)),
        ],
        compiler_params=params(8 * MB + 6 * message_bytes + weight_bytes),
        cost_estimate=pl.CostEstimate(
            flops=2 * plan.expert_rows * plan.columns * model,
            bytes_accessed=weight_bytes,
            transcendentals=0,
        ),
        name="grad_act",
    )(got_grads, in_hbm(w_down))

    returned = pl.pallas_call(
        functools.partial(expert_kernel, plan),
        in_specs=[inside, inside, inside, outside, outside],
        out_shape=messages,
        scratch_shapes=[
            pltpu.VMEM(w_gate.shape, BF),
            pltpu.VMEM(w_up.shape, BF),
            pltpu.VMEM((rows, model), F32),
            pltpu.VMEM((rows, model), BF),
            pltpu.VMEM((plan.expert_rows, plan.columns), BF),
            pltpu.VMEM((plan.expert_rows, plan.columns), BF),
            pltpu.SemaphoreType.DMA((plan.steps,)),
            pltpu.SemaphoreType.DMA((plan.steps,)),
        ] + [pltpu.VMEM((model, plan.expert_rows), BF)] * plan.local,
        compiler_params=params(12 * MB + 8 * message_bytes + 2 * weight_bytes),
        cost_estimate=pl.CostEstimate(
            flops=8 * plan.expert_rows * plan.columns * model,
            bytes_accessed=2 * weight_bytes,
            transcendentals=0,
        ),
        name="experts",
    )(got_hidden, gain, act, in_hbm(w_gate), in_hbm(w_up))
    combined = exchange(returned)

    grad_in = pl.pallas_call(
        functools.partial(finish_kernel, plan),
        out_shape=jax.ShapeDtypeStruct((stretch, model), BF),
        compiler_params=params(12 * MB + 3 * message_bytes),
        name="finish",
    )(target, gain, kept, back, grad_out[0], combined)
    return grad_in[None]


def solution(mesh):
    in_specs = (
        P("ep", "ctx", None),
        P("ep", "ctx", None),
        P("ep", "ctx", None),
        P("ep", "ctx"),
        P("ep", "ctx", None),
        P("ep", "ctx", None),
        P(),
        P(None, ("ctx", "ep")),
        P(None, ("ctx", "ep")),
        P(("ctx", "ep"), None),
        P("ep", "ctx", None),
    )
    out_specs = P("ep", "ctx", None)
    return jax.shard_map(shards, mesh=mesh, in_specs=in_specs, out_specs=out_specs, check_vma=False)
```

```python
import functools
import math

import jax
import jax.numpy as jnp
from jax import lax
from jax.experimental import pallas as pl
from jax.experimental.pallas import tpu as pltpu
from jax.sharding import PartitionSpec as P

HEADS = 16
HEAD = 128
EXPERTS = 64
FF = 1408
CAP = 2
REACH = 2
CHUNK = 256
TAG_ROWS = 16
CUT = 512
BF = jnp.bfloat16
F32 = jnp.float32
MB = 1024 * 1024


def iota(shape, dim):
    return lax.broadcasted_iota(jnp.int32, shape, dim)


def dot(left, right):
    return jnp.dot(left, right, preferred_element_type=F32)


def dot_nt(left, right):
    return lax.dot_general(left, right, (((1,), (1,)), ((), ())), preferred_element_type=F32)


class Plan:
    def __init__(self, devices, eps, columns, width, stretch):
        self.devices = devices
        self.eps = eps
        self.columns = columns
        self.model = width
        self.stretch = stretch
        self.local = max(1, columns // FF)
        self.sharers = max(1, FF // columns)
        self.slots = self.local * CAP
        self.fold = max(2, 8 // self.slots)
        self.width = width // self.fold
        self.rows = self.slots * self.fold
        self.total = devices * self.rows
        self.chunks = self.total // CHUNK
        self.group = CHUNK // self.rows
        self.expert_rows = devices * CAP
        self.half = width // 2
        self.half_parts = self.fold // 2
        own = columns // self.local
        self.cuts = [
            (expert, expert * own + start, min(own - start, CUT))
            for expert in range(self.local)
            for start in range(0, own, CUT)
        ]


def message_slot(plan, chunk, shape, dim):
    row = iota(shape, dim)
    device = chunk * plan.group + row // plan.rows
    within = row % plan.rows
    first = device * plan.local if plan.sharers == 1 else device // plan.sharers
    return first * CAP + within % plan.slots, within // plan.slots


def write_messages(plan, targets, values, out_ref):
    for chunk in range(plan.chunks):
        wanted, piece = message_slot(plan, chunk, (CHUNK, plan.stretch), 0)
        total = None
        for part in range(plan.fold):
            hit = (wanted == targets[part]) & (piece == part)
            term = dot(jnp.where(hit, 1.0, 0.0).astype(BF), values[part])
            total = term if total is None else total + term
        out_ref[chunk * CHUNK:(chunk + 1) * CHUNK, :] = total.astype(BF)


def split_columns(plan, value):
    count = value.shape[1] // plan.width
    return [value[:, part * plan.width:(part + 1) * plan.width] for part in range(count)]


def expert_pick(plan, expert, part, shape, row_dim, message_dim):
    row = iota(shape, row_dim)
    message = iota(shape, message_dim)
    wanted = (row // CAP) * plan.rows + part * plan.slots + expert * CAP + row % CAP
    return jnp.where(wanted == message, 1.0, 0.0).astype(BF)


def read_expert_rows(plan, message_ref, rows_ref):
    count = plan.group * CAP
    for expert in range(plan.local):
        for part in range(plan.fold):
            pick = expert_pick(plan, expert, part, (count, CHUNK), 0, 1)
            for chunk in range(plan.chunks):
                base = expert * plan.expert_rows + chunk * count
                got = dot(pick, message_ref[chunk * CHUNK:(chunk + 1) * CHUNK, :])
                rows_ref[base:base + count, part * plan.width:(part + 1) * plan.width] = got.astype(BF)


def read_hidden_rows(plan, message_ref, gain_ref, held_ref, rows_ref):
    count = plan.group * CAP
    shape = (count, CHUNK)
    row, message = iota(shape, 0), iota(shape, 1)
    owner = row // CAP
    parity = (owner // plan.eps) % 2
    for half in range(2):
        source = owner + (half - parity) * plan.eps
        for part in range(plan.half_parts):
            start = half * plan.half + part * plan.width
            first = source * plan.rows + (parity * plan.half_parts + part) * plan.slots
            for expert in range(plan.local):
                wanted = first + expert * CAP + row % CAP
                pick = jnp.where(wanted == message, 1.0, 0.0).astype(BF)
                for chunk in range(plan.chunks):
                    base = expert * plan.expert_rows + chunk * count
                    held_ref[base:base + count, start:start + plan.width] = dot(
                        pick, message_ref[chunk * CHUNK:(chunk + 1) * CHUNK, :]
                    )
    held = held_ref[...]
    mean = jnp.sum(held * held, axis=-1, keepdims=True) * (1.0 / plan.model)
    rows_ref[...] = (held * lax.rsqrt(mean + 1e-06) * gain_ref[...]).astype(BF)


def write_expert_rows(plan, columns, message_ref):
    count = plan.local * plan.expert_rows
    for chunk in range(plan.chunks):
        message = iota((CHUNK, count), 0) + chunk * CHUNK
        row = iota((CHUNK, count), 1)
        sender = (row % plan.expert_rows) // CAP
        slot = (row // plan.expert_rows) * CAP + row % CAP
        total = None
        for part in range(plan.fold):
            wanted = sender * plan.rows + part * plan.slots + slot
            pick = jnp.where(wanted == message, 1.0, 0.0).astype(BF)
            term = dot_nt(pick, columns[part * plan.width:(part + 1) * plan.width, :])
            total = term if total is None else total + term
        message_ref[chunk * CHUNK:(chunk + 1) * CHUNK, :] = total.astype(BF)


def to_column(row):
    size = row.shape[1]
    return jnp.transpose(jnp.broadcast_to(row, (size, size)))


def pack_kernel(
    plan, tags_hbm, routes_hbm, weight_hbm, q_hbm, k_hbm, v_hbm, grad_hbm,
    message_ref, mine_ref, other_ref, q_mine_ref, q_other_ref, target_ref,
    tags_ref, routes_ref, weight_ref, grad_ref, sems,
):
    size = plan.stretch
    odd = lax.axis_index("ctx") % 2
    mine = pl.ds(pl.multiple_of(odd * plan.half, HEAD), plan.half)
    other = pl.ds(pl.multiple_of((1 - odd) * plan.half, HEAD), plan.half)
    first, second = pl.ds(0, size), pl.ds(size, size)
    pieces = (
        (tags_hbm, tags_ref),
        (routes_hbm, routes_ref),
        (weight_hbm, weight_ref),
        (grad_hbm, grad_ref),
        (k_hbm.at[:, other], other_ref.at[first]),
        (v_hbm.at[:, other], other_ref.at[second]),
        (k_hbm.at[:, mine], mine_ref.at[first]),
        (v_hbm.at[:, mine], mine_ref.at[second]),
        (q_hbm.at[:, other], q_other_ref),
        (q_hbm.at[:, mine], q_mine_ref),
    )
    copies = [
        pltpu.make_async_copy(source, held, sems.at[index])
        for index, (source, held) in enumerate(pieces)
    ]
    for copy in copies:
        copy.start()
    for copy in copies[:4]:
        copy.wait()
    routes = routes_ref[...].astype(F32)
    earlier = iota((size, size), 0) < iota((size, size), 1)
    same = (to_column(routes) == routes) & earlier
    rank = jnp.sum(jnp.where(same, 1.0, 0.0), axis=0, keepdims=True)
    target = jnp.where(rank < CAP, routes * CAP + rank, -1.0)
    whole_target = target.astype(jnp.int32)
    target_ref[...] = whole_target
    tags = tags_ref[...].astype(F32) + 1.0
    row = iota((TAG_ROWS, size), 0)
    block = jnp.where(row == 0, tags, jnp.where(row == 1, target, 0.0)).astype(BF)
    for ref in (mine_ref, other_ref):
        ref[2 * size:, :] = jnp.zeros((TAG_ROWS, plan.half), BF)
        ref[2 * size:, 0:size] = block
    weight = to_column(weight_ref[...])[:, 0:1]
    grads = (weight * grad_ref[...].astype(F32)).astype(BF)
    write_messages(plan, [whole_target] * plan.fold, split_columns(plan, grads), message_ref)
    for copy in copies[4:]:
        copy.wait()


class Pair:
    def __init__(self, plan, mine_ref, pair_ref, far_ref, cross_ref):
        self.size = plan.stretch
        self.odd = lax.axis_index("ctx") % 2 == 1
        self.refs = (
            (cross_ref, far_ref), (far_ref, cross_ref), (pair_ref, mine_ref), (mine_ref, pair_ref)
        )

    def choose(self, if_odd, if_even):
        return jnp.where(self.odd, if_odd, if_even)

    def part(self, block, rows, span):
        if_odd, if_even = self.refs[block]
        return self.choose(if_odd[rows, span], if_even[rows, span])

    def keys(self, block, span):
        return self.part(block, slice(0, self.size), span)

    def values(self, block, span):
        return self.part(block, slice(self.size, 2 * self.size), span)

    def integers(self, block, row):
        rows = slice(2 * self.size, 2 * self.size + TAG_ROWS)
        return self.part(block, rows, slice(0, self.size)).astype(F32)[row:row + 1]


def softmax_kernel(
    plan, q_mine_ref, q_pair_ref, mine_ref, pair_ref, far_ref, cross_ref, probs_ref
):
    size = plan.stretch
    pair = Pair(plan, mine_ref, pair_ref, far_ref, cross_ref)
    tags = [pair.integers(block, 0) for block in range(4)]
    causal = iota((size, size), 1) <= iota((size, size), 0)
    masks = []
    for query in range(2):
        column = to_column(tags[2 + query])
        masks.append([column == tags[query + block] for block in range(3)])
        masks[query][2] = masks[query][2] & causal
    heads = plan.half // HEAD
    for head in range(heads):
        span = slice(head * HEAD, (head + 1) * HEAD)
        q_mine, q_pair = q_mine_ref[:, span], q_pair_ref[:, span]
        queries = (pair.choose(q_pair, q_mine), pair.choose(q_mine, q_pair))
        blocks = [pair.keys(block, span) for block in range(4)]
        for query in range(2):
            scores = [
                jnp.where(
                    masks[query][block],
                    dot_nt(queries[query], blocks[query + block]) * (1.0 / math.sqrt(HEAD)),
                    -1e30,
                )
                for block in range(3)
            ]
            top = jnp.max(
                jnp.maximum(jnp.maximum(scores[0], scores[1]), scores[2]), axis=-1, keepdims=True
            )
            weights = [jnp.exp(score - top) for score in scores]
            norm = jnp.sum(weights[0] + weights[1] + weights[2], axis=-1, keepdims=True)
            first = (query * heads + head) * size
            for index, weight in enumerate(weights):
                probs_ref[first:first + size, index * size:(index + 1) * size] = (
                    weight / norm
                ).astype(BF)


def hidden_kernel(
    plan, probs_ref, mine_ref, pair_ref, far_ref, cross_ref,
    kept_ref, sent_ref, message_ref, hidden_ref,
):
    size = plan.stretch
    pair = Pair(plan, mine_ref, pair_ref, far_ref, cross_ref)
    heads = plan.half // HEAD
    for head in range(heads):
        span = slice(head * HEAD, (head + 1) * HEAD)
        blocks = [pair.values(block, span) for block in range(4)]
        for query in range(2):
            first = (query * heads + head) * size
            total = None
            for index in range(3):
                probs = probs_ref[first:first + size, index * size:(index + 1) * size]
                term = dot(probs, blocks[query + index])
                total = term if total is None else total + term
            hidden_ref[query * size:(query + 1) * size, span] = total.astype(BF)
    even_rows, odd_rows = hidden_ref[0:size, :], hidden_ref[size:2 * size, :]
    kept_ref[...] = pair.choose(odd_rows, even_rows)
    sent_ref[...] = pair.choose(even_rows, odd_rows)
    targets = [pair.integers(2 + query, 1).astype(jnp.int32) for query in range(2)]
    write_messages(
        plan,
        [targets[part // plan.half_parts] for part in range(plan.fold)],
        split_columns(plan, even_rows) + split_columns(plan, odd_rows),
        message_ref,
    )


def act_kernel(
    plan, message_ref, down_hbm, gate_hbm, up_hbm, act_ref, gate_ref, up_ref,
    down_ref, rows_ref, down_sem, gate_sem, up_sem,
):
    copies = [
        pltpu.make_async_copy(
            down_hbm.at[pl.ds(start, size)], down_ref.at[pl.ds(start, size)], down_sem.at[index]
        )
        for index, (_, start, size) in enumerate(plan.cuts)
    ]
    gate_copy = pltpu.make_async_copy(gate_hbm, gate_ref, gate_sem)
    up_copy = pltpu.make_async_copy(up_hbm, up_ref, up_sem)
    for copy in copies:
        copy.start()
    gate_copy.start()
    up_copy.start()
    read_expert_rows(plan, message_ref, rows_ref)
    for copy, (expert, start, size) in zip(copies, plan.cuts):
        copy.wait()
        rows = rows_ref[expert * plan.expert_rows:(expert + 1) * plan.expert_rows, :]
        act_ref[:, start:start + size] = dot_nt(rows, down_ref[start:start + size, :])
    gate_copy.wait()
    up_copy.wait()


def expert_kernel(
    plan, message_ref, gain_ref, act_ref, gate_ref, up_ref, out_ref,
    held_ref, rows_ref, grad_gate_ref, grad_up_ref, sum_ref,
):
    read_hidden_rows(plan, message_ref, gain_ref, held_ref, rows_ref)
    grad_gate_ref[...] = jnp.zeros_like(grad_gate_ref)
    grad_up_ref[...] = jnp.zeros_like(grad_up_ref)
    for expert, start, size in plan.cuts:
        span = slice(start, start + size)
        own = slice(expert * plan.expert_rows, (expert + 1) * plan.expert_rows)
        rows, act = rows_ref[own, :], act_ref[:, span]
        gate_pre, up_pre = dot(rows, gate_ref[:, span]), dot(rows, up_ref[:, span])
        sig = jax.nn.sigmoid(gate_pre)
        grad_gate = act * up_pre * (sig * (1.0 + gate_pre * (1.0 - sig)))
        grad_gate_ref[own, span] = grad_gate.astype(BF)
        grad_up_ref[own, span] = (act * (gate_pre * sig)).astype(BF)
    for start in range(0, plan.model, CHUNK):
        span = slice(start, start + CHUNK)
        total = dot_nt(gate_ref[span, :], grad_gate_ref[...])
        total = total + dot_nt(up_ref[span, :], grad_up_ref[...])
        sum_ref[span, :] = total.astype(BF)
    write_expert_rows(plan, sum_ref, out_ref)


def finish_kernel(
    plan, target_ref, gain_ref, kept_ref, back_ref, grad_ref, message_ref, out_ref
):
    target = to_column(target_ref[...].astype(F32))[:, 0:1].astype(jnp.int32)
    parts = [None] * plan.fold
    for chunk in range(plan.chunks):
        wanted, piece = message_slot(plan, chunk, (plan.stretch, CHUNK), 1)
        messages = message_ref[chunk * CHUNK:(chunk + 1) * CHUNK, :]
        for part in range(plan.fold):
            pick = jnp.where((wanted == target) & (piece == part), 1.0, 0.0).astype(BF)
            term = dot(pick, messages)
            parts[part] = term if parts[part] is None else parts[part] + term
    spans = [slice(part * plan.width, (part + 1) * plan.width) for part in range(plan.fold)]
    gained = [
        part.astype(BF).astype(F32) * gain_ref[:, span] for part, span in zip(parts, spans)
    ]
    odd = lax.axis_index("ctx") % 2 == 1
    kept, back = kept_ref[...], back_ref[...]
    halves = (jnp.where(odd, back, kept), jnp.where(odd, kept, back))
    hidden = [
        piece.astype(F32) for half in halves for piece in split_columns(plan, half)
    ]
    squares = sum(jnp.sum(h * h, axis=-1, keepdims=True) for h in hidden)
    inv = lax.rsqrt(squares * (1.0 / plan.model) + 1e-06)
    moment = sum(jnp.sum(h * g, axis=-1, keepdims=True) for h, g in zip(hidden, gained))
    mean = moment * (1.0 / plan.model)
    cube = inv * inv * inv
    for h, g, span in zip(hidden, gained, spans):
        out = grad_ref[:, span].astype(F32) + inv * g - h * cube * mean
        out_ref[:, span] = out.astype(BF)


def params(limit):
    return pltpu.CompilerParams(vmem_limit_bytes=limit)


def in_hbm(value):
    return pltpu.with_memory_space_constraint(value, pltpu.HBM)


def shards(
    queries, keys, values, doc_ids, routes, route_weight, norm_gain, w_gate, w_up, w_down, grad_out
):
    stretch, model = queries.shape[1:]
    ctx_count = lax.axis_size("ctx")
    axes = ("ctx", "ep")
    ep_count = lax.axis_size("ep")
    plan = Plan(ctx_count * ep_count, ep_count, w_gate.shape[1], model, stretch)
    messages = jax.ShapeDtypeStruct((plan.total, plan.width), BF)
    message_bytes = 2 * plan.total * plan.width
    gain = norm_gain.reshape(1, model)

    def exchange(value):
        cut = value.reshape(plan.devices, plan.rows, plan.width)
        cut = lax.all_to_all(cut, axes, split_axis=0, concat_axis=0, tiled=True)
        return cut.reshape(plan.total, plan.width)

    two_up = [(source, source + 2) for source in range(ctx_count - 2)]
    next_pair = [(source, (source ^ 1) + 2) for source in range(ctx_count - 2)]
    pairs = [(source, source ^ 1) for source in range(ctx_count)]

    def send(value, route):
        return lax.ppermute(value, "ctx", route)

    inside = pl.BlockSpec(memory_space=pltpu.VMEM)
    outside = pl.BlockSpec(memory_space=pltpu.HBM)
    block = jax.ShapeDtypeStruct((2 * stretch + TAG_ROWS, plan.half), BF)
    half = jax.ShapeDtypeStruct((stretch, plan.half), BF)
    row = jax.ShapeDtypeStruct((1, stretch), jnp.int32)
    grad_messages, mine, other, q_mine, q_other, target = pl.pallas_call(
        functools.partial(pack_kernel, plan),
        in_specs=[outside] * 7,
        out_shape=(messages, block, block, half, half, row),
        scratch_shapes=[
            pltpu.VMEM((1, stretch), jnp.int32),
            pltpu.VMEM((1, stretch), jnp.int32),
            pltpu.VMEM((1, stretch), F32),
            pltpu.VMEM((stretch, model), BF),
            pltpu.SemaphoreType.DMA((10,)),
        ],
        compiler_params=params(12 * MB + 3 * message_bytes),
        name="pack",
    )(
        *map(
            in_hbm,
            (
                doc_ids, routes.reshape(1, stretch), route_weight.reshape(1, stretch),
                queries[0], keys[0], values[0], grad_out[0],
            ),
        )
    )
    got_grads = exchange(grad_messages)
    far, cross = send(mine, two_up), send(other, next_pair)
    pair, q_pair = send(other, pairs), send(q_other, pairs)

    rows = plan.local * plan.expert_rows
    weight_bytes = 2 * plan.columns * model
    act, gate, up = pl.pallas_call(
        functools.partial(act_kernel, plan),
        in_specs=[inside, outside, outside, outside],
        out_specs=[inside, inside, inside],
        out_shape=(
            jax.ShapeDtypeStruct((plan.expert_rows, plan.columns), F32),
            pltpu.VMEM(w_gate.shape, BF),
            pltpu.VMEM(w_up.shape, BF),
        ),
        scratch_shapes=[
            pltpu.VMEM(w_down.shape, BF),
            pltpu.VMEM((rows, model), BF),
            pltpu.SemaphoreType.DMA((len(plan.cuts),)),
            pltpu.SemaphoreType.DMA,
            pltpu.SemaphoreType.DMA,
        ],
        compiler_params=params(8 * MB + 6 * message_bytes + weight_bytes),
        cost_estimate=pl.CostEstimate(
            flops=2 * plan.expert_rows * plan.columns * model,
            bytes_accessed=3 * weight_bytes,
            transcendentals=0,
        ),
        name="grad_act",
    )(got_grads, in_hbm(w_down), in_hbm(w_gate), in_hbm(w_up))
    far, cross, pair, q_pair, act = lax.optimization_barrier((far, cross, pair, q_pair, act))

    probs = pl.pallas_call(
        functools.partial(softmax_kernel, plan),
        out_shape=jax.ShapeDtypeStruct((HEADS * stretch, (REACH + 1) * stretch), BF),
        compiler_params=params(16 * MB),
        name="softmax",
    )(q_mine, q_pair, mine, pair, far, cross)
    kept, sent, hidden_messages = pl.pallas_call(
        functools.partial(hidden_kernel, plan),
        out_shape=(half, half, messages),
        scratch_shapes=[pltpu.VMEM((2 * stretch, plan.half), BF)],
        compiler_params=params(12 * MB + 3 * message_bytes),
        name="hidden",
    )(probs, mine, pair, far, cross)
    got_hidden = exchange(hidden_messages)
    got_hidden, sent = lax.optimization_barrier((got_hidden, sent))
    back = send(sent, pairs)

    returned = pl.pallas_call(
        functools.partial(expert_kernel, plan),
        out_shape=messages,
        scratch_shapes=[
            pltpu.VMEM((rows, model), F32),
            pltpu.VMEM((rows, model), BF),
            pltpu.VMEM((rows, plan.columns), BF),
            pltpu.VMEM((rows, plan.columns), BF),
            pltpu.VMEM((model, rows), BF),
        ],
        compiler_params=params(12 * MB + 8 * message_bytes),
        cost_estimate=pl.CostEstimate(
            flops=8 * plan.expert_rows * plan.columns * model,
            bytes_accessed=2 * weight_bytes,
            transcendentals=0,
        ),
        name="experts",
    )(got_hidden, gain, act, gate, up)
    returned, back = lax.optimization_barrier((returned, back))
    combined = exchange(returned)

    grad_in = pl.pallas_call(
        functools.partial(finish_kernel, plan),
        out_shape=jax.ShapeDtypeStruct((stretch, model), BF),
        compiler_params=params(12 * MB + 3 * message_bytes),
        name="finish",
    )(target, gain, kept, back, grad_out[0], combined)
    return grad_in[None]


def solution(mesh):
    in_specs = (
        P("ep", "ctx", None),
        P("ep", "ctx", None),
        P("ep", "ctx", None),
        P("ep", "ctx"),
        P("ep", "ctx", None),
        P("ep", "ctx", None),
        P(),
        P(None, ("ctx", "ep")),
        P(None, ("ctx", "ep")),
        P(("ctx", "ep"), None),
        P("ep", "ctx", None),
    )
    out_specs = P("ep", "ctx", None)
    return jax.shard_map(shards, mesh=mesh, in_specs=in_specs, out_specs=out_specs, check_vma=False)
```

```python
import functools
import math

import jax
import jax.numpy as jnp
from jax import lax
from jax.experimental import pallas as pl
from jax.experimental.pallas import tpu as pltpu
from jax.sharding import PartitionSpec as P

HEADS = 16
HEAD = 128
EXPERTS = 64
FF = 1408
CAP = 2
REACH = 2
CHUNK = 256
TAG_ROWS = 16
CUT = 512
PIECE = 256
BF = jnp.bfloat16
F32 = jnp.float32
MB = 1024 * 1024


def iota(shape, dim):
    return lax.broadcasted_iota(jnp.int32, shape, dim)


def dot(left, right):
    return jnp.dot(left, right, preferred_element_type=F32)


def dot_nt(left, right):
    return lax.dot_general(left, right, (((1,), (1,)), ((), ())), preferred_element_type=F32)


class Plan:
    def __init__(self, devices, eps, columns, width, stretch):
        self.devices = devices
        self.eps = eps
        self.columns = columns
        self.model = width
        self.stretch = stretch
        self.local = max(1, columns // FF)
        self.sharers = max(1, FF // columns)
        self.slots = self.local * CAP
        self.fold = max(2, 8 // self.slots)
        self.width = width // self.fold
        self.rows = self.slots * self.fold
        self.total = devices * self.rows
        self.chunks = self.total // CHUNK
        self.group = CHUNK // self.rows
        self.expert_rows = devices * CAP
        self.half = width // 2
        self.half_parts = self.fold // 2
        self.pieces = self.half // PIECE
        self.block_rows = 2 * self.pieces * stretch + TAG_ROWS
        own = columns // self.local
        self.cuts = [
            (expert, expert * own + start, min(own - start, CUT))
            for expert in range(self.local)
            for start in range(0, own, CUT)
        ]


def message_slot(plan, chunk, shape, dim):
    row = iota(shape, dim)
    device = chunk * plan.group + row // plan.rows
    within = row % plan.rows
    first = device * plan.local if plan.sharers == 1 else device // plan.sharers
    return first * CAP + within % plan.slots, within // plan.slots


def write_messages(plan, targets, values, out_ref):
    for chunk in range(plan.chunks):
        wanted, piece = message_slot(plan, chunk, (CHUNK, plan.stretch), 0)
        total = None
        for part in range(plan.fold):
            hit = (wanted == targets[part]) & (piece == part)
            term = dot(jnp.where(hit, 1.0, 0.0).astype(BF), values[part])
            total = term if total is None else total + term
        out_ref[chunk * CHUNK:(chunk + 1) * CHUNK, :] = total.astype(BF)


def split_columns(plan, value):
    count = value.shape[1] // plan.width
    return [value[:, part * plan.width:(part + 1) * plan.width] for part in range(count)]


def expert_pick(plan, expert, part, shape, row_dim, message_dim):
    row = iota(shape, row_dim)
    message = iota(shape, message_dim)
    wanted = (row // CAP) * plan.rows + part * plan.slots + expert * CAP + row % CAP
    return jnp.where(wanted == message, 1.0, 0.0).astype(BF)


def read_expert_rows(plan, message_ref, rows_ref):
    count = plan.group * CAP
    for expert in range(plan.local):
        for part in range(plan.fold):
            pick = expert_pick(plan, expert, part, (count, CHUNK), 0, 1)
            for chunk in range(plan.chunks):
                base = expert * plan.expert_rows + chunk * count
                got = dot(pick, message_ref[chunk * CHUNK:(chunk + 1) * CHUNK, :])
                rows_ref[base:base + count, part * plan.width:(part + 1) * plan.width] = got.astype(BF)


def read_hidden_rows(plan, message_ref, gain_ref, held_ref, rows_ref):
    count = plan.group * CAP
    shape = (count, CHUNK)
    row, message = iota(shape, 0), iota(shape, 1)
    owner = row // CAP
    parity = (owner // plan.eps) % 2
    for half in range(2):
        source = owner + (half - parity) * plan.eps
        for part in range(plan.half_parts):
            start = half * plan.half + part * plan.width
            first = source * plan.rows + (parity * plan.half_parts + part) * plan.slots
            for expert in range(plan.local):
                wanted = first + expert * CAP + row % CAP
                pick = jnp.where(wanted == message, 1.0, 0.0).astype(BF)
                for chunk in range(plan.chunks):
                    base = expert * plan.expert_rows + chunk * count
                    held_ref[base:base + count, start:start + plan.width] = dot(
                        pick, message_ref[chunk * CHUNK:(chunk + 1) * CHUNK, :]
                    )
    held = held_ref[...]
    mean = jnp.sum(held * held, axis=-1, keepdims=True) * (1.0 / plan.model)
    rows_ref[...] = (held * lax.rsqrt(mean + 1e-06) * gain_ref[...]).astype(BF)


def write_expert_rows(plan, columns, message_ref):
    count = plan.local * plan.expert_rows
    for chunk in range(plan.chunks):
        message = iota((CHUNK, count), 0) + chunk * CHUNK
        row = iota((CHUNK, count), 1)
        sender = (row % plan.expert_rows) // CAP
        slot = (row // plan.expert_rows) * CAP + row % CAP
        total = None
        for part in range(plan.fold):
            wanted = sender * plan.rows + part * plan.slots + slot
            pick = jnp.where(wanted == message, 1.0, 0.0).astype(BF)
            term = dot_nt(pick, columns[part * plan.width:(part + 1) * plan.width, :])
            total = term if total is None else total + term
        message_ref[chunk * CHUNK:(chunk + 1) * CHUNK, :] = total.astype(BF)


def to_column(row):
    size = row.shape[1]
    return jnp.transpose(jnp.broadcast_to(row, (size, size)))


def grads_kernel(
    plan, routes_hbm, weight_hbm, grad_hbm, message_ref, target_ref,
    routes_ref, weight_ref, grad_ref, sems,
):
    size = plan.stretch
    pieces = ((routes_hbm, routes_ref), (weight_hbm, weight_ref), (grad_hbm, grad_ref))
    copies = [
        pltpu.make_async_copy(source, held, sems.at[index])
        for index, (source, held) in enumerate(pieces)
    ]
    for copy in copies:
        copy.start()
    copies[0].wait()
    routes = routes_ref[...].astype(F32)
    earlier = iota((size, size), 0) < iota((size, size), 1)
    same = (to_column(routes) == routes) & earlier
    rank = jnp.sum(jnp.where(same, 1.0, 0.0), axis=0, keepdims=True)
    target = jnp.where(rank < CAP, routes * CAP + rank, -1.0).astype(jnp.int32)
    target_ref[...] = target
    copies[1].wait()
    weight = to_column(weight_ref[...])[:, 0:1]
    copies[2].wait()
    grads = (weight * grad_ref[...].astype(F32)).astype(BF)
    write_messages(plan, [target] * plan.fold, split_columns(plan, grads), message_ref)


def pack_kernel(
    plan, target_ref, tags_hbm, q_hbm, k_hbm, v_hbm,
    mine_ref, other_ref, q_mine_ref, q_other_ref, tags_ref, sems,
):
    size = plan.stretch
    odd = lax.axis_index("ctx") % 2
    pieces = [(tags_hbm, tags_ref)]
    for side, block_ref, q_ref in ((1 - odd, other_ref, q_other_ref), (odd, mine_ref, q_mine_ref)):
        base = side * plan.half
        for index, source in enumerate((k_hbm, v_hbm)):
            for piece in range(plan.pieces):
                start = pl.multiple_of(base + piece * PIECE, HEAD)
                row = (index * plan.pieces + piece) * size
                pieces.append((source.at[:, pl.ds(start, PIECE)], block_ref.at[pl.ds(row, size)]))
        span = pl.ds(pl.multiple_of(base, HEAD), plan.half)
        pieces.append((q_hbm.at[:, span], q_ref))
    copies = [
        pltpu.make_async_copy(source, held, sems.at[index])
        for index, (source, held) in enumerate(pieces)
    ]
    for copy in copies:
        copy.start()
    copies[0].wait()
    tags = tags_ref[...].astype(F32) + 1.0
    row = iota((TAG_ROWS, size), 0)
    target = target_ref[...].astype(F32)
    block = jnp.where(row == 0, tags, jnp.where(row == 1, target, 0.0)).astype(BF)
    first = plan.block_rows - TAG_ROWS
    for ref in (mine_ref, other_ref):
        ref[first:, :] = jnp.zeros((TAG_ROWS, PIECE), BF)
        ref[first:, 0:size] = block
    for copy in copies[1:]:
        copy.wait()


class Pair:
    def __init__(self, plan, mine_ref, pair_ref, far_ref, cross_ref):
        self.plan = plan
        self.odd = lax.axis_index("ctx") % 2 == 1
        self.refs = (
            (cross_ref, far_ref), (far_ref, cross_ref), (pair_ref, mine_ref), (mine_ref, pair_ref)
        )

    def choose(self, if_odd, if_even):
        return jnp.where(self.odd, if_odd, if_even)

    def part(self, block, rows, span):
        if_odd, if_even = self.refs[block]
        return self.choose(if_odd[rows, span], if_even[rows, span])

    def head(self, block, piece, lane):
        first = piece * self.plan.stretch
        rows = slice(first, first + self.plan.stretch)
        return self.part(block, rows, slice(lane, lane + HEAD))

    def keys(self, block, head):
        return self.head(block, head * HEAD // PIECE, head * HEAD % PIECE)

    def values(self, block, head):
        return self.head(block, self.plan.pieces + head * HEAD // PIECE, head * HEAD % PIECE)

    def integers(self, block, row):
        rows = slice(self.plan.block_rows - TAG_ROWS, self.plan.block_rows)
        return self.part(block, rows, slice(0, self.plan.stretch)).astype(F32)[row:row + 1]


def softmax_kernel(
    plan, q_mine_ref, q_pair_ref, mine_ref, pair_ref, far_ref, cross_ref, probs_ref
):
    size = plan.stretch
    pair = Pair(plan, mine_ref, pair_ref, far_ref, cross_ref)
    tags = [pair.integers(block, 0) for block in range(4)]
    causal = iota((size, size), 1) <= iota((size, size), 0)
    masks = []
    for query in range(2):
        column = to_column(tags[2 + query])
        masks.append([column == tags[query + block] for block in range(3)])
        masks[query][2] = masks[query][2] & causal
    heads = plan.half // HEAD
    for head in range(heads):
        span = slice(head * HEAD, (head + 1) * HEAD)
        q_mine, q_pair = q_mine_ref[:, span], q_pair_ref[:, span]
        queries = (pair.choose(q_pair, q_mine), pair.choose(q_mine, q_pair))
        blocks = [pair.keys(block, head) for block in range(4)]
        for query in range(2):
            scores = [
                jnp.where(
                    masks[query][block],
                    dot_nt(queries[query], blocks[query + block]) * (1.0 / math.sqrt(HEAD)),
                    -1e30,
                )
                for block in range(3)
            ]
            top = jnp.max(
                jnp.maximum(jnp.maximum(scores[0], scores[1]), scores[2]), axis=-1, keepdims=True
            )
            weights = [jnp.exp(score - top) for score in scores]
            norm = jnp.sum(weights[0] + weights[1] + weights[2], axis=-1, keepdims=True)
            first = (query * heads + head) * size
            for index, weight in enumerate(weights):
                probs_ref[first:first + size, index * size:(index + 1) * size] = (
                    weight / norm
                ).astype(BF)


def hidden_kernel(
    plan, probs_ref, mine_ref, pair_ref, far_ref, cross_ref,
    kept_ref, sent_ref, message_ref, hidden_ref,
):
    size = plan.stretch
    pair = Pair(plan, mine_ref, pair_ref, far_ref, cross_ref)
    heads = plan.half // HEAD
    for head in range(heads):
        span = slice(head * HEAD, (head + 1) * HEAD)
        blocks = [pair.values(block, head) for block in range(4)]
        for query in range(2):
            first = (query * heads + head) * size
            total = None
            for index in range(3):
                probs = probs_ref[first:first + size, index * size:(index + 1) * size]
                term = dot(probs, blocks[query + index])
                total = term if total is None else total + term
            hidden_ref[query * size:(query + 1) * size, span] = total.astype(BF)
    even_rows, odd_rows = hidden_ref[0:size, :], hidden_ref[size:2 * size, :]
    kept_ref[...] = pair.choose(odd_rows, even_rows)
    sent_ref[...] = pair.choose(even_rows, odd_rows)
    targets = [pair.integers(2 + query, 1).astype(jnp.int32) for query in range(2)]
    write_messages(
        plan,
        [targets[part // plan.half_parts] for part in range(plan.fold)],
        split_columns(plan, even_rows) + split_columns(plan, odd_rows),
        message_ref,
    )


def act_kernel(
    plan, message_ref, down_hbm, gate_hbm, up_hbm, act_ref, gate_ref, up_ref,
    down_ref, rows_ref, down_sem, gate_sem, up_sem,
):
    copies = [
        pltpu.make_async_copy(
            down_hbm.at[pl.ds(start, size)], down_ref.at[pl.ds(start, size)], down_sem.at[index]
        )
        for index, (_, start, size) in enumerate(plan.cuts)
    ]
    gate_copy = pltpu.make_async_copy(gate_hbm, gate_ref, gate_sem)
    up_copy = pltpu.make_async_copy(up_hbm, up_ref, up_sem)
    for copy in copies:
        copy.start()
    gate_copy.start()
    up_copy.start()
    read_expert_rows(plan, message_ref, rows_ref)
    for copy, (expert, start, size) in zip(copies, plan.cuts):
        copy.wait()
        rows = rows_ref[expert * plan.expert_rows:(expert + 1) * plan.expert_rows, :]
        act_ref[:, start:start + size] = dot_nt(rows, down_ref[start:start + size, :])
    gate_copy.wait()
    up_copy.wait()


def expert_kernel(
    plan, message_ref, gain_ref, act_ref, gate_ref, up_ref, out_ref,
    held_ref, rows_ref, grad_gate_ref, grad_up_ref, sum_ref,
):
    read_hidden_rows(plan, message_ref, gain_ref, held_ref, rows_ref)
    grad_gate_ref[...] = jnp.zeros_like(grad_gate_ref)
    grad_up_ref[...] = jnp.zeros_like(grad_up_ref)
    for expert, start, size in plan.cuts:
        span = slice(start, start + size)
        own = slice(expert * plan.expert_rows, (expert + 1) * plan.expert_rows)
        rows, act = rows_ref[own, :], act_ref[:, span]
        gate_pre, up_pre = dot(rows, gate_ref[:, span]), dot(rows, up_ref[:, span])
        sig = jax.nn.sigmoid(gate_pre)
        grad_gate = act * up_pre * (sig * (1.0 + gate_pre * (1.0 - sig)))
        grad_gate_ref[own, span] = grad_gate.astype(BF)
        grad_up_ref[own, span] = (act * (gate_pre * sig)).astype(BF)
    for start in range(0, plan.model, CHUNK):
        span = slice(start, start + CHUNK)
        total = dot_nt(gate_ref[span, :], grad_gate_ref[...])
        total = total + dot_nt(up_ref[span, :], grad_up_ref[...])
        sum_ref[span, :] = total.astype(BF)
    write_expert_rows(plan, sum_ref, out_ref)


def finish_kernel(
    plan, target_ref, gain_ref, kept_ref, back_ref, grad_ref, message_ref, out_ref
):
    target = to_column(target_ref[...].astype(F32))[:, 0:1].astype(jnp.int32)
    parts = [None] * plan.fold
    for chunk in range(plan.chunks):
        wanted, piece = message_slot(plan, chunk, (plan.stretch, CHUNK), 1)
        messages = message_ref[chunk * CHUNK:(chunk + 1) * CHUNK, :]
        for part in range(plan.fold):
            pick = jnp.where((wanted == target) & (piece == part), 1.0, 0.0).astype(BF)
            term = dot(pick, messages)
            parts[part] = term if parts[part] is None else parts[part] + term
    spans = [slice(part * plan.width, (part + 1) * plan.width) for part in range(plan.fold)]
    gained = [
        part.astype(BF).astype(F32) * gain_ref[:, span] for part, span in zip(parts, spans)
    ]
    odd = lax.axis_index("ctx") % 2 == 1
    kept, back = kept_ref[...], back_ref[...]
    halves = (jnp.where(odd, back, kept), jnp.where(odd, kept, back))
    hidden = [
        piece.astype(F32) for half in halves for piece in split_columns(plan, half)
    ]
    squares = sum(jnp.sum(h * h, axis=-1, keepdims=True) for h in hidden)
    inv = lax.rsqrt(squares * (1.0 / plan.model) + 1e-06)
    moment = sum(jnp.sum(h * g, axis=-1, keepdims=True) for h, g in zip(hidden, gained))
    mean = moment * (1.0 / plan.model)
    cube = inv * inv * inv
    for h, g, span in zip(hidden, gained, spans):
        out = grad_ref[:, span].astype(F32) + inv * g - h * cube * mean
        out_ref[:, span] = out.astype(BF)


def params(limit):
    return pltpu.CompilerParams(vmem_limit_bytes=limit)


def in_hbm(value):
    return pltpu.with_memory_space_constraint(value, pltpu.HBM)


def shards(
    queries, keys, values, doc_ids, routes, route_weight, norm_gain, w_gate, w_up, w_down, grad_out
):
    stretch, model = queries.shape[1:]
    ctx_count = lax.axis_size("ctx")
    axes = ("ctx", "ep")
    ep_count = lax.axis_size("ep")
    plan = Plan(ctx_count * ep_count, ep_count, w_gate.shape[1], model, stretch)
    messages = jax.ShapeDtypeStruct((plan.total, plan.width), BF)
    message_bytes = 2 * plan.total * plan.width
    gain = norm_gain.reshape(1, model)

    def exchange(value):
        cut = value.reshape(plan.devices, plan.rows, plan.width)
        cut = lax.all_to_all(cut, axes, split_axis=0, concat_axis=0, tiled=True)
        return cut.reshape(plan.total, plan.width)

    two_up = [(source, source + 2) for source in range(ctx_count - 2)]
    next_pair = [(source, (source ^ 1) + 2) for source in range(ctx_count - 2)]
    pairs = [(source, source ^ 1) for source in range(ctx_count)]

    def send(value, route):
        return lax.ppermute(value, "ctx", route)

    inside = pl.BlockSpec(memory_space=pltpu.VMEM)
    outside = pl.BlockSpec(memory_space=pltpu.HBM)
    block = jax.ShapeDtypeStruct((plan.block_rows, PIECE), BF)
    half = jax.ShapeDtypeStruct((stretch, plan.half), BF)
    grad_messages, target = pl.pallas_call(
        functools.partial(grads_kernel, plan),
        in_specs=[outside] * 3,
        out_shape=(messages, jax.ShapeDtypeStruct((1, stretch), jnp.int32)),
        scratch_shapes=[
            pltpu.VMEM((1, stretch), jnp.int32),
            pltpu.VMEM((1, stretch), F32),
            pltpu.VMEM((stretch, model), BF),
            pltpu.SemaphoreType.DMA((3,)),
        ],
        compiler_params=params(8 * MB + 3 * message_bytes),
        name="route_grads",
    )(
        in_hbm(routes.reshape(1, stretch)), in_hbm(route_weight.reshape(1, stretch)),
        in_hbm(grad_out[0]),
    )
    got_grads = exchange(grad_messages)
    mine, other, q_mine, q_other = pl.pallas_call(
        functools.partial(pack_kernel, plan),
        in_specs=[inside] + [outside] * 4,
        out_shape=(block, block, half, half),
        scratch_shapes=[
            pltpu.VMEM((1, stretch), jnp.int32),
            pltpu.SemaphoreType.DMA((4 * plan.pieces + 3,)),
        ],
        compiler_params=params(8 * MB),
        name="pack",
    )(target, *map(in_hbm, (doc_ids, queries[0], keys[0], values[0])))
    far, cross = send(mine, two_up), send(other, next_pair)
    pair, q_pair = send(other, pairs), send(q_other, pairs)

    rows = plan.local * plan.expert_rows
    weight_bytes = 2 * plan.columns * model
    act, gate, up = pl.pallas_call(
        functools.partial(act_kernel, plan),
        in_specs=[inside, outside, outside, outside],
        out_specs=[inside, inside, inside],
        out_shape=(
            jax.ShapeDtypeStruct((plan.expert_rows, plan.columns), F32),
            pltpu.VMEM(w_gate.shape, BF),
            pltpu.VMEM(w_up.shape, BF),
        ),
        scratch_shapes=[
            pltpu.VMEM(w_down.shape, BF),
            pltpu.VMEM((rows, model), BF),
            pltpu.SemaphoreType.DMA((len(plan.cuts),)),
            pltpu.SemaphoreType.DMA,
            pltpu.SemaphoreType.DMA,
        ],
        compiler_params=params(8 * MB + 6 * message_bytes + weight_bytes),
        cost_estimate=pl.CostEstimate(
            flops=2 * plan.expert_rows * plan.columns * model,
            bytes_accessed=3 * weight_bytes,
            transcendentals=0,
        ),
        name="grad_act",
    )(got_grads, in_hbm(w_down), in_hbm(w_gate), in_hbm(w_up))
    far, cross, pair, q_pair, act = lax.optimization_barrier((far, cross, pair, q_pair, act))

    probs = pl.pallas_call(
        functools.partial(softmax_kernel, plan),
        out_shape=jax.ShapeDtypeStruct((HEADS * stretch, (REACH + 1) * stretch), BF),
        compiler_params=params(16 * MB),
        name="softmax",
    )(q_mine, q_pair, mine, pair, far, cross)
    kept, sent, hidden_messages = pl.pallas_call(
        functools.partial(hidden_kernel, plan),
        out_shape=(half, half, messages),
        scratch_shapes=[pltpu.VMEM((2 * stretch, plan.half), BF)],
        compiler_params=params(12 * MB + 3 * message_bytes),
        name="hidden",
    )(probs, mine, pair, far, cross)
    got_hidden = exchange(hidden_messages)
    got_hidden, sent = lax.optimization_barrier((got_hidden, sent))
    back = send(sent, pairs)

    returned = pl.pallas_call(
        functools.partial(expert_kernel, plan),
        out_shape=messages,
        scratch_shapes=[
            pltpu.VMEM((rows, model), F32),
            pltpu.VMEM((rows, model), BF),
            pltpu.VMEM((rows, plan.columns), BF),
            pltpu.VMEM((rows, plan.columns), BF),
            pltpu.VMEM((model, rows), BF),
        ],
        compiler_params=params(12 * MB + 8 * message_bytes),
        cost_estimate=pl.CostEstimate(
            flops=8 * plan.expert_rows * plan.columns * model,
            bytes_accessed=2 * weight_bytes,
            transcendentals=0,
        ),
        name="experts",
    )(got_hidden, gain, act, gate, up)
    returned, back = lax.optimization_barrier((returned, back))
    combined = exchange(returned)

    grad_in = pl.pallas_call(
        functools.partial(finish_kernel, plan),
        out_shape=jax.ShapeDtypeStruct((stretch, model), BF),
        compiler_params=params(12 * MB + 3 * message_bytes),
        name="finish",
    )(target, gain, kept, back, grad_out[0], combined)
    return grad_in[None]


def solution(mesh):
    in_specs = (
        P("ep", "ctx", None),
        P("ep", "ctx", None),
        P("ep", "ctx", None),
        P("ep", "ctx"),
        P("ep", "ctx", None),
        P("ep", "ctx", None),
        P(),
        P(None, ("ctx", "ep")),
        P(None, ("ctx", "ep")),
        P(("ctx", "ep"), None),
        P("ep", "ctx", None),
    )
    out_specs = P("ep", "ctx", None)
    return jax.shard_map(shards, mesh=mesh, in_specs=in_specs, out_specs=out_specs, check_vma=False)
```

```python
import functools
import math

import jax
import jax.numpy as jnp
from jax import lax
from jax.experimental import pallas as pl
from jax.experimental.pallas import tpu as pltpu
from jax.sharding import PartitionSpec as P

HEADS = 16
HEAD = 128
EXPERTS = 64
FF = 1408
CAP = 2
REACH = 2
CHUNK = 256
TAG_ROWS = 16
CUT = 512
PIECE = 256
BF = jnp.bfloat16
F32 = jnp.float32
MB = 1024 * 1024


def iota(shape, dim):
    return lax.broadcasted_iota(jnp.int32, shape, dim)


def dot(left, right):
    return jnp.dot(left, right, preferred_element_type=F32)


def dot_nt(left, right):
    return lax.dot_general(left, right, (((1,), (1,)), ((), ())), preferred_element_type=F32)


class Plan:
    def __init__(self, devices, eps, columns, width, stretch):
        self.devices = devices
        self.eps = eps
        self.columns = columns
        self.model = width
        self.stretch = stretch
        self.local = max(1, columns // FF)
        self.sharers = max(1, FF // columns)
        self.slots = self.local * CAP
        self.fold = max(2, 8 // self.slots)
        self.width = width // self.fold
        self.rows = self.slots * self.fold
        self.total = devices * self.rows
        self.chunks = self.total // CHUNK
        self.group = CHUNK // self.rows
        self.expert_rows = devices * CAP
        self.half = width // 2
        self.half_parts = self.fold // 2
        self.pieces = self.half // PIECE
        self.block_rows = 2 * self.pieces * stretch + TAG_ROWS
        own = columns // self.local
        self.cuts = [
            (expert, expert * own + start, min(own - start, CUT))
            for expert in range(self.local)
            for start in range(0, own, CUT)
        ]


def message_slot(plan, chunk, shape, dim):
    row = iota(shape, dim)
    device = chunk * plan.group + row // plan.rows
    within = row % plan.rows
    first = device * plan.local if plan.sharers == 1 else device // plan.sharers
    return first * CAP + within % plan.slots, within // plan.slots


def write_messages(plan, targets, values, out_ref):
    for chunk in range(plan.chunks):
        wanted, piece = message_slot(plan, chunk, (CHUNK, plan.stretch), 0)
        total = None
        for part in range(plan.fold):
            hit = (wanted == targets[part]) & (piece == part)
            term = dot(jnp.where(hit, 1.0, 0.0).astype(BF), values[part])
            total = term if total is None else total + term
        out_ref[chunk * CHUNK:(chunk + 1) * CHUNK, :] = total.astype(BF)


def split_columns(plan, value):
    count = value.shape[1] // plan.width
    return [value[:, part * plan.width:(part + 1) * plan.width] for part in range(count)]


def expert_pick(plan, expert, part, shape, row_dim, message_dim):
    row = iota(shape, row_dim)
    message = iota(shape, message_dim)
    wanted = (row // CAP) * plan.rows + part * plan.slots + expert * CAP + row % CAP
    return jnp.where(wanted == message, 1.0, 0.0).astype(BF)


def read_expert_rows(plan, message_ref, rows_ref):
    count = plan.group * CAP
    for expert in range(plan.local):
        for part in range(plan.fold):
            pick = expert_pick(plan, expert, part, (count, CHUNK), 0, 1)
            for chunk in range(plan.chunks):
                base = expert * plan.expert_rows + chunk * count
                got = dot(pick, message_ref[chunk * CHUNK:(chunk + 1) * CHUNK, :])
                rows_ref[base:base + count, part * plan.width:(part + 1) * plan.width] = got.astype(BF)


def read_hidden_rows(plan, message_ref, gain_ref, held_ref, rows_ref):
    count = plan.group * CAP
    shape = (count, CHUNK)
    row, message = iota(shape, 0), iota(shape, 1)
    owner = row // CAP
    parity = (owner // plan.eps) % 2
    for half in range(2):
        source = owner + (half - parity) * plan.eps
        for part in range(plan.half_parts):
            start = half * plan.half + part * plan.width
            first = source * plan.rows + (parity * plan.half_parts + part) * plan.slots
            for expert in range(plan.local):
                wanted = first + expert * CAP + row % CAP
                pick = jnp.where(wanted == message, 1.0, 0.0).astype(BF)
                for chunk in range(plan.chunks):
                    base = expert * plan.expert_rows + chunk * count
                    held_ref[base:base + count, start:start + plan.width] = dot(
                        pick, message_ref[chunk * CHUNK:(chunk + 1) * CHUNK, :]
                    )
    held = held_ref[...]
    mean = jnp.sum(held * held, axis=-1, keepdims=True) * (1.0 / plan.model)
    rows_ref[...] = (held * lax.rsqrt(mean + 1e-06) * gain_ref[...]).astype(BF)


def write_expert_rows(plan, rows_ref, message_ref):
    count = plan.local * plan.expert_rows
    for chunk in range(plan.chunks):
        message = iota((CHUNK, count), 0) + chunk * CHUNK
        row = iota((CHUNK, count), 1)
        sender = (row % plan.expert_rows) // CAP
        slot = (row // plan.expert_rows) * CAP + row % CAP
        total = None
        for part in range(plan.fold):
            wanted = sender * plan.rows + part * plan.slots + slot
            pick = jnp.where(wanted == message, 1.0, 0.0).astype(BF)
            term = dot(pick, rows_ref[:, part * plan.width:(part + 1) * plan.width])
            total = term if total is None else total + term
        message_ref[chunk * CHUNK:(chunk + 1) * CHUNK, :] = total.astype(BF)


def to_column(row):
    size = row.shape[1]
    return jnp.transpose(jnp.broadcast_to(row, (size, size)))


def grads_kernel(
    plan, routes_hbm, weight_hbm, grad_hbm, message_ref, target_ref,
    routes_ref, weight_ref, grad_ref, sems,
):
    size = plan.stretch
    pieces = ((routes_hbm, routes_ref), (weight_hbm, weight_ref), (grad_hbm, grad_ref))
    copies = [
        pltpu.make_async_copy(source, held, sems.at[index])
        for index, (source, held) in enumerate(pieces)
    ]
    for copy in copies:
        copy.start()
    copies[0].wait()
    routes = routes_ref[...].astype(F32)
    earlier = iota((size, size), 0) < iota((size, size), 1)
    same = (to_column(routes) == routes) & earlier
    rank = jnp.sum(jnp.where(same, 1.0, 0.0), axis=0, keepdims=True)
    target = jnp.where(rank < CAP, routes * CAP + rank, -1.0).astype(jnp.int32)
    target_ref[...] = target
    copies[1].wait()
    weight = to_column(weight_ref[...])[:, 0:1]
    copies[2].wait()
    grads = (weight * grad_ref[...].astype(F32)).astype(BF)
    write_messages(plan, [target] * plan.fold, split_columns(plan, grads), message_ref)


def pack_kernel(
    plan, target_ref, tags_hbm, q_hbm, k_hbm, v_hbm,
    mine_ref, other_ref, q_mine_ref, q_other_ref, tags_ref, sems,
):
    size = plan.stretch
    odd = lax.axis_index("ctx") % 2
    pieces = [(tags_hbm, tags_ref)]
    for side, block_ref, q_ref in ((1 - odd, other_ref, q_other_ref), (odd, mine_ref, q_mine_ref)):
        base = side * plan.half
        for index, source in enumerate((k_hbm, v_hbm)):
            for piece in range(plan.pieces):
                start = pl.multiple_of(base + piece * PIECE, HEAD)
                row = (index * plan.pieces + piece) * size
                pieces.append((source.at[:, pl.ds(start, PIECE)], block_ref.at[pl.ds(row, size)]))
        span = pl.ds(pl.multiple_of(base, HEAD), plan.half)
        pieces.append((q_hbm.at[:, span], q_ref))
    copies = [
        pltpu.make_async_copy(source, held, sems.at[index])
        for index, (source, held) in enumerate(pieces)
    ]
    for copy in copies:
        copy.start()
    copies[0].wait()
    tags = tags_ref[...].astype(F32) + 1.0
    row = iota((TAG_ROWS, size), 0)
    target = target_ref[...].astype(F32)
    block = jnp.where(row == 0, tags, jnp.where(row == 1, target, 0.0)).astype(BF)
    first = plan.block_rows - TAG_ROWS
    for ref in (mine_ref, other_ref):
        ref[first:, :] = jnp.zeros((TAG_ROWS, PIECE), BF)
        ref[first:, 0:size] = block
    for copy in copies[1:]:
        copy.wait()


class Pair:
    def __init__(self, plan, mine_ref, pair_ref, far_ref, cross_ref):
        self.plan = plan
        self.odd = lax.axis_index("ctx") % 2 == 1
        self.refs = (
            (cross_ref, far_ref), (far_ref, cross_ref), (pair_ref, mine_ref), (mine_ref, pair_ref)
        )

    def choose(self, if_odd, if_even):
        return jnp.where(self.odd, if_odd, if_even)

    def part(self, block, rows, span):
        if_odd, if_even = self.refs[block]
        return self.choose(if_odd[rows, span], if_even[rows, span])

    def head(self, block, piece, lane):
        first = piece * self.plan.stretch
        rows = slice(first, first + self.plan.stretch)
        return self.part(block, rows, slice(lane, lane + HEAD))

    def keys(self, block, head):
        return self.head(block, head * HEAD // PIECE, head * HEAD % PIECE)

    def values(self, block, head):
        return self.head(block, self.plan.pieces + head * HEAD // PIECE, head * HEAD % PIECE)

    def integers(self, block, row):
        rows = slice(self.plan.block_rows - TAG_ROWS, self.plan.block_rows)
        return self.part(block, rows, slice(0, self.plan.stretch)).astype(F32)[row:row + 1]


def softmax_kernel(
    plan, q_mine_ref, q_pair_ref, mine_ref, pair_ref, far_ref, cross_ref, probs_ref
):
    size = plan.stretch
    pair = Pair(plan, mine_ref, pair_ref, far_ref, cross_ref)
    tags = [pair.integers(block, 0) for block in range(4)]
    causal = iota((size, size), 1) <= iota((size, size), 0)
    masks = []
    for query in range(2):
        column = to_column(tags[2 + query])
        masks.append([column == tags[query + block] for block in range(3)])
        masks[query][2] = masks[query][2] & causal
    heads = plan.half // HEAD
    for head in range(heads):
        span = slice(head * HEAD, (head + 1) * HEAD)
        q_mine, q_pair = q_mine_ref[:, span], q_pair_ref[:, span]
        queries = (pair.choose(q_pair, q_mine), pair.choose(q_mine, q_pair))
        blocks = [pair.keys(block, head) for block in range(4)]
        for query in range(2):
            scores = [
                jnp.where(
                    masks[query][block],
                    dot_nt(queries[query], blocks[query + block]) * (1.0 / math.sqrt(HEAD)),
                    -1e30,
                )
                for block in range(3)
            ]
            top = jnp.max(
                jnp.maximum(jnp.maximum(scores[0], scores[1]), scores[2]), axis=-1, keepdims=True
            )
            weights = [jnp.exp(score - top) for score in scores]
            norm = jnp.sum(weights[0] + weights[1] + weights[2], axis=-1, keepdims=True)
            first = (query * heads + head) * size
            for index, weight in enumerate(weights):
                probs_ref[first:first + size, index * size:(index + 1) * size] = (
                    weight / norm
                ).astype(BF)


def hidden_kernel(
    plan, probs_ref, mine_ref, pair_ref, far_ref, cross_ref,
    kept_ref, sent_ref, message_ref, hidden_ref,
):
    size = plan.stretch
    pair = Pair(plan, mine_ref, pair_ref, far_ref, cross_ref)
    heads = plan.half // HEAD
    for head in range(heads):
        span = slice(head * HEAD, (head + 1) * HEAD)
        blocks = [pair.values(block, head) for block in range(4)]
        for query in range(2):
            first = (query * heads + head) * size
            total = None
            for index in range(3):
                probs = probs_ref[first:first + size, index * size:(index + 1) * size]
                term = dot(probs, blocks[query + index])
                total = term if total is None else total + term
            hidden_ref[query * size:(query + 1) * size, span] = total.astype(BF)
    even_rows, odd_rows = hidden_ref[0:size, :], hidden_ref[size:2 * size, :]
    kept_ref[...] = pair.choose(odd_rows, even_rows)
    sent_ref[...] = pair.choose(even_rows, odd_rows)
    targets = [pair.integers(2 + query, 1).astype(jnp.int32) for query in range(2)]
    write_messages(
        plan,
        [targets[part // plan.half_parts] for part in range(plan.fold)],
        split_columns(plan, even_rows) + split_columns(plan, odd_rows),
        message_ref,
    )


def act_kernel(
    plan, message_ref, down_hbm, gate_hbm, up_hbm, act_ref, gate_ref, up_ref,
    down_ref, rows_ref, down_sem, gate_sem, up_sem,
):
    copies = [
        pltpu.make_async_copy(
            down_hbm.at[pl.ds(start, size)], down_ref.at[pl.ds(start, size)], down_sem.at[index]
        )
        for index, (_, start, size) in enumerate(plan.cuts)
    ]
    gate_copy = pltpu.make_async_copy(gate_hbm, gate_ref, gate_sem)
    up_copy = pltpu.make_async_copy(up_hbm, up_ref, up_sem)
    for copy in copies:
        copy.start()
    gate_copy.start()
    up_copy.start()
    read_expert_rows(plan, message_ref, rows_ref)
    for copy, (expert, start, size) in zip(copies, plan.cuts):
        copy.wait()
        rows = rows_ref[expert * plan.expert_rows:(expert + 1) * plan.expert_rows, :]
        act_ref[:, start:start + size] = dot_nt(rows, down_ref[start:start + size, :])
    gate_copy.wait()
    up_copy.wait()


def expert_kernel(
    plan, message_ref, gain_ref, act_ref, gate_ref, up_ref, out_ref,
    held_ref, rows_ref, grad_gate_ref, grad_up_ref, sum_ref,
):
    read_hidden_rows(plan, message_ref, gain_ref, held_ref, rows_ref)
    for expert, start, size in plan.cuts:
        span = slice(start, start + size)
        own = slice(expert * plan.expert_rows, (expert + 1) * plan.expert_rows)
        rows, act = rows_ref[own, :], act_ref[:, span]
        gate_pre, up_pre = dot(rows, gate_ref[:, span]), dot(rows, up_ref[:, span])
        sig = jax.nn.sigmoid(gate_pre)
        grad_gate = act * up_pre * (sig * (1.0 + gate_pre * (1.0 - sig)))
        grad_gate_ref[:, span] = grad_gate.astype(BF)
        grad_up_ref[:, span] = (act * (gate_pre * sig)).astype(BF)
    width = plan.columns // plan.local
    for expert in range(plan.local):
        hidden = slice(expert * width, (expert + 1) * width)
        own = slice(expert * plan.expert_rows, (expert + 1) * plan.expert_rows)
        for start in range(0, plan.model, CUT):
            span = slice(start, start + CUT)
            total = dot_nt(grad_gate_ref[:, hidden], gate_ref[span, hidden])
            total = total + dot_nt(grad_up_ref[:, hidden], up_ref[span, hidden])
            sum_ref[own, span] = total.astype(BF)
    write_expert_rows(plan, sum_ref, out_ref)


def finish_kernel(
    plan, target_ref, gain_ref, kept_ref, back_ref, grad_ref, message_ref, out_ref
):
    target = to_column(target_ref[...].astype(F32))[:, 0:1].astype(jnp.int32)
    parts = [None] * plan.fold
    for chunk in range(plan.chunks):
        wanted, piece = message_slot(plan, chunk, (plan.stretch, CHUNK), 1)
        messages = message_ref[chunk * CHUNK:(chunk + 1) * CHUNK, :]
        for part in range(plan.fold):
            pick = jnp.where((wanted == target) & (piece == part), 1.0, 0.0).astype(BF)
            term = dot(pick, messages)
            parts[part] = term if parts[part] is None else parts[part] + term
    spans = [slice(part * plan.width, (part + 1) * plan.width) for part in range(plan.fold)]
    gained = [
        part.astype(BF).astype(F32) * gain_ref[:, span] for part, span in zip(parts, spans)
    ]
    odd = lax.axis_index("ctx") % 2 == 1
    kept, back = kept_ref[...], back_ref[...]
    halves = (jnp.where(odd, back, kept), jnp.where(odd, kept, back))
    hidden = [
        piece.astype(F32) for half in halves for piece in split_columns(plan, half)
    ]
    squares = sum(jnp.sum(h * h, axis=-1, keepdims=True) for h in hidden)
    inv = lax.rsqrt(squares * (1.0 / plan.model) + 1e-06)
    moment = sum(jnp.sum(h * g, axis=-1, keepdims=True) for h, g in zip(hidden, gained))
    mean = moment * (1.0 / plan.model)
    cube = inv * inv * inv
    for h, g, span in zip(hidden, gained, spans):
        out = grad_ref[:, span].astype(F32) + inv * g - h * cube * mean
        out_ref[:, span] = out.astype(BF)


def params(limit):
    return pltpu.CompilerParams(vmem_limit_bytes=limit)


def in_hbm(value):
    return pltpu.with_memory_space_constraint(value, pltpu.HBM)


def shards(
    queries, keys, values, doc_ids, routes, route_weight, norm_gain, w_gate, w_up, w_down, grad_out
):
    stretch, model = queries.shape[1:]
    ctx_count = lax.axis_size("ctx")
    axes = ("ctx", "ep")
    ep_count = lax.axis_size("ep")
    plan = Plan(ctx_count * ep_count, ep_count, w_gate.shape[1], model, stretch)
    messages = jax.ShapeDtypeStruct((plan.total, plan.width), BF)
    message_bytes = 2 * plan.total * plan.width
    gain = norm_gain.reshape(1, model)

    def exchange(value):
        cut = value.reshape(plan.devices, plan.rows, plan.width)
        cut = lax.all_to_all(cut, axes, split_axis=0, concat_axis=0, tiled=True)
        return cut.reshape(plan.total, plan.width)

    two_up = [(source, source + 2) for source in range(ctx_count - 2)]
    next_pair = [(source, (source ^ 1) + 2) for source in range(ctx_count - 2)]
    pairs = [(source, source ^ 1) for source in range(ctx_count)]

    def send(value, route):
        return lax.ppermute(value, "ctx", route)

    inside = pl.BlockSpec(memory_space=pltpu.VMEM)
    outside = pl.BlockSpec(memory_space=pltpu.HBM)
    block = jax.ShapeDtypeStruct((plan.block_rows, PIECE), BF)
    half = jax.ShapeDtypeStruct((stretch, plan.half), BF)
    grad_messages, target = pl.pallas_call(
        functools.partial(grads_kernel, plan),
        in_specs=[outside] * 3,
        out_shape=(messages, jax.ShapeDtypeStruct((1, stretch), jnp.int32)),
        scratch_shapes=[
            pltpu.VMEM((1, stretch), jnp.int32),
            pltpu.VMEM((1, stretch), F32),
            pltpu.VMEM((stretch, model), BF),
            pltpu.SemaphoreType.DMA((3,)),
        ],
        compiler_params=params(8 * MB + 3 * message_bytes),
        name="route_grads",
    )(
        in_hbm(routes.reshape(1, stretch)), in_hbm(route_weight.reshape(1, stretch)),
        in_hbm(grad_out[0]),
    )
    got_grads = exchange(grad_messages)
    mine, other, q_mine, q_other = pl.pallas_call(
        functools.partial(pack_kernel, plan),
        in_specs=[inside] + [outside] * 4,
        out_shape=(block, block, half, half),
        scratch_shapes=[
            pltpu.VMEM((1, stretch), jnp.int32),
            pltpu.SemaphoreType.DMA((4 * plan.pieces + 3,)),
        ],
        compiler_params=params(8 * MB),
        name="pack",
    )(target, *map(in_hbm, (doc_ids, queries[0], keys[0], values[0])))
    far, cross = send(mine, two_up), send(other, next_pair)
    pair, q_pair = send(other, pairs), send(q_other, pairs)

    rows = plan.local * plan.expert_rows
    weight_bytes = 2 * plan.columns * model
    act, gate, up = pl.pallas_call(
        functools.partial(act_kernel, plan),
        in_specs=[inside, outside, outside, outside],
        out_specs=[inside, inside, inside],
        out_shape=(
            jax.ShapeDtypeStruct((plan.expert_rows, plan.columns), F32),
            pltpu.VMEM(w_gate.shape, BF),
            pltpu.VMEM(w_up.shape, BF),
        ),
        scratch_shapes=[
            pltpu.VMEM(w_down.shape, BF),
            pltpu.VMEM((rows, model), BF),
            pltpu.SemaphoreType.DMA((len(plan.cuts),)),
            pltpu.SemaphoreType.DMA,
            pltpu.SemaphoreType.DMA,
        ],
        compiler_params=params(8 * MB + 6 * message_bytes + weight_bytes),
        cost_estimate=pl.CostEstimate(
            flops=2 * plan.expert_rows * plan.columns * model,
            bytes_accessed=3 * weight_bytes,
            transcendentals=0,
        ),
        name="grad_act",
    )(got_grads, in_hbm(w_down), in_hbm(w_gate), in_hbm(w_up))
    far, cross, pair, q_pair, act = lax.optimization_barrier((far, cross, pair, q_pair, act))

    probs = pl.pallas_call(
        functools.partial(softmax_kernel, plan),
        out_shape=jax.ShapeDtypeStruct((HEADS * stretch, (REACH + 1) * stretch), BF),
        compiler_params=params(16 * MB),
        name="softmax",
    )(q_mine, q_pair, mine, pair, far, cross)
    kept, sent, hidden_messages = pl.pallas_call(
        functools.partial(hidden_kernel, plan),
        out_shape=(half, half, messages),
        scratch_shapes=[pltpu.VMEM((2 * stretch, plan.half), BF)],
        compiler_params=params(12 * MB + 3 * message_bytes),
        name="hidden",
    )(probs, mine, pair, far, cross)
    got_hidden = exchange(hidden_messages)
    got_hidden, sent = lax.optimization_barrier((got_hidden, sent))
    back = send(sent, pairs)

    returned = pl.pallas_call(
        functools.partial(expert_kernel, plan),
        out_shape=messages,
        scratch_shapes=[
            pltpu.VMEM((rows, model), F32),
            pltpu.VMEM((rows, model), BF),
            pltpu.VMEM((plan.expert_rows, plan.columns), BF),
            pltpu.VMEM((plan.expert_rows, plan.columns), BF),
            pltpu.VMEM((rows, model), BF),
        ],
        compiler_params=params(12 * MB + 8 * message_bytes),
        cost_estimate=pl.CostEstimate(
            flops=8 * plan.expert_rows * plan.columns * model,
            bytes_accessed=2 * weight_bytes,
            transcendentals=0,
        ),
        name="experts",
    )(got_hidden, gain, act, gate, up)
    returned, back = lax.optimization_barrier((returned, back))
    combined = exchange(returned)

    grad_in = pl.pallas_call(
        functools.partial(finish_kernel, plan),
        out_shape=jax.ShapeDtypeStruct((stretch, model), BF),
        compiler_params=params(12 * MB + 3 * message_bytes),
        name="finish",
    )(target, gain, kept, back, grad_out[0], combined)
    return grad_in[None]


def solution(mesh):
    in_specs = (
        P("ep", "ctx", None),
        P("ep", "ctx", None),
        P("ep", "ctx", None),
        P("ep", "ctx"),
        P("ep", "ctx", None),
        P("ep", "ctx", None),
        P(),
        P(None, ("ctx", "ep")),
        P(None, ("ctx", "ep")),
        P(("ctx", "ep"), None),
        P("ep", "ctx", None),
    )
    out_specs = P("ep", "ctx", None)
    return jax.shard_map(shards, mesh=mesh, in_specs=in_specs, out_specs=out_specs, check_vma=False)
```

```python
import functools
import math

import jax
import jax.numpy as jnp
from jax import lax
from jax.experimental import pallas as pl
from jax.experimental.pallas import tpu as pltpu
from jax.sharding import PartitionSpec as P

HEADS = 16
HEAD = 128
EXPERTS = 64
FF = 1408
CAP = 2
REACH = 2
CHUNK = 256
TAG_ROWS = 16
CUT = 512
PIECE = 256
BF = jnp.bfloat16
F32 = jnp.float32
MB = 1024 * 1024


def iota(shape, dim):
    return lax.broadcasted_iota(jnp.int32, shape, dim)


def dot(left, right):
    return jnp.dot(left, right, preferred_element_type=F32)


def dot_nt(left, right):
    return lax.dot_general(left, right, (((1,), (1,)), ((), ())), preferred_element_type=F32)


class Plan:
    def __init__(self, devices, eps, columns, width, stretch):
        self.devices = devices
        self.eps = eps
        self.columns = columns
        self.model = width
        self.stretch = stretch
        self.local = max(1, columns // FF)
        self.sharers = max(1, FF // columns)
        self.slots = self.local * CAP
        self.fold = max(2, 8 // self.slots)
        self.width = width // self.fold
        self.rows = self.slots * self.fold
        self.total = devices * self.rows
        self.chunks = self.total // CHUNK
        self.group = CHUNK // self.rows
        self.expert_rows = devices * CAP
        self.half = width // 2
        self.half_parts = self.fold // 2
        self.pieces = self.half // PIECE
        self.block_rows = 2 * self.pieces * stretch + TAG_ROWS
        own = columns // self.local
        self.cuts = [
            (expert, expert * own + start, min(own - start, CUT))
            for expert in range(self.local)
            for start in range(0, own, CUT)
        ]


def message_slot(plan, chunk, shape, dim):
    row = iota(shape, dim)
    device = chunk * plan.group + row // plan.rows
    within = row % plan.rows
    first = device * plan.local if plan.sharers == 1 else device // plan.sharers
    return first * CAP + within % plan.slots, within // plan.slots


def write_messages(plan, targets, values, out_ref):
    for chunk in range(plan.chunks):
        wanted, piece = message_slot(plan, chunk, (CHUNK, plan.stretch), 0)
        total = None
        for part in range(plan.fold):
            hit = (wanted == targets[part]) & (piece == part)
            term = dot(jnp.where(hit, 1.0, 0.0).astype(BF), values[part])
            total = term if total is None else total + term
        out_ref[chunk * CHUNK:(chunk + 1) * CHUNK, :] = total.astype(BF)


def split_columns(plan, value):
    count = value.shape[1] // plan.width
    return [value[:, part * plan.width:(part + 1) * plan.width] for part in range(count)]


def expert_pick(plan, expert, part, shape, row_dim, message_dim):
    row = iota(shape, row_dim)
    message = iota(shape, message_dim)
    wanted = (row // CAP) * plan.rows + part * plan.slots + expert * CAP + row % CAP
    return jnp.where(wanted == message, 1.0, 0.0).astype(BF)


def read_expert_rows(plan, message_ref, rows_ref):
    count = plan.group * CAP
    for expert in range(plan.local):
        for part in range(plan.fold):
            pick = expert_pick(plan, expert, part, (count, CHUNK), 0, 1)
            for chunk in range(plan.chunks):
                base = expert * plan.expert_rows + chunk * count
                got = dot(pick, message_ref[chunk * CHUNK:(chunk + 1) * CHUNK, :])
                rows_ref[base:base + count, part * plan.width:(part + 1) * plan.width] = got.astype(BF)


def inv_rms(plan, held):
    mean = jnp.sum(held * held, axis=-1, keepdims=True) * (1.0 / plan.model)
    return lax.rsqrt(mean + 1e-06)


def read_hidden_rows(plan, message_ref, gain_ref, held_ref, rows_ref):
    count = plan.group * CAP
    shape = (count, CHUNK)
    row, message = iota(shape, 0), iota(shape, 1)
    owner = row // CAP
    parity = (owner // plan.eps) % 2
    for half in range(2):
        source = owner + (half - parity) * plan.eps
        for part in range(plan.half_parts):
            start = half * plan.half + part * plan.width
            first = source * plan.rows + (parity * plan.half_parts + part) * plan.slots
            for expert in range(plan.local):
                wanted = first + expert * CAP + row % CAP
                pick = jnp.where(wanted == message, 1.0, 0.0).astype(BF)
                for chunk in range(plan.chunks):
                    base = expert * plan.expert_rows + chunk * count
                    held_ref[base:base + count, start:start + plan.width] = dot(
                        pick, message_ref[chunk * CHUNK:(chunk + 1) * CHUNK, :]
                    )
    held = held_ref[...]
    rows_ref[...] = (held * inv_rms(plan, held) * gain_ref[...]).astype(BF)


def write_expert_rows(plan, rows, message_ref):
    count = plan.local * plan.expert_rows
    for chunk in range(plan.chunks):
        message = iota((CHUNK, count), 0) + chunk * CHUNK
        row = iota((CHUNK, count), 1)
        sender = (row % plan.expert_rows) // CAP
        slot = (row // plan.expert_rows) * CAP + row % CAP
        total = None
        for part in range(plan.fold):
            wanted = sender * plan.rows + part * plan.slots + slot
            pick = jnp.where(wanted == message, 1.0, 0.0).astype(BF)
            term = dot(pick, rows[:, part * plan.width:(part + 1) * plan.width])
            total = term if total is None else total + term
        message_ref[chunk * CHUNK:(chunk + 1) * CHUNK, :] = total.astype(BF)


def norm_backward(plan, columns_ref, held_ref, gain_ref):
    count = plan.local * plan.expert_rows
    same = iota((count, count), 0) == iota((count, count), 1)
    grads = dot_nt(jnp.where(same, 1.0, 0.0).astype(BF), columns_ref[...])
    gained = grads * gain_ref[...]
    held = held_ref[...]
    inv = inv_rms(plan, held)
    mean = jnp.sum(held * gained, axis=-1, keepdims=True) * (1.0 / plan.model)
    return (inv * gained - held * (inv * inv * inv) * mean).astype(BF)


def to_column(row):
    size = row.shape[1]
    return jnp.transpose(jnp.broadcast_to(row, (size, size)))


def grads_kernel(
    plan, routes_hbm, weight_hbm, grad_hbm, message_ref, target_ref,
    routes_ref, weight_ref, grad_ref, sems,
):
    size = plan.stretch
    pieces = ((routes_hbm, routes_ref), (weight_hbm, weight_ref), (grad_hbm, grad_ref))
    copies = [
        pltpu.make_async_copy(source, held, sems.at[index])
        for index, (source, held) in enumerate(pieces)
    ]
    for copy in copies:
        copy.start()
    copies[0].wait()
    routes = routes_ref[...].astype(F32)
    earlier = iota((size, size), 0) < iota((size, size), 1)
    same = (to_column(routes) == routes) & earlier
    rank = jnp.sum(jnp.where(same, 1.0, 0.0), axis=0, keepdims=True)
    target = jnp.where(rank < CAP, routes * CAP + rank, -1.0).astype(jnp.int32)
    target_ref[...] = target
    copies[1].wait()
    weight = to_column(weight_ref[...])[:, 0:1]
    copies[2].wait()
    grads = (weight * grad_ref[...].astype(F32)).astype(BF)
    write_messages(plan, [target] * plan.fold, split_columns(plan, grads), message_ref)


def pack_kernel(
    plan, target_ref, tags_hbm, q_hbm, k_hbm, v_hbm,
    mine_ref, other_ref, q_mine_ref, q_other_ref, tags_ref, sems,
):
    size = plan.stretch
    odd = lax.axis_index("ctx") % 2
    pieces = [(tags_hbm, tags_ref)]
    for side, block_ref, q_ref in ((1 - odd, other_ref, q_other_ref), (odd, mine_ref, q_mine_ref)):
        base = side * plan.half
        for index, source in enumerate((k_hbm, v_hbm)):
            for piece in range(plan.pieces):
                start = pl.multiple_of(base + piece * PIECE, HEAD)
                row = (index * plan.pieces + piece) * size
                pieces.append((source.at[:, pl.ds(start, PIECE)], block_ref.at[pl.ds(row, size)]))
        span = pl.ds(pl.multiple_of(base, HEAD), plan.half)
        pieces.append((q_hbm.at[:, span], q_ref))
    copies = [
        pltpu.make_async_copy(source, held, sems.at[index])
        for index, (source, held) in enumerate(pieces)
    ]
    for copy in copies:
        copy.start()
    copies[0].wait()
    tags = tags_ref[...].astype(F32) + 1.0
    row = iota((TAG_ROWS, size), 0)
    target = target_ref[...].astype(F32)
    block = jnp.where(row == 0, tags, jnp.where(row == 1, target, 0.0)).astype(BF)
    first = plan.block_rows - TAG_ROWS
    for ref in (mine_ref, other_ref):
        ref[first:, :] = jnp.zeros((TAG_ROWS, PIECE), BF)
        ref[first:, 0:size] = block
    for copy in copies[1:]:
        copy.wait()


class Pair:
    def __init__(self, plan, mine_ref, pair_ref, far_ref, cross_ref):
        self.plan = plan
        self.odd = lax.axis_index("ctx") % 2 == 1
        self.refs = (
            (cross_ref, far_ref), (far_ref, cross_ref), (pair_ref, mine_ref), (mine_ref, pair_ref)
        )

    def choose(self, if_odd, if_even):
        return jnp.where(self.odd, if_odd, if_even)

    def part(self, block, rows, span):
        if_odd, if_even = self.refs[block]
        return self.choose(if_odd[rows, span], if_even[rows, span])

    def head(self, block, piece, lane):
        first = piece * self.plan.stretch
        rows = slice(first, first + self.plan.stretch)
        return self.part(block, rows, slice(lane, lane + HEAD))

    def keys(self, block, head):
        return self.head(block, head * HEAD // PIECE, head * HEAD % PIECE)

    def values(self, block, head):
        return self.head(block, self.plan.pieces + head * HEAD // PIECE, head * HEAD % PIECE)

    def integers(self, block, row):
        rows = slice(self.plan.block_rows - TAG_ROWS, self.plan.block_rows)
        return self.part(block, rows, slice(0, self.plan.stretch)).astype(F32)[row:row + 1]


def softmax_kernel(
    plan, q_mine_ref, q_pair_ref, mine_ref, pair_ref, far_ref, cross_ref, probs_ref
):
    size = plan.stretch
    pair = Pair(plan, mine_ref, pair_ref, far_ref, cross_ref)
    tags = [pair.integers(block, 0) for block in range(4)]
    causal = iota((size, size), 1) <= iota((size, size), 0)
    masks = []
    for query in range(2):
        column = to_column(tags[2 + query])
        masks.append([column == tags[query + block] for block in range(3)])
        masks[query][2] = masks[query][2] & causal
    heads = plan.half // HEAD
    for head in range(heads):
        span = slice(head * HEAD, (head + 1) * HEAD)
        q_mine, q_pair = q_mine_ref[:, span], q_pair_ref[:, span]
        queries = (pair.choose(q_pair, q_mine), pair.choose(q_mine, q_pair))
        blocks = [pair.keys(block, head) for block in range(4)]
        for query in range(2):
            scores = [
                jnp.where(
                    masks[query][block],
                    dot_nt(queries[query], blocks[query + block]) * (1.0 / math.sqrt(HEAD)),
                    -1e30,
                )
                for block in range(3)
            ]
            top = jnp.max(
                jnp.maximum(jnp.maximum(scores[0], scores[1]), scores[2]), axis=-1, keepdims=True
            )
            weights = [jnp.exp(score - top) for score in scores]
            norm = jnp.sum(weights[0] + weights[1] + weights[2], axis=-1, keepdims=True)
            first = (query * heads + head) * size
            for index, weight in enumerate(weights):
                probs_ref[first:first + size, index * size:(index + 1) * size] = (
                    weight / norm
                ).astype(BF)


def hidden_kernel(
    plan, probs_ref, mine_ref, pair_ref, far_ref, cross_ref, message_ref, hidden_ref
):
    size = plan.stretch
    pair = Pair(plan, mine_ref, pair_ref, far_ref, cross_ref)
    heads = plan.half // HEAD
    for head in range(heads):
        span = slice(head * HEAD, (head + 1) * HEAD)
        blocks = [pair.values(block, head) for block in range(4)]
        for query in range(2):
            first = (query * heads + head) * size
            total = None
            for index in range(3):
                probs = probs_ref[first:first + size, index * size:(index + 1) * size]
                term = dot(probs, blocks[query + index])
                total = term if total is None else total + term
            hidden_ref[query * size:(query + 1) * size, span] = total.astype(BF)
    even_rows, odd_rows = hidden_ref[0:size, :], hidden_ref[size:2 * size, :]
    targets = [pair.integers(2 + query, 1).astype(jnp.int32) for query in range(2)]
    write_messages(
        plan,
        [targets[part // plan.half_parts] for part in range(plan.fold)],
        split_columns(plan, even_rows) + split_columns(plan, odd_rows),
        message_ref,
    )


def act_kernel(
    plan, message_ref, down_hbm, gate_hbm, up_hbm, act_ref, gate_ref, up_ref,
    down_ref, rows_ref, down_sem, gate_sem, up_sem,
):
    copies = [
        pltpu.make_async_copy(
            down_hbm.at[pl.ds(start, size)], down_ref.at[pl.ds(start, size)], down_sem.at[index]
        )
        for index, (_, start, size) in enumerate(plan.cuts)
    ]
    gate_copy = pltpu.make_async_copy(gate_hbm, gate_ref, gate_sem)
    up_copy = pltpu.make_async_copy(up_hbm, up_ref, up_sem)
    for copy in copies:
        copy.start()
    gate_copy.start()
    up_copy.start()
    read_expert_rows(plan, message_ref, rows_ref)
    for copy, (expert, start, size) in zip(copies, plan.cuts):
        copy.wait()
        rows = rows_ref[expert * plan.expert_rows:(expert + 1) * plan.expert_rows, :]
        act_ref[:, start:start + size] = dot_nt(rows, down_ref[start:start + size, :])
    gate_copy.wait()
    up_copy.wait()


def expert_kernel(
    plan, message_ref, gain_ref, act_ref, gate_ref, up_ref, out_ref,
    held_ref, rows_ref, grad_gate_ref, grad_up_ref, sum_ref,
):
    read_hidden_rows(plan, message_ref, gain_ref, held_ref, rows_ref)
    grad_gate_ref[...] = jnp.zeros_like(grad_gate_ref)
    grad_up_ref[...] = jnp.zeros_like(grad_up_ref)
    for expert, start, size in plan.cuts:
        span = slice(start, start + size)
        own = slice(expert * plan.expert_rows, (expert + 1) * plan.expert_rows)
        rows, act = rows_ref[own, :], act_ref[:, span]
        gate_pre, up_pre = dot(rows, gate_ref[:, span]), dot(rows, up_ref[:, span])
        sig = jax.nn.sigmoid(gate_pre)
        grad_gate = act * up_pre * (sig * (1.0 + gate_pre * (1.0 - sig)))
        grad_gate_ref[own, span] = grad_gate.astype(BF)
        grad_up_ref[own, span] = (act * (gate_pre * sig)).astype(BF)
    for start in range(0, plan.model, CHUNK):
        span = slice(start, start + CHUNK)
        total = dot_nt(gate_ref[span, :], grad_gate_ref[...])
        total = total + dot_nt(up_ref[span, :], grad_up_ref[...])
        sum_ref[span, :] = total.astype(BF)
    write_expert_rows(plan, norm_backward(plan, sum_ref, held_ref, gain_ref), out_ref)


def finish_kernel(plan, target_ref, grad_ref, message_ref, out_ref):
    target = to_column(target_ref[...].astype(F32))[:, 0:1].astype(jnp.int32)
    parts = [None] * plan.fold
    for chunk in range(plan.chunks):
        wanted, piece = message_slot(plan, chunk, (plan.stretch, CHUNK), 1)
        messages = message_ref[chunk * CHUNK:(chunk + 1) * CHUNK, :]
        for part in range(plan.fold):
            pick = jnp.where((wanted == target) & (piece == part), 1.0, 0.0).astype(BF)
            term = dot(pick, messages)
            parts[part] = term if parts[part] is None else parts[part] + term
    for part, term in enumerate(parts):
        span = slice(part * plan.width, (part + 1) * plan.width)
        out_ref[:, span] = (grad_ref[:, span].astype(F32) + term).astype(BF)


def params(limit):
    return pltpu.CompilerParams(vmem_limit_bytes=limit)


def in_hbm(value):
    return pltpu.with_memory_space_constraint(value, pltpu.HBM)


def shards(
    queries, keys, values, doc_ids, routes, route_weight, norm_gain, w_gate, w_up, w_down, grad_out
):
    stretch, model = queries.shape[1:]
    ctx_count = lax.axis_size("ctx")
    axes = ("ctx", "ep")
    ep_count = lax.axis_size("ep")
    plan = Plan(ctx_count * ep_count, ep_count, w_gate.shape[1], model, stretch)
    messages = jax.ShapeDtypeStruct((plan.total, plan.width), BF)
    message_bytes = 2 * plan.total * plan.width
    gain = norm_gain.reshape(1, model)

    def exchange(value):
        cut = value.reshape(plan.devices, plan.rows, plan.width)
        cut = lax.all_to_all(cut, axes, split_axis=0, concat_axis=0, tiled=True)
        return cut.reshape(plan.total, plan.width)

    two_up = [(source, source + 2) for source in range(ctx_count - 2)]
    next_pair = [(source, (source ^ 1) + 2) for source in range(ctx_count - 2)]
    pairs = [(source, source ^ 1) for source in range(ctx_count)]

    def send(value, route):
        return lax.ppermute(value, "ctx", route)

    inside = pl.BlockSpec(memory_space=pltpu.VMEM)
    outside = pl.BlockSpec(memory_space=pltpu.HBM)
    block = jax.ShapeDtypeStruct((plan.block_rows, PIECE), BF)
    half = jax.ShapeDtypeStruct((stretch, plan.half), BF)
    grad_messages, target = pl.pallas_call(
        functools.partial(grads_kernel, plan),
        in_specs=[outside] * 3,
        out_shape=(messages, jax.ShapeDtypeStruct((1, stretch), jnp.int32)),
        scratch_shapes=[
            pltpu.VMEM((1, stretch), jnp.int32),
            pltpu.VMEM((1, stretch), F32),
            pltpu.VMEM((stretch, model), BF),
            pltpu.SemaphoreType.DMA((3,)),
        ],
        compiler_params=params(8 * MB + 3 * message_bytes),
        name="route_grads",
    )(
        in_hbm(routes.reshape(1, stretch)), in_hbm(route_weight.reshape(1, stretch)),
        in_hbm(grad_out[0]),
    )
    got_grads = exchange(grad_messages)
    mine, other, q_mine, q_other = pl.pallas_call(
        functools.partial(pack_kernel, plan),
        in_specs=[inside] + [outside] * 4,
        out_shape=(block, block, half, half),
        scratch_shapes=[
            pltpu.VMEM((1, stretch), jnp.int32),
            pltpu.SemaphoreType.DMA((4 * plan.pieces + 3,)),
        ],
        compiler_params=params(8 * MB),
        name="pack",
    )(target, *map(in_hbm, (doc_ids, queries[0], keys[0], values[0])))
    far, cross = send(mine, two_up), send(other, next_pair)
    pair, q_pair = send(other, pairs), send(q_other, pairs)

    rows = plan.local * plan.expert_rows
    weight_bytes = 2 * plan.columns * model
    act, gate, up = pl.pallas_call(
        functools.partial(act_kernel, plan),
        in_specs=[inside, outside, outside, outside],
        out_specs=[inside, inside, inside],
        out_shape=(
            jax.ShapeDtypeStruct((plan.expert_rows, plan.columns), F32),
            pltpu.VMEM(w_gate.shape, BF),
            pltpu.VMEM(w_up.shape, BF),
        ),
        scratch_shapes=[
            pltpu.VMEM(w_down.shape, BF),
            pltpu.VMEM((rows, model), BF),
            pltpu.SemaphoreType.DMA((len(plan.cuts),)),
            pltpu.SemaphoreType.DMA,
            pltpu.SemaphoreType.DMA,
        ],
        compiler_params=params(8 * MB + 6 * message_bytes + weight_bytes),
        cost_estimate=pl.CostEstimate(
            flops=2 * plan.expert_rows * plan.columns * model,
            bytes_accessed=3 * weight_bytes,
            transcendentals=0,
        ),
        name="grad_act",
    )(got_grads, in_hbm(w_down), in_hbm(w_gate), in_hbm(w_up))
    far, cross, pair, q_pair, act = lax.optimization_barrier((far, cross, pair, q_pair, act))

    probs = pl.pallas_call(
        functools.partial(softmax_kernel, plan),
        out_shape=jax.ShapeDtypeStruct((HEADS * stretch, (REACH + 1) * stretch), BF),
        compiler_params=params(16 * MB),
        name="softmax",
    )(q_mine, q_pair, mine, pair, far, cross)
    hidden_messages = pl.pallas_call(
        functools.partial(hidden_kernel, plan),
        out_shape=messages,
        scratch_shapes=[pltpu.VMEM((2 * stretch, plan.half), BF)],
        compiler_params=params(12 * MB + 3 * message_bytes),
        name="hidden",
    )(probs, mine, pair, far, cross)
    got_hidden = exchange(hidden_messages)

    returned = pl.pallas_call(
        functools.partial(expert_kernel, plan),
        out_shape=messages,
        scratch_shapes=[
            pltpu.VMEM((rows, model), F32),
            pltpu.VMEM((rows, model), BF),
            pltpu.VMEM((rows, plan.columns), BF),
            pltpu.VMEM((rows, plan.columns), BF),
            pltpu.VMEM((model, rows), BF),
        ],
        compiler_params=params(12 * MB + 8 * message_bytes),
        cost_estimate=pl.CostEstimate(
            flops=8 * plan.expert_rows * plan.columns * model,
            bytes_accessed=2 * weight_bytes,
            transcendentals=0,
        ),
        name="experts",
    )(got_hidden, gain, act, gate, up)
    combined = exchange(returned)

    grad_in = pl.pallas_call(
        functools.partial(finish_kernel, plan),
        out_shape=jax.ShapeDtypeStruct((stretch, model), BF),
        compiler_params=params(12 * MB + 3 * message_bytes),
        name="finish",
    )(target, grad_out[0], combined)
    return grad_in[None]


def solution(mesh):
    in_specs = (
        P("ep", "ctx", None),
        P("ep", "ctx", None),
        P("ep", "ctx", None),
        P("ep", "ctx"),
        P("ep", "ctx", None),
        P("ep", "ctx", None),
        P(),
        P(None, ("ctx", "ep")),
        P(None, ("ctx", "ep")),
        P(("ctx", "ep"), None),
        P("ep", "ctx", None),
    )
    out_specs = P("ep", "ctx", None)
    return jax.shard_map(shards, mesh=mesh, in_specs=in_specs, out_specs=out_specs, check_vma=False)
```

```python
import functools
import math

import jax
import jax.numpy as jnp
from jax import lax
from jax.experimental import pallas as pl
from jax.experimental.pallas import tpu as pltpu
from jax.sharding import PartitionSpec as P

HEADS = 16
HEAD = 128
EXPERTS = 64
FF = 1408
CAP = 2
REACH = 2
CHUNK = 256
TAG_ROWS = 16
CUT = 512
PIECE = 256
BF = jnp.bfloat16
F32 = jnp.float32
MB = 1024 * 1024


def iota(shape, dim):
    return lax.broadcasted_iota(jnp.int32, shape, dim)


def dot(left, right):
    return jnp.dot(left, right, preferred_element_type=F32)


def dot_nt(left, right):
    return lax.dot_general(left, right, (((1,), (1,)), ((), ())), preferred_element_type=F32)


class Plan:
    def __init__(self, devices, eps, columns, width, stretch):
        self.devices = devices
        self.eps = eps
        self.columns = columns
        self.model = width
        self.stretch = stretch
        self.local = max(1, columns // FF)
        self.sharers = max(1, FF // columns)
        self.slots = self.local * CAP
        self.fold = max(2, 8 // self.slots)
        self.width = width // self.fold
        self.rows = self.slots * self.fold
        self.total = devices * self.rows
        self.chunks = self.total // CHUNK
        self.group = CHUNK // self.rows
        self.expert_rows = devices * CAP
        self.half = width // 2
        self.half_parts = self.fold // 2
        self.pieces = self.half // PIECE
        self.block_rows = 2 * self.pieces * stretch + TAG_ROWS
        own = columns // self.local
        self.cuts = [
            (expert, expert * own + start, min(own - start, CUT))
            for expert in range(self.local)
            for start in range(0, own, CUT)
        ]


def message_slot(plan, chunk, shape, dim):
    row = iota(shape, dim)
    device = chunk * plan.group + row // plan.rows
    within = row % plan.rows
    first = device * plan.local if plan.sharers == 1 else device // plan.sharers
    return first * CAP + within % plan.slots, within // plan.slots


def write_messages(plan, targets, values, out_ref):
    shape = (CHUNK, plan.fold * plan.stretch)
    column_part = iota(shape, 1) // plan.stretch
    target = jnp.concatenate(targets, axis=1)
    stacked = jnp.concatenate(values, axis=0)
    for chunk in range(plan.chunks):
        wanted, piece = message_slot(plan, chunk, shape, 0)
        hit = (wanted == target) & (piece == column_part)
        total = dot(jnp.where(hit, 1.0, 0.0).astype(BF), stacked)
        out_ref[chunk * CHUNK:(chunk + 1) * CHUNK, :] = total.astype(BF)


def split_columns(plan, value):
    count = value.shape[1] // plan.width
    return [value[:, part * plan.width:(part + 1) * plan.width] for part in range(count)]


def expert_pick(plan, expert, part, shape, row_dim, message_dim):
    row = iota(shape, row_dim)
    message = iota(shape, message_dim)
    wanted = (row // CAP) * plan.rows + part * plan.slots + expert * CAP + row % CAP
    return jnp.where(wanted == message, 1.0, 0.0).astype(BF)


def read_expert_rows(plan, message_ref, rows_ref):
    count = plan.group * CAP
    for expert in range(plan.local):
        for part in range(plan.fold):
            pick = expert_pick(plan, expert, part, (count, CHUNK), 0, 1)
            for chunk in range(plan.chunks):
                base = expert * plan.expert_rows + chunk * count
                got = dot(pick, message_ref[chunk * CHUNK:(chunk + 1) * CHUNK, :])
                rows_ref[base:base + count, part * plan.width:(part + 1) * plan.width] = got.astype(BF)


def inv_rms(plan, held):
    mean = jnp.sum(held * held, axis=-1, keepdims=True) * (1.0 / plan.model)
    return lax.rsqrt(mean + 1e-06)


def read_hidden_rows(plan, message_ref, gain_ref, held_ref, rows_ref):
    count = plan.group * CAP
    shape = (plan.local * count, CHUNK)
    row, message = iota(shape, 0), iota(shape, 1)
    expert, owner = row // count, row % count // CAP
    parity = (owner // plan.eps) % 2
    for half in range(2):
        source = owner + (half - parity) * plan.eps
        for part in range(plan.half_parts):
            span = slice(half * plan.half + part * plan.width, half * plan.half + (part + 1) * plan.width)
            first = source * plan.rows + (parity * plan.half_parts + part) * plan.slots
            pick = jnp.where(first + expert * CAP + row % CAP == message, 1.0, 0.0).astype(BF)
            for chunk in range(plan.chunks):
                got = dot(pick, message_ref[chunk * CHUNK:(chunk + 1) * CHUNK, :])
                for index in range(plan.local):
                    base = index * plan.expert_rows + chunk * count
                    held_ref[base:base + count, span] = got[index * count:(index + 1) * count]
    held = held_ref[...]
    rows_ref[...] = (held * inv_rms(plan, held) * gain_ref[...]).astype(BF)


def write_expert_rows(plan, rows, message_ref):
    count = plan.local * plan.expert_rows
    shape = (CHUNK, plan.fold * count)
    column = iota(shape, 1)
    part, row = column // count, column % count
    sender = (row % plan.expert_rows) // CAP
    slot = (row // plan.expert_rows) * CAP + row % CAP
    wanted = sender * plan.rows + part * plan.slots + slot
    stacked = jnp.concatenate(split_columns(plan, rows), axis=0)
    for chunk in range(plan.chunks):
        message = iota(shape, 0) + chunk * CHUNK
        total = dot(jnp.where(wanted == message, 1.0, 0.0).astype(BF), stacked)
        message_ref[chunk * CHUNK:(chunk + 1) * CHUNK, :] = total.astype(BF)


def norm_backward(plan, columns_ref, held_ref, gain_ref):
    count = plan.local * plan.expert_rows
    same = iota((count, count), 0) == iota((count, count), 1)
    grads = dot_nt(jnp.where(same, 1.0, 0.0).astype(BF), columns_ref[...])
    gained = grads * gain_ref[...]
    held = held_ref[...]
    inv = inv_rms(plan, held)
    mean = jnp.sum(held * gained, axis=-1, keepdims=True) * (1.0 / plan.model)
    return (inv * gained - held * (inv * inv * inv) * mean).astype(BF)


def to_column(row):
    size = row.shape[1]
    return jnp.transpose(jnp.broadcast_to(row, (size, size)))


def grads_kernel(
    plan, routes_hbm, weight_hbm, grad_hbm, message_ref, target_ref,
    routes_ref, weight_ref, grad_ref, sems,
):
    size = plan.stretch
    pieces = ((routes_hbm, routes_ref), (weight_hbm, weight_ref), (grad_hbm, grad_ref))
    copies = [
        pltpu.make_async_copy(source, held, sems.at[index])
        for index, (source, held) in enumerate(pieces)
    ]
    for copy in copies:
        copy.start()
    copies[0].wait()
    routes = routes_ref[...].astype(F32)
    earlier = iota((size, size), 0) < iota((size, size), 1)
    same = (to_column(routes) == routes) & earlier
    rank = jnp.sum(jnp.where(same, 1.0, 0.0), axis=0, keepdims=True)
    target = jnp.where(rank < CAP, routes * CAP + rank, -1.0).astype(jnp.int32)
    target_ref[...] = target
    copies[1].wait()
    weight = to_column(weight_ref[...])[:, 0:1]
    copies[2].wait()
    grads = (weight * grad_ref[...].astype(F32)).astype(BF)
    write_messages(plan, [target] * plan.fold, split_columns(plan, grads), message_ref)


def pack_kernel(
    plan, target_ref, tags_hbm, q_hbm, k_hbm, v_hbm,
    mine_ref, other_ref, q_mine_ref, q_other_ref, tags_ref, sems,
):
    size = plan.stretch
    odd = lax.axis_index("ctx") % 2
    pieces = [(tags_hbm, tags_ref)]
    for side, block_ref, q_ref in ((1 - odd, other_ref, q_other_ref), (odd, mine_ref, q_mine_ref)):
        base = side * plan.half
        for index, source in enumerate((k_hbm, v_hbm)):
            for piece in range(plan.pieces):
                start = pl.multiple_of(base + piece * PIECE, HEAD)
                row = (index * plan.pieces + piece) * size
                pieces.append((source.at[:, pl.ds(start, PIECE)], block_ref.at[pl.ds(row, size)]))
        span = pl.ds(pl.multiple_of(base, HEAD), plan.half)
        pieces.append((q_hbm.at[:, span], q_ref))
    copies = [
        pltpu.make_async_copy(source, held, sems.at[index])
        for index, (source, held) in enumerate(pieces)
    ]
    for copy in copies:
        copy.start()
    copies[0].wait()
    tags = tags_ref[...].astype(F32) + 1.0
    row = iota((TAG_ROWS, size), 0)
    target = target_ref[...].astype(F32)
    block = jnp.where(row == 0, tags, jnp.where(row == 1, target, 0.0)).astype(BF)
    first = plan.block_rows - TAG_ROWS
    for ref in (mine_ref, other_ref):
        ref[first:, :] = jnp.zeros((TAG_ROWS, PIECE), BF)
        ref[first:, 0:size] = block
    for copy in copies[1:]:
        copy.wait()


class Pair:
    def __init__(self, plan, mine_ref, pair_ref, far_ref, cross_ref):
        self.plan = plan
        self.odd = lax.axis_index("ctx") % 2 == 1
        self.refs = (
            (cross_ref, far_ref), (far_ref, cross_ref), (pair_ref, mine_ref), (mine_ref, pair_ref)
        )

    def choose(self, if_odd, if_even):
        return jnp.where(self.odd, if_odd, if_even)

    def part(self, block, rows, span):
        if_odd, if_even = self.refs[block]
        return self.choose(if_odd[rows, span], if_even[rows, span])

    def head(self, block, piece, lane):
        first = piece * self.plan.stretch
        rows = slice(first, first + self.plan.stretch)
        return self.part(block, rows, slice(lane, lane + HEAD))

    def keys(self, block, head):
        return self.head(block, head * HEAD // PIECE, head * HEAD % PIECE)

    def values(self, block, head):
        return self.head(block, self.plan.pieces + head * HEAD // PIECE, head * HEAD % PIECE)

    def integers(self, block, row):
        rows = slice(self.plan.block_rows - TAG_ROWS, self.plan.block_rows)
        return self.part(block, rows, slice(0, self.plan.stretch)).astype(F32)[row:row + 1]


def softmax_kernel(
    plan, q_mine_ref, q_pair_ref, mine_ref, pair_ref, far_ref, cross_ref, probs_ref
):
    size = plan.stretch
    pair = Pair(plan, mine_ref, pair_ref, far_ref, cross_ref)
    tags = [pair.integers(block, 0) for block in range(4)]
    causal = iota((size, size), 1) <= iota((size, size), 0)
    masks = []
    for query in range(2):
        column = to_column(tags[2 + query])
        masks.append([column == tags[query + block] for block in range(3)])
        masks[query][2] = masks[query][2] & causal
    heads = plan.half // HEAD
    for head in range(heads):
        span = slice(head * HEAD, (head + 1) * HEAD)
        q_mine, q_pair = q_mine_ref[:, span], q_pair_ref[:, span]
        queries = (pair.choose(q_pair, q_mine), pair.choose(q_mine, q_pair))
        blocks = [pair.keys(block, head) for block in range(4)]
        for query in range(2):
            scores = [
                jnp.where(
                    masks[query][block],
                    dot_nt(queries[query], blocks[query + block]) * (1.0 / math.sqrt(HEAD)),
                    -1e30,
                )
                for block in range(3)
            ]
            top = jnp.max(
                jnp.maximum(jnp.maximum(scores[0], scores[1]), scores[2]), axis=-1, keepdims=True
            )
            weights = [jnp.exp(score - top) for score in scores]
            norm = jnp.sum(weights[0] + weights[1] + weights[2], axis=-1, keepdims=True)
            first = (query * heads + head) * size
            for index, weight in enumerate(weights):
                probs_ref[first:first + size, index * size:(index + 1) * size] = (
                    weight / norm
                ).astype(BF)


def hidden_kernel(
    plan, probs_ref, mine_ref, pair_ref, far_ref, cross_ref, message_ref, hidden_ref
):
    size = plan.stretch
    pair = Pair(plan, mine_ref, pair_ref, far_ref, cross_ref)
    heads = plan.half // HEAD
    for head in range(heads):
        span = slice(head * HEAD, (head + 1) * HEAD)
        blocks = [pair.values(block, head) for block in range(4)]
        for query in range(2):
            first = (query * heads + head) * size
            total = None
            for index in range(3):
                probs = probs_ref[first:first + size, index * size:(index + 1) * size]
                term = dot(probs, blocks[query + index])
                total = term if total is None else total + term
            hidden_ref[query * size:(query + 1) * size, span] = total.astype(BF)
    even_rows, odd_rows = hidden_ref[0:size, :], hidden_ref[size:2 * size, :]
    targets = [pair.integers(2 + query, 1).astype(jnp.int32) for query in range(2)]
    write_messages(
        plan,
        [targets[part // plan.half_parts] for part in range(plan.fold)],
        split_columns(plan, even_rows) + split_columns(plan, odd_rows),
        message_ref,
    )


def act_kernel(
    plan, message_ref, down_hbm, gate_hbm, up_hbm, act_ref, gate_ref, up_ref,
    down_ref, rows_ref, down_sem, gate_sem, up_sem,
):
    copies = [
        pltpu.make_async_copy(
            down_hbm.at[pl.ds(start, size)], down_ref.at[pl.ds(start, size)], down_sem.at[index]
        )
        for index, (_, start, size) in enumerate(plan.cuts)
    ]
    gate_copy = pltpu.make_async_copy(gate_hbm, gate_ref, gate_sem)
    up_copy = pltpu.make_async_copy(up_hbm, up_ref, up_sem)
    for copy in copies:
        copy.start()
    gate_copy.start()
    up_copy.start()
    read_expert_rows(plan, message_ref, rows_ref)
    for copy, (expert, start, size) in zip(copies, plan.cuts):
        copy.wait()
        rows = rows_ref[expert * plan.expert_rows:(expert + 1) * plan.expert_rows, :]
        act_ref[:, start:start + size] = dot_nt(rows, down_ref[start:start + size, :])
    gate_copy.wait()
    up_copy.wait()


def expert_kernel(
    plan, message_ref, gain_ref, act_ref, gate_ref, up_ref, out_ref,
    held_ref, rows_ref, grad_gate_ref, grad_up_ref, sum_ref,
):
    read_hidden_rows(plan, message_ref, gain_ref, held_ref, rows_ref)
    grad_gate_ref[...] = jnp.zeros_like(grad_gate_ref)
    grad_up_ref[...] = jnp.zeros_like(grad_up_ref)
    for expert, start, size in plan.cuts:
        span = slice(start, start + size)
        own = slice(expert * plan.expert_rows, (expert + 1) * plan.expert_rows)
        rows, act = rows_ref[own, :], act_ref[:, span]
        gate_pre, up_pre = dot(rows, gate_ref[:, span]), dot(rows, up_ref[:, span])
        sig = jax.nn.sigmoid(gate_pre)
        grad_gate = act * up_pre * (sig * (1.0 + gate_pre * (1.0 - sig)))
        grad_gate_ref[own, span] = grad_gate.astype(BF)
        grad_up_ref[own, span] = (act * (gate_pre * sig)).astype(BF)
    for start in range(0, plan.model, CUT):
        span = slice(start, start + CUT)
        total = dot_nt(gate_ref[span, :], grad_gate_ref[...])
        total = total + dot_nt(up_ref[span, :], grad_up_ref[...])
        sum_ref[span, :] = total.astype(BF)
    write_expert_rows(plan, norm_backward(plan, sum_ref, held_ref, gain_ref), out_ref)


def finish_kernel(plan, target_ref, grad_ref, message_ref, out_ref):
    target = to_column(target_ref[...].astype(F32))[:, 0:1].astype(jnp.int32)
    parts = [None] * plan.fold
    for chunk in range(plan.chunks):
        wanted, piece = message_slot(plan, chunk, (plan.stretch, CHUNK), 1)
        messages = message_ref[chunk * CHUNK:(chunk + 1) * CHUNK, :]
        for part in range(plan.fold):
            pick = jnp.where((wanted == target) & (piece == part), 1.0, 0.0).astype(BF)
            term = dot(pick, messages)
            parts[part] = term if parts[part] is None else parts[part] + term
    for part, term in enumerate(parts):
        span = slice(part * plan.width, (part + 1) * plan.width)
        out_ref[:, span] = (grad_ref[:, span].astype(F32) + term).astype(BF)


def params(limit):
    return pltpu.CompilerParams(vmem_limit_bytes=limit)


def in_hbm(value):
    return pltpu.with_memory_space_constraint(value, pltpu.HBM)


def shards(
    queries, keys, values, doc_ids, routes, route_weight, norm_gain, w_gate, w_up, w_down, grad_out
):
    stretch, model = queries.shape[1:]
    ctx_count = lax.axis_size("ctx")
    axes = ("ctx", "ep")
    ep_count = lax.axis_size("ep")
    plan = Plan(ctx_count * ep_count, ep_count, w_gate.shape[1], model, stretch)
    messages = jax.ShapeDtypeStruct((plan.total, plan.width), BF)
    message_bytes = 2 * plan.total * plan.width
    gain = norm_gain.reshape(1, model)

    def exchange(value):
        cut = value.reshape(plan.devices, plan.rows, plan.width)
        cut = lax.all_to_all(cut, axes, split_axis=0, concat_axis=0, tiled=True)
        return cut.reshape(plan.total, plan.width)

    two_up = [(source, source + 2) for source in range(ctx_count - 2)]
    next_pair = [(source, (source ^ 1) + 2) for source in range(ctx_count - 2)]
    pairs = [(source, source ^ 1) for source in range(ctx_count)]

    def send(value, route):
        return lax.ppermute(value, "ctx", route)

    inside = pl.BlockSpec(memory_space=pltpu.VMEM)
    outside = pl.BlockSpec(memory_space=pltpu.HBM)
    block = jax.ShapeDtypeStruct((plan.block_rows, PIECE), BF)
    half = jax.ShapeDtypeStruct((stretch, plan.half), BF)
    grad_messages, target = pl.pallas_call(
        functools.partial(grads_kernel, plan),
        in_specs=[outside] * 3,
        out_shape=(messages, jax.ShapeDtypeStruct((1, stretch), jnp.int32)),
        scratch_shapes=[
            pltpu.VMEM((1, stretch), jnp.int32),
            pltpu.VMEM((1, stretch), F32),
            pltpu.VMEM((stretch, model), BF),
            pltpu.SemaphoreType.DMA((3,)),
        ],
        compiler_params=params(8 * MB + 3 * message_bytes),
        name="route_grads",
    )(
        in_hbm(routes.reshape(1, stretch)), in_hbm(route_weight.reshape(1, stretch)),
        in_hbm(grad_out[0]),
    )
    got_grads = exchange(grad_messages)
    mine, other, q_mine, q_other = pl.pallas_call(
        functools.partial(pack_kernel, plan),
        in_specs=[inside] + [outside] * 4,
        out_shape=(block, block, half, half),
        scratch_shapes=[
            pltpu.VMEM((1, stretch), jnp.int32),
            pltpu.SemaphoreType.DMA((4 * plan.pieces + 3,)),
        ],
        compiler_params=params(8 * MB),
        name="pack",
    )(target, *map(in_hbm, (doc_ids, queries[0], keys[0], values[0])))
    far, cross = send(mine, two_up), send(other, next_pair)
    pair, q_pair = send(other, pairs), send(q_other, pairs)

    rows = plan.local * plan.expert_rows
    weight_bytes = 2 * plan.columns * model
    act, gate, up = pl.pallas_call(
        functools.partial(act_kernel, plan),
        in_specs=[inside, outside, outside, outside],
        out_specs=[inside, inside, inside],
        out_shape=(
            jax.ShapeDtypeStruct((plan.expert_rows, plan.columns), F32),
            pltpu.VMEM(w_gate.shape, BF),
            pltpu.VMEM(w_up.shape, BF),
        ),
        scratch_shapes=[
            pltpu.VMEM(w_down.shape, BF),
            pltpu.VMEM((rows, model), BF),
            pltpu.SemaphoreType.DMA((len(plan.cuts),)),
            pltpu.SemaphoreType.DMA,
            pltpu.SemaphoreType.DMA,
        ],
        compiler_params=params(8 * MB + 6 * message_bytes + weight_bytes),
        cost_estimate=pl.CostEstimate(
            flops=2 * plan.expert_rows * plan.columns * model,
            bytes_accessed=3 * weight_bytes,
            transcendentals=0,
        ),
        name="grad_act",
    )(got_grads, in_hbm(w_down), in_hbm(w_gate), in_hbm(w_up))
    far, cross, pair, q_pair, act = lax.optimization_barrier((far, cross, pair, q_pair, act))

    probs = pl.pallas_call(
        functools.partial(softmax_kernel, plan),
        out_shape=jax.ShapeDtypeStruct((HEADS * stretch, (REACH + 1) * stretch), BF),
        compiler_params=params(16 * MB),
        name="softmax",
    )(q_mine, q_pair, mine, pair, far, cross)
    hidden_messages = pl.pallas_call(
        functools.partial(hidden_kernel, plan),
        out_shape=messages,
        scratch_shapes=[pltpu.VMEM((2 * stretch, plan.half), BF)],
        compiler_params=params(12 * MB + 3 * message_bytes),
        name="hidden",
    )(probs, mine, pair, far, cross)
    got_hidden = exchange(hidden_messages)

    returned = pl.pallas_call(
        functools.partial(expert_kernel, plan),
        out_shape=messages,
        scratch_shapes=[
            pltpu.VMEM((rows, model), F32),
            pltpu.VMEM((rows, model), BF),
            pltpu.VMEM((rows, plan.columns), BF),
            pltpu.VMEM((rows, plan.columns), BF),
            pltpu.VMEM((model, rows), BF),
        ],
        compiler_params=params(12 * MB + 8 * message_bytes),
        cost_estimate=pl.CostEstimate(
            flops=8 * plan.expert_rows * plan.columns * model,
            bytes_accessed=2 * weight_bytes,
            transcendentals=0,
        ),
        name="experts",
    )(got_hidden, gain, act, gate, up)
    combined = exchange(returned)

    grad_in = pl.pallas_call(
        functools.partial(finish_kernel, plan),
        out_shape=jax.ShapeDtypeStruct((stretch, model), BF),
        compiler_params=params(12 * MB + 3 * message_bytes),
        name="finish",
    )(target, grad_out[0], combined)
    return grad_in[None]


def solution(mesh):
    in_specs = (
        P("ep", "ctx", None),
        P("ep", "ctx", None),
        P("ep", "ctx", None),
        P("ep", "ctx"),
        P("ep", "ctx", None),
        P("ep", "ctx", None),
        P(),
        P(None, ("ctx", "ep")),
        P(None, ("ctx", "ep")),
        P(("ctx", "ep"), None),
        P("ep", "ctx", None),
    )
    out_specs = P("ep", "ctx", None)
    return jax.shard_map(shards, mesh=mesh, in_specs=in_specs, out_specs=out_specs, check_vma=False)
```

```python
import functools
import math

import jax
import jax.numpy as jnp
from jax import lax
from jax.experimental import pallas as pl
from jax.experimental.pallas import tpu as pltpu
from jax.sharding import PartitionSpec as P

HEADS = 16
HEAD = 128
EXPERTS = 64
FF = 1408
CAP = 2
REACH = 2
CHUNK = 256
TAG_ROWS = 16
CUT = 1408
TILE = 1024
PIECE = 256
BF = jnp.bfloat16
F32 = jnp.float32
MB = 1024 * 1024


def iota(shape, dim):
    return lax.broadcasted_iota(jnp.int32, shape, dim)


def dot(left, right):
    return jnp.dot(left, right, preferred_element_type=F32)


def dot_nt(left, right):
    return lax.dot_general(left, right, (((1,), (1,)), ((), ())), preferred_element_type=F32)


class Plan:
    def __init__(self, devices, eps, columns, width, stretch):
        self.devices = devices
        self.eps = eps
        self.columns = columns
        self.model = width
        self.stretch = stretch
        self.local = max(1, columns // FF)
        self.sharers = max(1, FF // columns)
        self.slots = self.local * CAP
        self.fold = max(2, 8 // self.slots)
        self.width = width // self.fold
        self.rows = self.slots * self.fold
        self.total = devices * self.rows
        self.chunks = self.total // CHUNK
        self.group = CHUNK // self.rows
        self.expert_rows = devices * CAP
        self.half = width // 2
        self.half_parts = self.fold // 2
        self.pieces = self.half // PIECE
        self.block_rows = 2 * self.pieces * stretch + TAG_ROWS
        own = columns // self.local
        self.cuts = [
            (expert, expert * own + start, min(own - start, CUT))
            for expert in range(self.local)
            for start in range(0, own, CUT)
        ]


def message_slot(plan, chunk, shape, dim):
    row = iota(shape, dim)
    device = chunk * plan.group + row // plan.rows
    within = row % plan.rows
    first = device * plan.local if plan.sharers == 1 else device // plan.sharers
    return first * CAP + within % plan.slots, within // plan.slots


def write_messages(plan, targets, values, out_ref):
    shape = (CHUNK, plan.fold * plan.stretch)
    column_part = iota(shape, 1) // plan.stretch
    target = jnp.concatenate(targets, axis=1)
    stacked = jnp.concatenate(values, axis=0)
    for chunk in range(plan.chunks):
        wanted, piece = message_slot(plan, chunk, shape, 0)
        hit = (wanted == target) & (piece == column_part)
        total = dot(jnp.where(hit, 1.0, 0.0).astype(BF), stacked)
        out_ref[chunk * CHUNK:(chunk + 1) * CHUNK, :] = total.astype(BF)


def split_columns(plan, value):
    count = value.shape[1] // plan.width
    return [value[:, part * plan.width:(part + 1) * plan.width] for part in range(count)]


def expert_pick(plan, expert, part, shape, row_dim, message_dim):
    row = iota(shape, row_dim)
    message = iota(shape, message_dim)
    wanted = (row // CAP) * plan.rows + part * plan.slots + expert * CAP + row % CAP
    return jnp.where(wanted == message, 1.0, 0.0).astype(BF)


def read_expert_rows(plan, message_ref, rows_ref):
    count = plan.group * CAP
    for expert in range(plan.local):
        for part in range(plan.fold):
            pick = expert_pick(plan, expert, part, (count, CHUNK), 0, 1)
            for chunk in range(plan.chunks):
                base = expert * plan.expert_rows + chunk * count
                got = dot(pick, message_ref[chunk * CHUNK:(chunk + 1) * CHUNK, :])
                rows_ref[base:base + count, part * plan.width:(part + 1) * plan.width] = got.astype(BF)


def inv_rms(plan, held):
    mean = jnp.sum(held * held, axis=-1, keepdims=True) * (1.0 / plan.model)
    return lax.rsqrt(mean + 1e-06)


def read_hidden_rows(plan, message_ref, gain_ref, held_ref, rows_ref):
    count = plan.group * CAP
    shape = (plan.local * count, CHUNK)
    row, message = iota(shape, 0), iota(shape, 1)
    expert, owner = row // count, row % count // CAP
    parity = (owner // plan.eps) % 2
    for half in range(2):
        source = owner + (half - parity) * plan.eps
        for part in range(plan.half_parts):
            span = slice(half * plan.half + part * plan.width, half * plan.half + (part + 1) * plan.width)
            first = source * plan.rows + (parity * plan.half_parts + part) * plan.slots
            pick = jnp.where(first + expert * CAP + row % CAP == message, 1.0, 0.0).astype(BF)
            for chunk in range(plan.chunks):
                got = dot(pick, message_ref[chunk * CHUNK:(chunk + 1) * CHUNK, :])
                for index in range(plan.local):
                    base = index * plan.expert_rows + chunk * count
                    held_ref[base:base + count, span] = got[index * count:(index + 1) * count]
    held = held_ref[...]
    rows_ref[...] = (held * inv_rms(plan, held) * gain_ref[...]).astype(BF)


def write_expert_rows(plan, rows, message_ref):
    count = plan.local * plan.expert_rows
    shape = (CHUNK, plan.fold * count)
    column = iota(shape, 1)
    part, row = column // count, column % count
    sender = (row % plan.expert_rows) // CAP
    slot = (row // plan.expert_rows) * CAP + row % CAP
    wanted = sender * plan.rows + part * plan.slots + slot
    stacked = jnp.concatenate(split_columns(plan, rows), axis=0)
    for chunk in range(plan.chunks):
        message = iota(shape, 0) + chunk * CHUNK
        total = dot(jnp.where(wanted == message, 1.0, 0.0).astype(BF), stacked)
        message_ref[chunk * CHUNK:(chunk + 1) * CHUNK, :] = total.astype(BF)


def norm_backward(plan, columns_ref, held_ref, gain_ref):
    count = plan.local * plan.expert_rows
    same = iota((count, count), 0) == iota((count, count), 1)
    grads = dot_nt(jnp.where(same, 1.0, 0.0).astype(BF), columns_ref[...])
    gained = grads * gain_ref[...]
    held = held_ref[...]
    inv = inv_rms(plan, held)
    mean = jnp.sum(held * gained, axis=-1, keepdims=True) * (1.0 / plan.model)
    return (inv * gained - held * (inv * inv * inv) * mean).astype(BF)


def to_column(row):
    size = row.shape[1]
    return jnp.transpose(jnp.broadcast_to(row, (size, size)))


def pack_kernel(
    plan, routes_hbm, weight_hbm, grad_hbm, tags_hbm, q_hbm, k_hbm, v_hbm,
    message_ref, target_ref, mine_ref, other_ref, q_mine_ref, q_other_ref,
    routes_ref, weight_ref, grad_ref, tags_ref, sems,
):
    size = plan.stretch
    odd = lax.axis_index("ctx") % 2
    pieces = [
        (routes_hbm, routes_ref), (weight_hbm, weight_ref), (grad_hbm, grad_ref),
        (tags_hbm, tags_ref),
    ]
    for side, block_ref, q_ref in ((1 - odd, other_ref, q_other_ref), (odd, mine_ref, q_mine_ref)):
        base = side * plan.half
        for index, source in enumerate((k_hbm, v_hbm)):
            for piece in range(plan.pieces):
                start = pl.multiple_of(base + piece * PIECE, HEAD)
                row = (index * plan.pieces + piece) * size
                pieces.append((source.at[:, pl.ds(start, PIECE)], block_ref.at[pl.ds(row, size)]))
        span = pl.ds(pl.multiple_of(base, HEAD), plan.half)
        pieces.append((q_hbm.at[:, span], q_ref))
    copies = [
        pltpu.make_async_copy(source, held, sems.at[index])
        for index, (source, held) in enumerate(pieces)
    ]
    for copy in copies:
        copy.start()
    copies[0].wait()
    routes = routes_ref[...].astype(F32)
    earlier = iota((size, size), 0) < iota((size, size), 1)
    same = (to_column(routes) == routes) & earlier
    rank = jnp.sum(jnp.where(same, 1.0, 0.0), axis=0, keepdims=True)
    target = jnp.where(rank < CAP, routes * CAP + rank, -1.0)
    whole_target = target.astype(jnp.int32)
    target_ref[...] = whole_target
    copies[1].wait()
    weight = to_column(weight_ref[...])[:, 0:1]
    copies[2].wait()
    grads = (weight * grad_ref[...].astype(F32)).astype(BF)
    write_messages(plan, [whole_target] * plan.fold, split_columns(plan, grads), message_ref)
    copies[3].wait()
    tags = tags_ref[...].astype(F32) + 1.0
    row = iota((TAG_ROWS, size), 0)
    block = jnp.where(row == 0, tags, jnp.where(row == 1, target, 0.0)).astype(BF)
    first = plan.block_rows - TAG_ROWS
    for ref in (mine_ref, other_ref):
        ref[first:, :] = jnp.zeros((TAG_ROWS, PIECE), BF)
        ref[first:, 0:size] = block
    for copy in copies[4:]:
        copy.wait()


class Pair:
    def __init__(self, plan, mine_ref, pair_ref, far_ref, cross_ref):
        self.plan = plan
        self.odd = lax.axis_index("ctx") % 2 == 1
        self.refs = (
            (cross_ref, far_ref), (far_ref, cross_ref), (pair_ref, mine_ref), (mine_ref, pair_ref)
        )

    def choose(self, if_odd, if_even):
        return jnp.where(self.odd, if_odd, if_even)

    def part(self, block, rows, span):
        if_odd, if_even = self.refs[block]
        return self.choose(if_odd[rows, span], if_even[rows, span])

    def head(self, block, piece, lane):
        first = piece * self.plan.stretch
        rows = slice(first, first + self.plan.stretch)
        return self.part(block, rows, slice(lane, lane + HEAD))

    def keys(self, block, head):
        return self.head(block, head * HEAD // PIECE, head * HEAD % PIECE)

    def values(self, block, head):
        return self.head(block, self.plan.pieces + head * HEAD // PIECE, head * HEAD % PIECE)

    def integers(self, block, row):
        rows = slice(self.plan.block_rows - TAG_ROWS, self.plan.block_rows)
        return self.part(block, rows, slice(0, self.plan.stretch)).astype(F32)[row:row + 1]


def softmax_kernel(
    plan, q_mine_ref, q_pair_ref, mine_ref, pair_ref, far_ref, cross_ref, probs_ref
):
    size = plan.stretch
    pair = Pair(plan, mine_ref, pair_ref, far_ref, cross_ref)
    tags = [pair.integers(block, 0) for block in range(4)]
    causal = iota((size, size), 1) <= iota((size, size), 0)
    masks = []
    for query in range(2):
        column = to_column(tags[2 + query])
        masks.append([column == tags[query + block] for block in range(3)])
        masks[query][2] = masks[query][2] & causal
    heads = plan.half // HEAD
    for head in range(heads):
        span = slice(head * HEAD, (head + 1) * HEAD)
        q_mine, q_pair = q_mine_ref[:, span], q_pair_ref[:, span]
        queries = (pair.choose(q_pair, q_mine), pair.choose(q_mine, q_pair))
        blocks = [pair.keys(block, head) for block in range(4)]
        for query in range(2):
            scores = [
                jnp.where(
                    masks[query][block],
                    dot_nt(queries[query], blocks[query + block]) * (1.0 / math.sqrt(HEAD)),
                    -1e30,
                )
                for block in range(3)
            ]
            top = jnp.max(
                jnp.maximum(jnp.maximum(scores[0], scores[1]), scores[2]), axis=-1, keepdims=True
            )
            weights = [jnp.exp(score - top) for score in scores]
            norm = jnp.sum(weights[0] + weights[1] + weights[2], axis=-1, keepdims=True)
            first = (query * heads + head) * size
            for index, weight in enumerate(weights):
                probs_ref[first:first + size, index * size:(index + 1) * size] = (
                    weight / norm
                ).astype(BF)


def hidden_kernel(
    plan, probs_ref, mine_ref, pair_ref, far_ref, cross_ref, message_ref, hidden_ref
):
    size = plan.stretch
    pair = Pair(plan, mine_ref, pair_ref, far_ref, cross_ref)
    heads = plan.half // HEAD
    for head in range(heads):
        span = slice(head * HEAD, (head + 1) * HEAD)
        blocks = [pair.values(block, head) for block in range(4)]
        for query in range(2):
            first = (query * heads + head) * size
            total = None
            for index in range(3):
                probs = probs_ref[first:first + size, index * size:(index + 1) * size]
                term = dot(probs, blocks[query + index])
                total = term if total is None else total + term
            hidden_ref[query * size:(query + 1) * size, span] = total.astype(BF)
    even_rows, odd_rows = hidden_ref[0:size, :], hidden_ref[size:2 * size, :]
    targets = [pair.integers(2 + query, 1).astype(jnp.int32) for query in range(2)]
    write_messages(
        plan,
        [targets[part // plan.half_parts] for part in range(plan.fold)],
        split_columns(plan, even_rows) + split_columns(plan, odd_rows),
        message_ref,
    )


def act_kernel(
    plan, message_ref, down_hbm, gate_hbm, up_hbm, act_ref, gate_ref, up_ref,
    down_ref, rows_ref, down_sem, gate_sem, up_sem,
):
    copies = [
        pltpu.make_async_copy(
            down_hbm.at[pl.ds(start, size)], down_ref.at[pl.ds(start, size)], down_sem.at[index]
        )
        for index, (_, start, size) in enumerate(plan.cuts)
    ]
    gate_copy = pltpu.make_async_copy(gate_hbm, gate_ref, gate_sem)
    up_copy = pltpu.make_async_copy(up_hbm, up_ref, up_sem)
    for copy in copies:
        copy.start()
    gate_copy.start()
    up_copy.start()
    read_expert_rows(plan, message_ref, rows_ref)
    for copy, (expert, start, size) in zip(copies, plan.cuts):
        copy.wait()
        rows = rows_ref[expert * plan.expert_rows:(expert + 1) * plan.expert_rows, :]
        act_ref[:, start:start + size] = dot_nt(rows, down_ref[start:start + size, :])
    gate_copy.wait()
    up_copy.wait()


def expert_kernel(
    plan, message_ref, gain_ref, act_ref, gate_ref, up_ref, out_ref,
    held_ref, rows_ref, grad_gate_ref, grad_up_ref, sum_ref,
):
    read_hidden_rows(plan, message_ref, gain_ref, held_ref, rows_ref)
    grad_gate_ref[...] = jnp.zeros_like(grad_gate_ref)
    grad_up_ref[...] = jnp.zeros_like(grad_up_ref)
    for expert, start, size in plan.cuts:
        span = slice(start, start + size)
        own = slice(expert * plan.expert_rows, (expert + 1) * plan.expert_rows)
        rows, act = rows_ref[own, :], act_ref[:, span]
        gate_pre, up_pre = dot(rows, gate_ref[:, span]), dot(rows, up_ref[:, span])
        sig = jax.nn.sigmoid(gate_pre)
        grad_gate = act * up_pre * (sig * (1.0 + gate_pre * (1.0 - sig)))
        grad_gate_ref[own, span] = grad_gate.astype(BF)
        grad_up_ref[own, span] = (act * (gate_pre * sig)).astype(BF)
    for start in range(0, plan.model, TILE):
        span = slice(start, start + TILE)
        total = dot_nt(gate_ref[span, :], grad_gate_ref[...])
        total = total + dot_nt(up_ref[span, :], grad_up_ref[...])
        sum_ref[span, :] = total.astype(BF)
    write_expert_rows(plan, norm_backward(plan, sum_ref, held_ref, gain_ref), out_ref)


def finish_kernel(plan, target_ref, grad_ref, message_ref, out_ref):
    target = to_column(target_ref[...].astype(F32))[:, 0:1].astype(jnp.int32)
    parts = [None] * plan.fold
    for chunk in range(plan.chunks):
        wanted, piece = message_slot(plan, chunk, (plan.stretch, CHUNK), 1)
        messages = message_ref[chunk * CHUNK:(chunk + 1) * CHUNK, :]
        for part in range(plan.fold):
            pick = jnp.where((wanted == target) & (piece == part), 1.0, 0.0).astype(BF)
            term = dot(pick, messages)
            parts[part] = term if parts[part] is None else parts[part] + term
    for part, term in enumerate(parts):
        span = slice(part * plan.width, (part + 1) * plan.width)
        out_ref[:, span] = (grad_ref[:, span].astype(F32) + term).astype(BF)


def params(limit):
    return pltpu.CompilerParams(vmem_limit_bytes=limit)


def in_hbm(value):
    return pltpu.with_memory_space_constraint(value, pltpu.HBM)


def shards(
    queries, keys, values, doc_ids, routes, route_weight, norm_gain, w_gate, w_up, w_down, grad_out
):
    stretch, model = queries.shape[1:]
    ctx_count = lax.axis_size("ctx")
    axes = ("ctx", "ep")
    ep_count = lax.axis_size("ep")
    plan = Plan(ctx_count * ep_count, ep_count, w_gate.shape[1], model, stretch)
    messages = jax.ShapeDtypeStruct((plan.total, plan.width), BF)
    message_bytes = 2 * plan.total * plan.width
    gain = norm_gain.reshape(1, model)

    def exchange(value):
        cut = value.reshape(plan.devices, plan.rows, plan.width)
        cut = lax.all_to_all(cut, axes, split_axis=0, concat_axis=0, tiled=True)
        return cut.reshape(plan.total, plan.width)

    two_up = [(source, source + 2) for source in range(ctx_count - 2)]
    next_pair = [(source, (source ^ 1) + 2) for source in range(ctx_count - 2)]
    pairs = [(source, source ^ 1) for source in range(ctx_count)]

    def send(value, route):
        return lax.ppermute(value, "ctx", route)

    inside = pl.BlockSpec(memory_space=pltpu.VMEM)
    outside = pl.BlockSpec(memory_space=pltpu.HBM)
    block = jax.ShapeDtypeStruct((plan.block_rows, PIECE), BF)
    half = jax.ShapeDtypeStruct((stretch, plan.half), BF)
    row = jax.ShapeDtypeStruct((1, stretch), jnp.int32)
    grad_messages, target, mine, other, q_mine, q_other = pl.pallas_call(
        functools.partial(pack_kernel, plan),
        in_specs=[outside] * 7,
        out_shape=(messages, row, block, block, half, half),
        scratch_shapes=[
            pltpu.VMEM((1, stretch), jnp.int32),
            pltpu.VMEM((1, stretch), F32),
            pltpu.VMEM((stretch, model), BF),
            pltpu.VMEM((1, stretch), jnp.int32),
            pltpu.SemaphoreType.DMA((4 * plan.pieces + 6,)),
        ],
        compiler_params=params(12 * MB + 3 * message_bytes),
        name="pack",
    )(
        *map(
            in_hbm,
            (
                routes.reshape(1, stretch), route_weight.reshape(1, stretch), grad_out[0],
                doc_ids, queries[0], keys[0], values[0],
            ),
        )
    )
    got_grads = exchange(grad_messages)
    far, cross = send(mine, two_up), send(other, next_pair)
    pair, q_pair = send(other, pairs), send(q_other, pairs)

    rows = plan.local * plan.expert_rows
    weight_bytes = 2 * plan.columns * model
    act, gate, up = pl.pallas_call(
        functools.partial(act_kernel, plan),
        in_specs=[inside, outside, outside, outside],
        out_specs=[inside, inside, inside],
        out_shape=(
            jax.ShapeDtypeStruct((plan.expert_rows, plan.columns), F32),
            pltpu.VMEM(w_gate.shape, BF),
            pltpu.VMEM(w_up.shape, BF),
        ),
        scratch_shapes=[
            pltpu.VMEM(w_down.shape, BF),
            pltpu.VMEM((rows, model), BF),
            pltpu.SemaphoreType.DMA((len(plan.cuts),)),
            pltpu.SemaphoreType.DMA,
            pltpu.SemaphoreType.DMA,
        ],
        compiler_params=params(8 * MB + 6 * message_bytes + weight_bytes),
        cost_estimate=pl.CostEstimate(
            flops=2 * plan.expert_rows * plan.columns * model,
            bytes_accessed=3 * weight_bytes,
            transcendentals=0,
        ),
        name="grad_act",
    )(got_grads, in_hbm(w_down), in_hbm(w_gate), in_hbm(w_up))
    far, cross, pair, q_pair, act = lax.optimization_barrier((far, cross, pair, q_pair, act))

    probs = pl.pallas_call(
        functools.partial(softmax_kernel, plan),
        out_shape=jax.ShapeDtypeStruct((HEADS * stretch, (REACH + 1) * stretch), BF),
        compiler_params=params(16 * MB),
        name="softmax",
    )(q_mine, q_pair, mine, pair, far, cross)
    hidden_messages = pl.pallas_call(
        functools.partial(hidden_kernel, plan),
        out_shape=messages,
        scratch_shapes=[pltpu.VMEM((2 * stretch, plan.half), BF)],
        compiler_params=params(12 * MB + 3 * message_bytes),
        name="hidden",
    )(probs, mine, pair, far, cross)
    got_hidden = exchange(hidden_messages)

    returned = pl.pallas_call(
        functools.partial(expert_kernel, plan),
        out_shape=messages,
        scratch_shapes=[
            pltpu.VMEM((rows, model), F32),
            pltpu.VMEM((rows, model), BF),
            pltpu.VMEM((rows, plan.columns), BF),
            pltpu.VMEM((rows, plan.columns), BF),
            pltpu.VMEM((model, rows), BF),
        ],
        compiler_params=params(12 * MB + 8 * message_bytes),
        cost_estimate=pl.CostEstimate(
            flops=8 * plan.expert_rows * plan.columns * model,
            bytes_accessed=2 * weight_bytes,
            transcendentals=0,
        ),
        name="experts",
    )(got_hidden, gain, act, gate, up)
    combined = exchange(returned)

    grad_in = pl.pallas_call(
        functools.partial(finish_kernel, plan),
        out_shape=jax.ShapeDtypeStruct((stretch, model), BF),
        compiler_params=params(12 * MB + 3 * message_bytes),
        name="finish",
    )(target, grad_out[0], combined)
    return grad_in[None]


def solution(mesh):
    in_specs = (
        P("ep", "ctx", None),
        P("ep", "ctx", None),
        P("ep", "ctx", None),
        P("ep", "ctx"),
        P("ep", "ctx", None),
        P("ep", "ctx", None),
        P(),
        P(None, ("ctx", "ep")),
        P(None, ("ctx", "ep")),
        P(("ctx", "ep"), None),
        P("ep", "ctx", None),
    )
    out_specs = P("ep", "ctx", None)
    return jax.shard_map(shards, mesh=mesh, in_specs=in_specs, out_specs=out_specs, check_vma=False)
```

```python
import functools
import math

import jax
import jax.numpy as jnp
from jax import lax
from jax.experimental import pallas as pl
from jax.experimental.pallas import tpu as pltpu
from jax.sharding import PartitionSpec as P

HEADS = 16
HEAD = 128
EXPERTS = 64
FF = 1408
CAP = 2
REACH = 2
CHUNK = 256
TAG_ROWS = 16
CUT = 512
PIECE = 256
BF = jnp.bfloat16
F32 = jnp.float32
MB = 1024 * 1024


def iota(shape, dim):
    return lax.broadcasted_iota(jnp.int32, shape, dim)


def dot(left, right):
    return jnp.dot(left, right, preferred_element_type=F32)


def dot_nt(left, right):
    return lax.dot_general(left, right, (((1,), (1,)), ((), ())), preferred_element_type=F32)


class Plan:
    def __init__(self, devices, eps, columns, width, stretch):
        self.devices = devices
        self.eps = eps
        self.columns = columns
        self.model = width
        self.stretch = stretch
        self.local = max(1, columns // FF)
        self.sharers = max(1, FF // columns)
        self.slots = self.local * CAP
        self.fold = max(2, 8 // self.slots)
        self.width = width // self.fold
        self.rows = self.slots * self.fold
        self.total = devices * self.rows
        self.chunks = self.total // CHUNK
        self.group = CHUNK // self.rows
        self.expert_rows = devices * CAP
        self.half = width // 2
        self.half_parts = self.fold // 2
        self.pieces = self.half // PIECE
        self.block_rows = 2 * self.pieces * stretch + TAG_ROWS
        own = columns // self.local
        self.cuts = [
            (expert, expert * own + start, min(own - start, CUT))
            for expert in range(self.local)
            for start in range(0, own, CUT)
        ]


def message_slot(plan, chunk, shape, dim):
    row = iota(shape, dim)
    place = chunk * plan.group + row // plan.rows
    contexts = plan.devices // plan.eps
    device = place % contexts * plan.eps + place // contexts
    within = row % plan.rows
    first = device * plan.local if plan.sharers == 1 else device // plan.sharers
    return first * CAP + within % plan.slots, within // plan.slots


def write_messages(plan, targets, values, out_ref):
    shape = (CHUNK, plan.fold * plan.stretch)
    column_part = iota(shape, 1) // plan.stretch
    target = jnp.concatenate(targets, axis=1)
    stacked = jnp.concatenate(values, axis=0)
    for chunk in range(plan.chunks):
        wanted, piece = message_slot(plan, chunk, shape, 0)
        hit = (wanted == target) & (piece == column_part)
        total = dot(jnp.where(hit, 1.0, 0.0).astype(BF), stacked)
        out_ref[chunk * CHUNK:(chunk + 1) * CHUNK, :] = total.astype(BF)


def split_columns(plan, value):
    count = value.shape[1] // plan.width
    return [value[:, part * plan.width:(part + 1) * plan.width] for part in range(count)]


def expert_pick(plan, expert, part, shape, row_dim, message_dim):
    row = iota(shape, row_dim)
    message = iota(shape, message_dim)
    wanted = (row // CAP) * plan.rows + part * plan.slots + expert * CAP + row % CAP
    return jnp.where(wanted == message, 1.0, 0.0).astype(BF)


def read_expert_rows(plan, message_ref, rows_ref):
    count = plan.group * CAP
    for expert in range(plan.local):
        for part in range(plan.fold):
            pick = expert_pick(plan, expert, part, (count, CHUNK), 0, 1)
            for chunk in range(plan.chunks):
                base = expert * plan.expert_rows + chunk * count
                got = dot(pick, message_ref[chunk * CHUNK:(chunk + 1) * CHUNK, :])
                rows_ref[base:base + count, part * plan.width:(part + 1) * plan.width] = got.astype(BF)


def inv_rms(plan, held):
    mean = jnp.sum(held * held, axis=-1, keepdims=True) * (1.0 / plan.model)
    return lax.rsqrt(mean + 1e-06)


def read_hidden_rows(plan, message_ref, gain_ref, held_ref, rows_ref):
    count = plan.group * CAP
    shape = (plan.local * count, CHUNK)
    row, message = iota(shape, 0), iota(shape, 1)
    expert, owner = row // count, row % count // CAP
    parity = owner % 2
    for half in range(2):
        source = owner + half - parity
        for part in range(plan.half_parts):
            span = slice(half * plan.half + part * plan.width, half * plan.half + (part + 1) * plan.width)
            first = source * plan.rows + (parity * plan.half_parts + part) * plan.slots
            pick = jnp.where(first + expert * CAP + row % CAP == message, 1.0, 0.0).astype(BF)
            for chunk in range(plan.chunks):
                got = dot(pick, message_ref[chunk * CHUNK:(chunk + 1) * CHUNK, :])
                for index in range(plan.local):
                    base = index * plan.expert_rows + chunk * count
                    held_ref[base:base + count, span] = got[index * count:(index + 1) * count]
    held = held_ref[...]
    rows_ref[...] = (held * inv_rms(plan, held) * gain_ref[...]).astype(BF)


def write_expert_rows(plan, rows, message_ref):
    count = plan.local * plan.expert_rows
    shape = (CHUNK, plan.fold * count)
    column = iota(shape, 1)
    part, row = column // count, column % count
    sender = (row % plan.expert_rows) // CAP
    slot = (row // plan.expert_rows) * CAP + row % CAP
    wanted = sender * plan.rows + part * plan.slots + slot
    stacked = jnp.concatenate(split_columns(plan, rows), axis=0)
    for chunk in range(plan.chunks):
        message = iota(shape, 0) + chunk * CHUNK
        total = dot(jnp.where(wanted == message, 1.0, 0.0).astype(BF), stacked)
        message_ref[chunk * CHUNK:(chunk + 1) * CHUNK, :] = total.astype(BF)


def norm_backward(plan, columns_ref, held_ref, gain_ref):
    count = plan.local * plan.expert_rows
    same = iota((count, count), 0) == iota((count, count), 1)
    grads = dot_nt(jnp.where(same, 1.0, 0.0).astype(BF), columns_ref[...])
    gained = grads * gain_ref[...]
    held = held_ref[...]
    inv = inv_rms(plan, held)
    mean = jnp.sum(held * gained, axis=-1, keepdims=True) * (1.0 / plan.model)
    return (inv * gained - held * (inv * inv * inv) * mean).astype(BF)


def to_column(row):
    size = row.shape[1]
    return jnp.transpose(jnp.broadcast_to(row, (size, size)))


def grads_kernel(
    plan, routes_hbm, weight_hbm, grad_hbm, message_ref, target_ref,
    routes_ref, weight_ref, grad_ref, sems,
):
    size = plan.stretch
    pieces = ((routes_hbm, routes_ref), (weight_hbm, weight_ref), (grad_hbm, grad_ref))
    copies = [
        pltpu.make_async_copy(source, held, sems.at[index])
        for index, (source, held) in enumerate(pieces)
    ]
    for copy in copies:
        copy.start()
    copies[0].wait()
    routes = routes_ref[...].astype(F32)
    earlier = iota((size, size), 0) < iota((size, size), 1)
    same = (to_column(routes) == routes) & earlier
    rank = jnp.sum(jnp.where(same, 1.0, 0.0), axis=0, keepdims=True)
    target = jnp.where(rank < CAP, routes * CAP + rank, -1.0).astype(jnp.int32)
    target_ref[...] = target
    copies[1].wait()
    weight = to_column(weight_ref[...])[:, 0:1]
    copies[2].wait()
    grads = (weight * grad_ref[...].astype(F32)).astype(BF)
    write_messages(plan, [target] * plan.fold, split_columns(plan, grads), message_ref)


def pack_kernel(
    plan, target_ref, tags_hbm, q_hbm, k_hbm, v_hbm,
    mine_ref, other_ref, q_mine_ref, q_other_ref, tags_ref, sems,
):
    size = plan.stretch
    odd = lax.axis_index("ctx") % 2
    pieces = [(tags_hbm, tags_ref)]
    for side, block_ref, q_ref in ((1 - odd, other_ref, q_other_ref), (odd, mine_ref, q_mine_ref)):
        base = side * plan.half
        for index, source in enumerate((k_hbm, v_hbm)):
            for piece in range(plan.pieces):
                start = pl.multiple_of(base + piece * PIECE, HEAD)
                row = (index * plan.pieces + piece) * size
                pieces.append((source.at[:, pl.ds(start, PIECE)], block_ref.at[pl.ds(row, size)]))
        span = pl.ds(pl.multiple_of(base, HEAD), plan.half)
        pieces.append((q_hbm.at[:, span], q_ref))
    copies = [
        pltpu.make_async_copy(source, held, sems.at[index])
        for index, (source, held) in enumerate(pieces)
    ]
    for copy in copies:
        copy.start()
    copies[0].wait()
    tags = tags_ref[...].astype(F32) + 1.0
    row = iota((TAG_ROWS, size), 0)
    target = target_ref[...].astype(F32)
    block = jnp.where(row == 0, tags, jnp.where(row == 1, target, 0.0)).astype(BF)
    first = plan.block_rows - TAG_ROWS
    for ref in (mine_ref, other_ref):
        ref[first:, :] = jnp.zeros((TAG_ROWS, PIECE), BF)
        ref[first:, 0:size] = block
    for copy in copies[1:]:
        copy.wait()


class Pair:
    def __init__(self, plan, mine_ref, pair_ref, far_ref, cross_ref):
        self.plan = plan
        self.odd = lax.axis_index("ctx") % 2 == 1
        self.refs = (
            (cross_ref, far_ref), (far_ref, cross_ref), (pair_ref, mine_ref), (mine_ref, pair_ref)
        )

    def choose(self, if_odd, if_even):
        return jnp.where(self.odd, if_odd, if_even)

    def part(self, block, rows, span):
        if_odd, if_even = self.refs[block]
        return self.choose(if_odd[rows, span], if_even[rows, span])

    def head(self, block, piece, lane):
        first = piece * self.plan.stretch
        rows = slice(first, first + self.plan.stretch)
        return self.part(block, rows, slice(lane, lane + HEAD))

    def keys(self, block, head):
        return self.head(block, head * HEAD // PIECE, head * HEAD % PIECE)

    def values(self, block, head):
        return self.head(block, self.plan.pieces + head * HEAD // PIECE, head * HEAD % PIECE)

    def integers(self, block, row):
        rows = slice(self.plan.block_rows - TAG_ROWS, self.plan.block_rows)
        return self.part(block, rows, slice(0, self.plan.stretch)).astype(F32)[row:row + 1]


def softmax_kernel(
    plan, q_mine_ref, q_pair_ref, mine_ref, pair_ref, far_ref, cross_ref, probs_ref
):
    size = plan.stretch
    pair = Pair(plan, mine_ref, pair_ref, far_ref, cross_ref)
    tags = [pair.integers(block, 0) for block in range(4)]
    causal = iota((size, size), 1) <= iota((size, size), 0)
    masks = []
    for query in range(2):
        column = to_column(tags[2 + query])
        masks.append([column == tags[query + block] for block in range(3)])
        masks[query][2] = masks[query][2] & causal
    heads = plan.half // HEAD
    for head in range(heads):
        span = slice(head * HEAD, (head + 1) * HEAD)
        q_mine, q_pair = q_mine_ref[:, span], q_pair_ref[:, span]
        queries = (pair.choose(q_pair, q_mine), pair.choose(q_mine, q_pair))
        blocks = [pair.keys(block, head) for block in range(4)]
        for query in range(2):
            scores = [
                jnp.where(
                    masks[query][block],
                    dot_nt(queries[query], blocks[query + block]) * (1.0 / math.sqrt(HEAD)),
                    -1e30,
                )
                for block in range(3)
            ]
            top = jnp.max(
                jnp.maximum(jnp.maximum(scores[0], scores[1]), scores[2]), axis=-1, keepdims=True
            )
            weights = [jnp.exp(score - top) for score in scores]
            norm = jnp.sum(weights[0] + weights[1] + weights[2], axis=-1, keepdims=True)
            first = (query * heads + head) * size
            for index, weight in enumerate(weights):
                probs_ref[first:first + size, index * size:(index + 1) * size] = (
                    weight / norm
                ).astype(BF)


def hidden_kernel(
    plan, probs_ref, mine_ref, pair_ref, far_ref, cross_ref, message_ref, hidden_ref
):
    size = plan.stretch
    pair = Pair(plan, mine_ref, pair_ref, far_ref, cross_ref)
    heads = plan.half // HEAD
    for head in range(heads):
        span = slice(head * HEAD, (head + 1) * HEAD)
        blocks = [pair.values(block, head) for block in range(4)]
        for query in range(2):
            first = (query * heads + head) * size
            total = None
            for index in range(3):
                probs = probs_ref[first:first + size, index * size:(index + 1) * size]
                term = dot(probs, blocks[query + index])
                total = term if total is None else total + term
            hidden_ref[query * size:(query + 1) * size, span] = total.astype(BF)
    even_rows, odd_rows = hidden_ref[0:size, :], hidden_ref[size:2 * size, :]
    targets = [pair.integers(2 + query, 1).astype(jnp.int32) for query in range(2)]
    write_messages(
        plan,
        [targets[part // plan.half_parts] for part in range(plan.fold)],
        split_columns(plan, even_rows) + split_columns(plan, odd_rows),
        message_ref,
    )


def act_kernel(
    plan, message_ref, down_hbm, gate_hbm, up_hbm, act_ref, gate_ref, up_ref,
    down_ref, rows_ref, down_sem, gate_sem, up_sem,
):
    copies = [
        pltpu.make_async_copy(
            down_hbm.at[pl.ds(start, size)], down_ref.at[pl.ds(start, size)], down_sem.at[index]
        )
        for index, (_, start, size) in enumerate(plan.cuts)
    ]
    gate_copy = pltpu.make_async_copy(gate_hbm, gate_ref, gate_sem)
    up_copy = pltpu.make_async_copy(up_hbm, up_ref, up_sem)
    for copy in copies:
        copy.start()
    gate_copy.start()
    up_copy.start()
    read_expert_rows(plan, message_ref, rows_ref)
    for copy, (expert, start, size) in zip(copies, plan.cuts):
        copy.wait()
        rows = rows_ref[expert * plan.expert_rows:(expert + 1) * plan.expert_rows, :]
        act_ref[:, start:start + size] = dot_nt(rows, down_ref[start:start + size, :])
    gate_copy.wait()
    up_copy.wait()


def expert_kernel(
    plan, message_ref, gain_ref, act_ref, gate_ref, up_ref, out_ref,
    held_ref, rows_ref, grad_gate_ref, grad_up_ref, sum_ref,
):
    read_hidden_rows(plan, message_ref, gain_ref, held_ref, rows_ref)
    grad_gate_ref[...] = jnp.zeros_like(grad_gate_ref)
    grad_up_ref[...] = jnp.zeros_like(grad_up_ref)
    for expert, start, size in plan.cuts:
        span = slice(start, start + size)
        own = slice(expert * plan.expert_rows, (expert + 1) * plan.expert_rows)
        rows, act = rows_ref[own, :], act_ref[:, span]
        gate_pre, up_pre = dot(rows, gate_ref[:, span]), dot(rows, up_ref[:, span])
        sig = jax.nn.sigmoid(gate_pre)
        grad_gate = act * up_pre * (sig * (1.0 + gate_pre * (1.0 - sig)))
        grad_gate_ref[own, span] = grad_gate.astype(BF)
        grad_up_ref[own, span] = (act * (gate_pre * sig)).astype(BF)
    for start in range(0, plan.model, CUT):
        span = slice(start, start + CUT)
        total = dot_nt(gate_ref[span, :], grad_gate_ref[...])
        total = total + dot_nt(up_ref[span, :], grad_up_ref[...])
        sum_ref[span, :] = total.astype(BF)
    write_expert_rows(plan, norm_backward(plan, sum_ref, held_ref, gain_ref), out_ref)


def finish_kernel(plan, target_ref, grad_ref, message_ref, out_ref):
    target = to_column(target_ref[...].astype(F32))[:, 0:1].astype(jnp.int32)
    parts = [None] * plan.fold
    for chunk in range(plan.chunks):
        wanted, piece = message_slot(plan, chunk, (plan.stretch, CHUNK), 1)
        messages = message_ref[chunk * CHUNK:(chunk + 1) * CHUNK, :]
        for part in range(plan.fold):
            pick = jnp.where((wanted == target) & (piece == part), 1.0, 0.0).astype(BF)
            term = dot(pick, messages)
            parts[part] = term if parts[part] is None else parts[part] + term
    for part, term in enumerate(parts):
        span = slice(part * plan.width, (part + 1) * plan.width)
        out_ref[:, span] = (grad_ref[:, span].astype(F32) + term).astype(BF)


def params(limit):
    return pltpu.CompilerParams(vmem_limit_bytes=limit)


def in_hbm(value):
    return pltpu.with_memory_space_constraint(value, pltpu.HBM)


def shards(
    queries, keys, values, doc_ids, routes, route_weight, norm_gain, w_gate, w_up, w_down, grad_out
):
    stretch, model = queries.shape[1:]
    ctx_count = lax.axis_size("ctx")
    axes = ("ep", "ctx")
    ep_count = lax.axis_size("ep")
    plan = Plan(ctx_count * ep_count, ep_count, w_gate.shape[1], model, stretch)
    messages = jax.ShapeDtypeStruct((plan.total, plan.width), BF)
    message_bytes = 2 * plan.total * plan.width
    gain = norm_gain.reshape(1, model)

    def exchange(value):
        cut = value.reshape(plan.devices, plan.rows, plan.width)
        cut = lax.all_to_all(cut, axes, split_axis=0, concat_axis=0, tiled=True)
        return cut.reshape(plan.total, plan.width)

    two_up = [(source, source + 2) for source in range(ctx_count - 2)]
    next_pair = [(source, (source ^ 1) + 2) for source in range(ctx_count - 2)]
    pairs = [(source, source ^ 1) for source in range(ctx_count)]

    def send(value, route):
        return lax.ppermute(value, "ctx", route)

    inside = pl.BlockSpec(memory_space=pltpu.VMEM)
    outside = pl.BlockSpec(memory_space=pltpu.HBM)
    block = jax.ShapeDtypeStruct((plan.block_rows, PIECE), BF)
    half = jax.ShapeDtypeStruct((stretch, plan.half), BF)
    grad_messages, target = pl.pallas_call(
        functools.partial(grads_kernel, plan),
        in_specs=[outside] * 3,
        out_shape=(messages, jax.ShapeDtypeStruct((1, stretch), jnp.int32)),
        scratch_shapes=[
            pltpu.VMEM((1, stretch), jnp.int32),
            pltpu.VMEM((1, stretch), F32),
            pltpu.VMEM((stretch, model), BF),
            pltpu.SemaphoreType.DMA((3,)),
        ],
        compiler_params=params(8 * MB + 3 * message_bytes),
        name="route_grads",
    )(
        in_hbm(routes.reshape(1, stretch)), in_hbm(route_weight.reshape(1, stretch)),
        in_hbm(grad_out[0]),
    )
    got_grads = exchange(grad_messages)
    mine, other, q_mine, q_other = pl.pallas_call(
        functools.partial(pack_kernel, plan),
        in_specs=[inside] + [outside] * 4,
        out_shape=(block, block, half, half),
        scratch_shapes=[
            pltpu.VMEM((1, stretch), jnp.int32),
            pltpu.SemaphoreType.DMA((4 * plan.pieces + 3,)),
        ],
        compiler_params=params(8 * MB),
        name="pack",
    )(target, *map(in_hbm, (doc_ids, queries[0], keys[0], values[0])))
    far, cross = send(mine, two_up), send(other, next_pair)
    pair, q_pair = send(other, pairs), send(q_other, pairs)

    rows = plan.local * plan.expert_rows
    weight_bytes = 2 * plan.columns * model
    act, gate, up = pl.pallas_call(
        functools.partial(act_kernel, plan),
        in_specs=[inside, outside, outside, outside],
        out_specs=[inside, inside, inside],
        out_shape=(
            jax.ShapeDtypeStruct((plan.expert_rows, plan.columns), F32),
            pltpu.VMEM(w_gate.shape, BF),
            pltpu.VMEM(w_up.shape, BF),
        ),
        scratch_shapes=[
            pltpu.VMEM(w_down.shape, BF),
            pltpu.VMEM((rows, model), BF),
            pltpu.SemaphoreType.DMA((len(plan.cuts),)),
            pltpu.SemaphoreType.DMA,
            pltpu.SemaphoreType.DMA,
        ],
        compiler_params=params(8 * MB + 6 * message_bytes + weight_bytes),
        cost_estimate=pl.CostEstimate(
            flops=2 * plan.expert_rows * plan.columns * model,
            bytes_accessed=3 * weight_bytes,
            transcendentals=0,
        ),
        name="grad_act",
    )(got_grads, in_hbm(w_down), in_hbm(w_gate), in_hbm(w_up))
    far, cross, pair, q_pair, act = lax.optimization_barrier((far, cross, pair, q_pair, act))

    probs = pl.pallas_call(
        functools.partial(softmax_kernel, plan),
        out_shape=jax.ShapeDtypeStruct((HEADS * stretch, (REACH + 1) * stretch), BF),
        compiler_params=params(16 * MB),
        name="softmax",
    )(q_mine, q_pair, mine, pair, far, cross)
    hidden_messages = pl.pallas_call(
        functools.partial(hidden_kernel, plan),
        out_shape=messages,
        scratch_shapes=[pltpu.VMEM((2 * stretch, plan.half), BF)],
        compiler_params=params(12 * MB + 3 * message_bytes),
        name="hidden",
    )(probs, mine, pair, far, cross)
    got_hidden = exchange(hidden_messages)

    returned = pl.pallas_call(
        functools.partial(expert_kernel, plan),
        out_shape=messages,
        scratch_shapes=[
            pltpu.VMEM((rows, model), F32),
            pltpu.VMEM((rows, model), BF),
            pltpu.VMEM((rows, plan.columns), BF),
            pltpu.VMEM((rows, plan.columns), BF),
            pltpu.VMEM((model, rows), BF),
        ],
        compiler_params=params(12 * MB + 8 * message_bytes),
        cost_estimate=pl.CostEstimate(
            flops=8 * plan.expert_rows * plan.columns * model,
            bytes_accessed=2 * weight_bytes,
            transcendentals=0,
        ),
        name="experts",
    )(got_hidden, gain, act, gate, up)
    combined = exchange(returned)

    grad_in = pl.pallas_call(
        functools.partial(finish_kernel, plan),
        out_shape=jax.ShapeDtypeStruct((stretch, model), BF),
        compiler_params=params(12 * MB + 3 * message_bytes),
        name="finish",
    )(target, grad_out[0], combined)
    return grad_in[None]


def solution(mesh):
    in_specs = (
        P("ep", "ctx", None),
        P("ep", "ctx", None),
        P("ep", "ctx", None),
        P("ep", "ctx"),
        P("ep", "ctx", None),
        P("ep", "ctx", None),
        P(),
        P(None, ("ctx", "ep")),
        P(None, ("ctx", "ep")),
        P(("ctx", "ep"), None),
        P("ep", "ctx", None),
    )
    out_specs = P("ep", "ctx", None)
    return jax.shard_map(shards, mesh=mesh, in_specs=in_specs, out_specs=out_specs, check_vma=False)
```

```python
import functools
import math

import jax
import jax.numpy as jnp
from jax import lax
from jax.experimental import pallas as pl
from jax.experimental.pallas import tpu as pltpu
from jax.sharding import PartitionSpec as P

HEADS = 16
HEAD = 128
EXPERTS = 64
FF = 1408
CAP = 2
REACH = 2
CHUNK = 256
TAG_ROWS = 16
CUT = 512
PIECE = 128
BF = jnp.bfloat16
F32 = jnp.float32
MB = 1024 * 1024


def iota(shape, dim):
    return lax.broadcasted_iota(jnp.int32, shape, dim)


def dot(left, right):
    return jnp.dot(left, right, preferred_element_type=F32)


def dot_nt(left, right):
    return lax.dot_general(left, right, (((1,), (1,)), ((), ())), preferred_element_type=F32)


class Plan:
    def __init__(self, devices, eps, columns, width, stretch):
        self.devices = devices
        self.eps = eps
        self.columns = columns
        self.model = width
        self.stretch = stretch
        self.local = max(1, columns // FF)
        self.sharers = max(1, FF // columns)
        self.slots = self.local * CAP
        self.fold = max(2, 8 // self.slots)
        self.width = width // self.fold
        self.rows = self.slots * self.fold
        self.total = devices * self.rows
        self.chunks = self.total // CHUNK
        self.group = CHUNK // self.rows
        self.expert_rows = devices * CAP
        self.half = width // 2
        self.half_parts = self.fold // 2
        self.pieces = self.half // PIECE
        self.block_rows = 2 * self.pieces * stretch + TAG_ROWS
        own = columns // self.local
        self.cuts = [
            (expert, expert * own + start, min(own - start, CUT))
            for expert in range(self.local)
            for start in range(0, own, CUT)
        ]


def message_slot(plan, chunk, shape, dim):
    row = iota(shape, dim)
    device = chunk * plan.group + row // plan.rows
    within = row % plan.rows
    first = device * plan.local if plan.sharers == 1 else device // plan.sharers
    return first * CAP + within % plan.slots, within // plan.slots


def write_messages(plan, targets, values, out_ref):
    shape = (CHUNK, plan.fold * plan.stretch)
    column_part = iota(shape, 1) // plan.stretch
    target = jnp.concatenate(targets, axis=1)
    stacked = jnp.concatenate(values, axis=0)
    for chunk in range(plan.chunks):
        wanted, piece = message_slot(plan, chunk, shape, 0)
        hit = (wanted == target) & (piece == column_part)
        total = dot(jnp.where(hit, 1.0, 0.0).astype(BF), stacked)
        out_ref[chunk * CHUNK:(chunk + 1) * CHUNK, :] = total.astype(BF)


def split_columns(plan, value):
    count = value.shape[1] // plan.width
    return [value[:, part * plan.width:(part + 1) * plan.width] for part in range(count)]


def expert_pick(plan, expert, part, shape, row_dim, message_dim):
    row = iota(shape, row_dim)
    message = iota(shape, message_dim)
    wanted = (row // CAP) * plan.rows + part * plan.slots + expert * CAP + row % CAP
    return jnp.where(wanted == message, 1.0, 0.0).astype(BF)


def read_expert_rows(plan, message_ref, rows_ref):
    count = plan.group * CAP
    for expert in range(plan.local):
        for part in range(plan.fold):
            pick = expert_pick(plan, expert, part, (count, CHUNK), 0, 1)
            for chunk in range(plan.chunks):
                base = expert * plan.expert_rows + chunk * count
                got = dot(pick, message_ref[chunk * CHUNK:(chunk + 1) * CHUNK, :])
                rows_ref[base:base + count, part * plan.width:(part + 1) * plan.width] = got.astype(BF)


def inv_rms(plan, held):
    mean = jnp.sum(held * held, axis=-1, keepdims=True) * (1.0 / plan.model)
    return lax.rsqrt(mean + 1e-06)


def read_hidden_rows(plan, message_ref, gain_ref, held_ref, rows_ref):
    count = plan.group * CAP
    shape = (plan.local * count, CHUNK)
    row, message = iota(shape, 0), iota(shape, 1)
    expert, owner = row // count, row % count // CAP
    parity = (owner // plan.eps) % 2
    for half in range(2):
        source = owner + (half - parity) * plan.eps
        for part in range(plan.half_parts):
            span = slice(half * plan.half + part * plan.width, half * plan.half + (part + 1) * plan.width)
            first = source * plan.rows + (parity * plan.half_parts + part) * plan.slots
            pick = jnp.where(first + expert * CAP + row % CAP == message, 1.0, 0.0).astype(BF)
            for chunk in range(plan.chunks):
                got = dot(pick, message_ref[chunk * CHUNK:(chunk + 1) * CHUNK, :])
                for index in range(plan.local):
                    base = index * plan.expert_rows + chunk * count
                    held_ref[base:base + count, span] = got[index * count:(index + 1) * count]
    held = held_ref[...]
    rows_ref[...] = (held * inv_rms(plan, held) * gain_ref[...]).astype(BF)


def write_expert_rows(plan, rows, message_ref):
    count = plan.local * plan.expert_rows
    shape = (CHUNK, plan.fold * count)
    column = iota(shape, 1)
    part, row = column // count, column % count
    sender = (row % plan.expert_rows) // CAP
    slot = (row // plan.expert_rows) * CAP + row % CAP
    wanted = sender * plan.rows + part * plan.slots + slot
    stacked = jnp.concatenate(split_columns(plan, rows), axis=0)
    for chunk in range(plan.chunks):
        message = iota(shape, 0) + chunk * CHUNK
        total = dot(jnp.where(wanted == message, 1.0, 0.0).astype(BF), stacked)
        message_ref[chunk * CHUNK:(chunk + 1) * CHUNK, :] = total.astype(BF)


def norm_backward(plan, columns_ref, held_ref, gain_ref):
    count = plan.local * plan.expert_rows
    same = iota((count, count), 0) == iota((count, count), 1)
    grads = dot_nt(jnp.where(same, 1.0, 0.0).astype(BF), columns_ref[...])
    gained = grads * gain_ref[...]
    held = held_ref[...]
    inv = inv_rms(plan, held)
    mean = jnp.sum(held * gained, axis=-1, keepdims=True) * (1.0 / plan.model)
    return (inv * gained - held * (inv * inv * inv) * mean).astype(BF)


def to_column(row):
    size = row.shape[1]
    return jnp.transpose(jnp.broadcast_to(row, (size, size)))


def grads_kernel(
    plan, routes_hbm, weight_hbm, grad_hbm, message_ref, target_ref,
    routes_ref, weight_ref, grad_ref, sems,
):
    size = plan.stretch
    pieces = ((routes_hbm, routes_ref), (weight_hbm, weight_ref), (grad_hbm, grad_ref))
    copies = [
        pltpu.make_async_copy(source, held, sems.at[index])
        for index, (source, held) in enumerate(pieces)
    ]
    for copy in copies:
        copy.start()
    copies[0].wait()
    routes = routes_ref[...].astype(F32)
    earlier = iota((size, size), 0) < iota((size, size), 1)
    same = (to_column(routes) == routes) & earlier
    rank = jnp.sum(jnp.where(same, 1.0, 0.0), axis=0, keepdims=True)
    target = jnp.where(rank < CAP, routes * CAP + rank, -1.0).astype(jnp.int32)
    target_ref[...] = target
    copies[1].wait()
    weight = to_column(weight_ref[...])[:, 0:1]
    copies[2].wait()
    grads = (weight * grad_ref[...].astype(F32)).astype(BF)
    write_messages(plan, [target] * plan.fold, split_columns(plan, grads), message_ref)


def pack_kernel(
    plan, target_ref, tags_hbm, q_hbm, k_hbm, v_hbm,
    mine_ref, other_ref, q_mine_ref, q_other_ref, tags_ref, sems,
):
    size = plan.stretch
    odd = lax.axis_index("ctx") % 2
    pieces = [(tags_hbm, tags_ref)]
    for side, block_ref, q_ref in ((1 - odd, other_ref, q_other_ref), (odd, mine_ref, q_mine_ref)):
        base = side * plan.half
        for index, source in enumerate((k_hbm, v_hbm)):
            for piece in range(plan.pieces):
                start = pl.multiple_of(base + piece * PIECE, HEAD)
                row = (index * plan.pieces + piece) * size
                pieces.append((source.at[:, pl.ds(start, PIECE)], block_ref.at[pl.ds(row, size)]))
        span = pl.ds(pl.multiple_of(base, HEAD), plan.half)
        pieces.append((q_hbm.at[:, span], q_ref))
    copies = [
        pltpu.make_async_copy(source, held, sems.at[index])
        for index, (source, held) in enumerate(pieces)
    ]
    for copy in copies:
        copy.start()
    copies[0].wait()
    tags = tags_ref[...].astype(F32) + 1.0
    row = iota((TAG_ROWS, size), 0)
    target = target_ref[...].astype(F32)
    block = jnp.where(row == 0, tags, jnp.where(row == 1, target, 0.0)).astype(BF)
    first = plan.block_rows - TAG_ROWS
    for ref in (mine_ref, other_ref):
        ref[first:, :] = jnp.zeros((TAG_ROWS, PIECE), BF)
        ref[first:, 0:size] = block
    for copy in copies[1:]:
        copy.wait()


class Pair:
    def __init__(self, plan, mine_ref, pair_ref, far_ref, cross_ref):
        self.plan = plan
        self.odd = lax.axis_index("ctx") % 2 == 1
        self.refs = (
            (cross_ref, far_ref), (far_ref, cross_ref), (pair_ref, mine_ref), (mine_ref, pair_ref)
        )

    def choose(self, if_odd, if_even):
        return jnp.where(self.odd, if_odd, if_even)

    def part(self, block, rows, span):
        if_odd, if_even = self.refs[block]
        return self.choose(if_odd[rows, span], if_even[rows, span])

    def head(self, block, piece, lane):
        first = piece * self.plan.stretch
        rows = slice(first, first + self.plan.stretch)
        return self.part(block, rows, slice(lane, lane + HEAD))

    def keys(self, block, head):
        return self.head(block, head * HEAD // PIECE, head * HEAD % PIECE)

    def values(self, block, head):
        return self.head(block, self.plan.pieces + head * HEAD // PIECE, head * HEAD % PIECE)

    def integers(self, block, row):
        rows = slice(self.plan.block_rows - TAG_ROWS, self.plan.block_rows)
        return self.part(block, rows, slice(0, self.plan.stretch)).astype(F32)[row:row + 1]


def softmax_kernel(
    plan, q_mine_ref, q_pair_ref, mine_ref, pair_ref, far_ref, cross_ref, probs_ref
):
    size = plan.stretch
    pair = Pair(plan, mine_ref, pair_ref, far_ref, cross_ref)
    tags = [pair.integers(block, 0) for block in range(4)]
    causal = iota((size, size), 1) <= iota((size, size), 0)
    masks = []
    for query in range(2):
        column = to_column(tags[2 + query])
        masks.append([column == tags[query + block] for block in range(3)])
        masks[query][2] = masks[query][2] & causal
    heads = plan.half // HEAD
    for head in range(heads):
        span = slice(head * HEAD, (head + 1) * HEAD)
        q_mine, q_pair = q_mine_ref[:, span], q_pair_ref[:, span]
        queries = (pair.choose(q_pair, q_mine), pair.choose(q_mine, q_pair))
        blocks = [pair.keys(block, head) for block in range(4)]
        for query in range(2):
            scores = [
                jnp.where(
                    masks[query][block],
                    dot_nt(queries[query], blocks[query + block]) * (1.0 / math.sqrt(HEAD)),
                    -1e30,
                )
                for block in range(3)
            ]
            top = jnp.max(
                jnp.maximum(jnp.maximum(scores[0], scores[1]), scores[2]), axis=-1, keepdims=True
            )
            weights = [jnp.exp(score - top) for score in scores]
            norm = jnp.sum(weights[0] + weights[1] + weights[2], axis=-1, keepdims=True)
            scale = 1.0 / norm
            first = (query * heads + head) * size
            for index, weight in enumerate(weights):
                probs_ref[first:first + size, index * size:(index + 1) * size] = (
                    weight * scale
                ).astype(BF)


def hidden_kernel(
    plan, probs_ref, mine_ref, pair_ref, far_ref, cross_ref, message_ref, hidden_ref
):
    size = plan.stretch
    pair = Pair(plan, mine_ref, pair_ref, far_ref, cross_ref)
    heads = plan.half // HEAD
    for head in range(heads):
        span = slice(head * HEAD, (head + 1) * HEAD)
        blocks = [pair.values(block, head) for block in range(4)]
        for query in range(2):
            first = (query * heads + head) * size
            total = None
            for index in range(3):
                probs = probs_ref[first:first + size, index * size:(index + 1) * size]
                term = dot(probs, blocks[query + index])
                total = term if total is None else total + term
            hidden_ref[query * size:(query + 1) * size, span] = total.astype(BF)
    even_rows, odd_rows = hidden_ref[0:size, :], hidden_ref[size:2 * size, :]
    targets = [pair.integers(2 + query, 1).astype(jnp.int32) for query in range(2)]
    write_messages(
        plan,
        [targets[part // plan.half_parts] for part in range(plan.fold)],
        split_columns(plan, even_rows) + split_columns(plan, odd_rows),
        message_ref,
    )


def act_kernel(
    plan, message_ref, down_hbm, gate_hbm, up_hbm, act_ref, gate_ref, up_ref,
    down_ref, rows_ref, down_sem, gate_sem, up_sem,
):
    copies = [
        pltpu.make_async_copy(
            down_hbm.at[pl.ds(start, size)], down_ref.at[pl.ds(start, size)], down_sem.at[index]
        )
        for index, (_, start, size) in enumerate(plan.cuts)
    ]
    gate_copy = pltpu.make_async_copy(gate_hbm, gate_ref, gate_sem)
    up_copy = pltpu.make_async_copy(up_hbm, up_ref, up_sem)
    for copy in copies:
        copy.start()
    gate_copy.start()
    up_copy.start()
    read_expert_rows(plan, message_ref, rows_ref)
    for copy, (expert, start, size) in zip(copies, plan.cuts):
        copy.wait()
        rows = rows_ref[expert * plan.expert_rows:(expert + 1) * plan.expert_rows, :]
        act_ref[:, start:start + size] = dot_nt(rows, down_ref[start:start + size, :])
    gate_copy.wait()
    up_copy.wait()


def expert_kernel(
    plan, message_ref, gain_ref, act_ref, gate_ref, up_ref, out_ref,
    held_ref, rows_ref, grad_gate_ref, grad_up_ref, sum_ref,
):
    read_hidden_rows(plan, message_ref, gain_ref, held_ref, rows_ref)
    grad_gate_ref[...] = jnp.zeros_like(grad_gate_ref)
    grad_up_ref[...] = jnp.zeros_like(grad_up_ref)
    for expert, start, size in plan.cuts:
        span = slice(start, start + size)
        own = slice(expert * plan.expert_rows, (expert + 1) * plan.expert_rows)
        rows, act = rows_ref[own, :], act_ref[:, span]
        gate_pre, up_pre = dot(rows, gate_ref[:, span]), dot(rows, up_ref[:, span])
        sig = jax.nn.sigmoid(gate_pre)
        grad_gate = act * up_pre * (sig * (1.0 + gate_pre * (1.0 - sig)))
        grad_gate_ref[own, span] = grad_gate.astype(BF)
        grad_up_ref[own, span] = (act * (gate_pre * sig)).astype(BF)
    for start in range(0, plan.model, CUT):
        span = slice(start, start + CUT)
        total = dot_nt(gate_ref[span, :], grad_gate_ref[...])
        total = total + dot_nt(up_ref[span, :], grad_up_ref[...])
        sum_ref[span, :] = total.astype(BF)
    write_expert_rows(plan, norm_backward(plan, sum_ref, held_ref, gain_ref), out_ref)


def finish_kernel(plan, target_ref, grad_ref, message_ref, out_ref):
    target = to_column(target_ref[...].astype(F32))[:, 0:1].astype(jnp.int32)
    parts = [None] * plan.fold
    for chunk in range(plan.chunks):
        wanted, piece = message_slot(plan, chunk, (plan.stretch, CHUNK), 1)
        messages = message_ref[chunk * CHUNK:(chunk + 1) * CHUNK, :]
        for part in range(plan.fold):
            pick = jnp.where((wanted == target) & (piece == part), 1.0, 0.0).astype(BF)
            term = dot(pick, messages)
            parts[part] = term if parts[part] is None else parts[part] + term
    for part, term in enumerate(parts):
        span = slice(part * plan.width, (part + 1) * plan.width)
        out_ref[:, span] = (grad_ref[:, span].astype(F32) + term).astype(BF)


def params(limit):
    return pltpu.CompilerParams(vmem_limit_bytes=limit)


def in_hbm(value):
    return pltpu.with_memory_space_constraint(value, pltpu.HBM)


def shards(
    queries, keys, values, doc_ids, routes, route_weight, norm_gain, w_gate, w_up, w_down, grad_out
):
    stretch, model = queries.shape[1:]
    ctx_count = lax.axis_size("ctx")
    axes = ("ctx", "ep")
    ep_count = lax.axis_size("ep")
    plan = Plan(ctx_count * ep_count, ep_count, w_gate.shape[1], model, stretch)
    messages = jax.ShapeDtypeStruct((plan.total, plan.width), BF)
    message_bytes = 2 * plan.total * plan.width
    gain = norm_gain.reshape(1, model)

    def exchange(value):
        cut = value.reshape(plan.devices, plan.rows, plan.width)
        cut = lax.all_to_all(cut, axes, split_axis=0, concat_axis=0, tiled=True)
        return cut.reshape(plan.total, plan.width)

    two_up = [(source, source + 2) for source in range(ctx_count - 2)]
    next_pair = [(source, (source ^ 1) + 2) for source in range(ctx_count - 2)]
    pairs = [(source, source ^ 1) for source in range(ctx_count)]

    def send(value, route):
        return lax.ppermute(value, "ctx", route)

    inside = pl.BlockSpec(memory_space=pltpu.VMEM)
    outside = pl.BlockSpec(memory_space=pltpu.HBM)
    block = jax.ShapeDtypeStruct((plan.block_rows, PIECE), BF)
    half = jax.ShapeDtypeStruct((stretch, plan.half), BF)
    grad_messages, target = pl.pallas_call(
        functools.partial(grads_kernel, plan),
        in_specs=[outside] * 3,
        out_shape=(messages, jax.ShapeDtypeStruct((1, stretch), jnp.int32)),
        scratch_shapes=[
            pltpu.VMEM((1, stretch), jnp.int32),
            pltpu.VMEM((1, stretch), F32),
            pltpu.VMEM((stretch, model), BF),
            pltpu.SemaphoreType.DMA((3,)),
        ],
        compiler_params=params(8 * MB + 3 * message_bytes),
        name="route_grads",
    )(
        in_hbm(routes.reshape(1, stretch)), in_hbm(route_weight.reshape(1, stretch)),
        in_hbm(grad_out[0]),
    )
    got_grads = exchange(grad_messages)
    mine, other, q_mine, q_other = pl.pallas_call(
        functools.partial(pack_kernel, plan),
        in_specs=[inside] + [outside] * 4,
        out_shape=(block, block, half, half),
        scratch_shapes=[
            pltpu.VMEM((1, stretch), jnp.int32),
            pltpu.SemaphoreType.DMA((4 * plan.pieces + 3,)),
        ],
        compiler_params=params(8 * MB),
        name="pack",
    )(target, *map(in_hbm, (doc_ids, queries[0], keys[0], values[0])))
    far, cross = send(mine, two_up), send(other, next_pair)
    pair, q_pair = send(other, pairs), send(q_other, pairs)

    rows = plan.local * plan.expert_rows
    weight_bytes = 2 * plan.columns * model
    act, gate, up = pl.pallas_call(
        functools.partial(act_kernel, plan),
        in_specs=[inside, outside, outside, outside],
        out_specs=[inside, inside, inside],
        out_shape=(
            jax.ShapeDtypeStruct((plan.expert_rows, plan.columns), F32),
            pltpu.VMEM(w_gate.shape, BF),
            pltpu.VMEM(w_up.shape, BF),
        ),
        scratch_shapes=[
            pltpu.VMEM(w_down.shape, BF),
            pltpu.VMEM((rows, model), BF),
            pltpu.SemaphoreType.DMA((len(plan.cuts),)),
            pltpu.SemaphoreType.DMA,
            pltpu.SemaphoreType.DMA,
        ],
        compiler_params=params(8 * MB + 6 * message_bytes + weight_bytes),
        cost_estimate=pl.CostEstimate(
            flops=2 * plan.expert_rows * plan.columns * model,
            bytes_accessed=3 * weight_bytes,
            transcendentals=0,
        ),
        name="grad_act",
    )(got_grads, in_hbm(w_down), in_hbm(w_gate), in_hbm(w_up))
    far, cross, pair, q_pair, act = lax.optimization_barrier((far, cross, pair, q_pair, act))

    probs = pl.pallas_call(
        functools.partial(softmax_kernel, plan),
        out_shape=jax.ShapeDtypeStruct((HEADS * stretch, (REACH + 1) * stretch), BF),
        compiler_params=params(16 * MB),
        name="softmax",
    )(q_mine, q_pair, mine, pair, far, cross)
    hidden_messages = pl.pallas_call(
        functools.partial(hidden_kernel, plan),
        out_shape=messages,
        scratch_shapes=[pltpu.VMEM((2 * stretch, plan.half), BF)],
        compiler_params=params(12 * MB + 3 * message_bytes),
        name="hidden",
    )(probs, mine, pair, far, cross)
    got_hidden = exchange(hidden_messages)

    returned = pl.pallas_call(
        functools.partial(expert_kernel, plan),
        out_shape=messages,
        scratch_shapes=[
            pltpu.VMEM((rows, model), F32),
            pltpu.VMEM((rows, model), BF),
            pltpu.VMEM((rows, plan.columns), BF),
            pltpu.VMEM((rows, plan.columns), BF),
            pltpu.VMEM((model, rows), BF),
        ],
        compiler_params=params(12 * MB + 8 * message_bytes),
        cost_estimate=pl.CostEstimate(
            flops=8 * plan.expert_rows * plan.columns * model,
            bytes_accessed=2 * weight_bytes,
            transcendentals=0,
        ),
        name="experts",
    )(got_hidden, gain, act, gate, up)
    combined = exchange(returned)

    grad_in = pl.pallas_call(
        functools.partial(finish_kernel, plan),
        out_shape=jax.ShapeDtypeStruct((stretch, model), BF),
        compiler_params=params(12 * MB + 3 * message_bytes),
        name="finish",
    )(target, grad_out[0], combined)
    return grad_in[None]


def solution(mesh):
    in_specs = (
        P("ep", "ctx", None),
        P("ep", "ctx", None),
        P("ep", "ctx", None),
        P("ep", "ctx"),
        P("ep", "ctx", None),
        P("ep", "ctx", None),
        P(),
        P(None, ("ctx", "ep")),
        P(None, ("ctx", "ep")),
        P(("ctx", "ep"), None),
        P("ep", "ctx", None),
    )
    out_specs = P("ep", "ctx", None)
    return jax.shard_map(shards, mesh=mesh, in_specs=in_specs, out_specs=out_specs, check_vma=False)
```
